32 devices in a mesh: band: 4 (over x, core), gx: 4 (over z), gy: 2 (over y).
Axes of the slice: x: 2, y: 2, z: 4, core: 2. Of those that a mesh axis runs over, the one named last changes fastest.
Arguments:
- start_bands: float32 [64, 24, 16, 128], P('band', 'gx', 'gy'), may hold values from -40 to 40
- potential: float32 [24, 16, 128], P('gx', 'gy'), may hold values from 0 to 2
Outputs:
- new_bands: float32 [64, 24, 16, 128], P('band', 'gx', 'gy')
The draws below stay inside these ranges and needn't reach their ends.
All inputs are finite; a program needn't handle non-finite values.
Results may differ from the reference program's by a relative error of at most 0.00025.
Values sent between devices are 32-bit elements; how exact they have to be, the bound alone decides.
No kernel may reach another device: no remote copies, remote signals or barrier semaphores. Data moves between devices by JAX's collectives and lax.ppermute only.
A program may use at most 64 MiB of HBM per device.

```python
import math
import jax
import jax.numpy as jnp
from jax import lax

BANDS = 64
NZ = 128
DEGREE = 4
NX = 24
NY = 16


def draw_start_bands(key, part):
    first_key, second_key = jax.random.split(key, 2)
    column_scale = jnp.exp(jax.random.uniform(second_key, (1, NX, NY, 1), jnp.float32) * math.log(10.0))
    values = jax.random.normal(first_key, (BANDS, NX, NY, NZ), jnp.float32) * column_scale
    return jnp.clip(values, -40.0, 40.0).astype(jnp.float32)


def steps_of(key, dims, shards, smallest, top_value):
    def one(axis_at, parts):
        heights = jax.random.uniform(jax.random.fold_in(jax.random.fold_in(key, 6), axis_at), (parts,), jnp.float32, smallest / len(shards), top_value / len(shards))
        return jnp.repeat(jnp.exp(heights), dims[axis_at] // parts).reshape((-1,) + (1,) * (len(dims) - axis_at - 1))

    gain = one(*shards[0])
    for cut in shards[1:]:
        gain = gain * one(*cut)
    return gain


def setup_inputs(seed: int = 0) -> dict:
    streams_of = jax.random.split(jax.random.key(seed), 3)
    return {
        "start_bands": draw_start_bands(jax.random.fold_in(streams_of[2], 71), 0),
        "potential": jnp.clip(2.0 * jax.random.uniform(streams_of[1], (NX, NY, NZ), jnp.float32) ** steps_of(streams_of[1], (NX, NY, NZ), ((0, 4), (1, 2)), -0.2, 0.2), 0.0, 2.0),
    }


COEFFS = (-5369.0 / 1800.0, 12.0 / 7.0, -15.0 / 56.0, 10.0 / 189.0, -1.0 / 112.0, 2.0 / 1925.0, -1.0 / 16632.0)
LOWER_END = -0.5
CUT_LOW = 3.0
CUT_HIGH = 12.7

def filter_weights(degree):
    half_width = (CUT_HIGH - CUT_LOW) / 2.0
    middle = (CUT_HIGH + CUT_LOW) / 2.0
    sigma = half_width / (LOWER_END - middle)
    tau = 2.0 / sigma
    first = sigma / half_width
    others = []
    for index in range(degree - 1):
        sigma_new = 1.0 / (tau - sigma)
        others.append((2.0 * sigma_new / half_width, sigma * sigma_new))
        sigma = sigma_new
    return (middle, first, others)

def hamiltonian(field, potential):
    laplace = 3.0 * COEFFS[0] * field
    for offset in range(1, len(COEFFS)):
        neighbours = jnp.roll(field, -offset, 0) + jnp.roll(field, offset, 0)
        neighbours = neighbours + jnp.roll(field, -offset, 1) + jnp.roll(field, offset, 1)
        neighbours = neighbours + jnp.roll(field, -offset, 2) + jnp.roll(field, offset, 2)
        laplace = laplace + COEFFS[offset] * neighbours
    return -0.5 * laplace + potential * field

def filter_band(field, potential):
    middle, first, others = filter_weights(DEGREE)
    current = (hamiltonian(field, potential) - middle * field) * first
    previous = field
    for scale_now, scale_back in others:
        following = (hamiltonian(current, potential) - middle * current) * scale_now - scale_back * previous
        previous = current
        current = following
    return current

def reference(start_bands, potential):
    filtered = lax.map(lambda field: filter_band(field, potential), start_bands)
    flattened = filtered.reshape(filtered.shape[0], -1)
    margin = jnp.dot(flattened.astype(jnp.float32), flattened.T.astype(jnp.float32), precision=lax.Precision.HIGHEST, preferred_element_type=jnp.float32) * (1.0 / (NX * NY * NZ))
    lower_factor = jnp.linalg.cholesky(margin)
    identity = jnp.eye(margin.shape[0], dtype=jnp.float32)
    inverse = jax.scipy.linalg.solve_triangular(lower_factor, identity, lower=True)
    rotated = jnp.dot(inverse.astype(jnp.float32), flattened.astype(jnp.float32), precision=lax.Precision.HIGHEST, preferred_element_type=jnp.float32)
    return rotated.reshape(start_bands.shape)
```

```python
import functools

import jax
import jax.numpy as jnp
import ml_dtypes
import numpy as np
from jax import lax
from jax.experimental import pallas as pl
from jax.experimental.pallas import tpu as pltpu
from jax.sharding import PartitionSpec as P

DEGREE = 4


COEFFS = (
    -5369.0 / 1800.0,
    12.0 / 7.0,
    -15.0 / 56.0,
    10.0 / 189.0,
    -1.0 / 112.0,
    2.0 / 1925.0,
    -1.0 / 16632.0,
)
REACH = len(COEFFS) - 1
LOWER_END = -0.5
CUT_LOW = 3.0
CUT_HIGH = 12.7
TILE = 8


def filter_weights(degree):
    half_width = (CUT_HIGH - CUT_LOW) / 2.0
    middle = (CUT_HIGH + CUT_LOW) / 2.0
    sigma = half_width / (LOWER_END - middle)
    tau = 2.0 / sigma
    first = sigma / half_width
    others = []
    for index in range(degree - 1):
        sigma_new = 1.0 / (tau - sigma)
        others.append((2.0 * sigma_new / half_width, sigma * sigma_new))
        sigma = sigma_new
    return (middle, first, others)


def padded_2(block, sides, width):
    for axis, dim in sides:
        count = lax.axis_size(axis)
        forward = [(i, i + 1) for i in range(count - 1)]
        forward.append((count - 1, 0))
        backward = [(target, source) for source, target in forward]
        low = lax.ppermute(
            lax.slice_in_dim(block, block.shape[dim] - width, None, axis=dim), axis, forward
        )
        high = lax.ppermute(lax.slice_in_dim(block, 0, width, axis=dim), axis, backward)
        block = jnp.concatenate([low, block, high], axis=dim)
    return block


def hamiltonian(field, potential):
    width_x = field.shape[1]
    width_y = field.shape[2]
    padded = padded_2(field, (("gx", 1), ("gy", 2)), REACH)
    laplace = 3.0 * COEFFS[0] * field
    for offset in range(1, REACH + 1):
        ahead_x = padded[:, REACH + offset : REACH + offset + width_x, REACH : REACH + width_y]
        behind_x = padded[:, REACH - offset : REACH - offset + width_x, REACH : REACH + width_y]
        ahead_y = padded[:, REACH : REACH + width_x, REACH + offset : REACH + offset + width_y]
        behind_y = padded[:, REACH : REACH + width_x, REACH - offset : REACH - offset + width_y]
        neighbours = ahead_x + behind_x
        neighbours = neighbours + ahead_y + behind_y
        neighbours = neighbours + jnp.roll(field, -offset, 3) + jnp.roll(field, offset, 3)
        laplace = laplace + COEFFS[offset] * neighbours
    return -0.5 * laplace + potential * field


def chebyshev(field, potential):
    middle, first, others = filter_weights(DEGREE)
    current = (hamiltonian(field, potential) - middle * field) * first
    previous = field
    for scale_now, scale_back in others:
        following = (
            hamiltonian(current, potential) - middle * current
        ) * scale_now - scale_back * previous
        previous = current
        current = following
    return current


def invert_factor(margin, identity):
    lower_factor = jnp.linalg.cholesky(margin)
    return jax.scipy.linalg.solve_triangular(lower_factor, identity, lower=True)


def on_device_halo(start_bands, potential):
    filtered = chebyshev(start_bands, potential)
    own_bands = filtered.shape[0]
    flattened = filtered.reshape(own_bands, -1)
    total_cells = flattened.shape[1] * lax.axis_size("gx") * lax.axis_size("gy")
    all_bands = own_bands * lax.axis_size("band")
    identity = jnp.eye(all_bands, dtype=jnp.float32)
    products = jnp.dot(
        flattened,
        lax.all_gather(flattened, "band", axis=0, tiled=True).T,
        precision=lax.Precision.HIGHEST,
        preferred_element_type=jnp.float32,
    )
    first_row = lax.axis_index("band") * own_bands
    summed = lax.psum(products, ("gx", "gy"))
    margin = lax.all_gather(summed, "band", axis=0, tiled=True) * (1.0 / total_cells)
    inverse = invert_factor(margin, identity)
    own_rows = lax.dynamic_slice_in_dim(inverse, first_row, own_bands, 0)
    rotated = jnp.dot(
        own_rows,
        lax.all_gather(flattened, "band", axis=0, tiled=True),
        precision=lax.Precision.HIGHEST,
        preferred_element_type=jnp.float32,
    )
    return rotated.reshape(filtered.shape)


def split3(value):
    high = value.astype(jnp.bfloat16)
    rest = value - high.astype(jnp.float32)
    mid = rest.astype(jnp.bfloat16)
    low = (rest - mid.astype(jnp.float32)).astype(jnp.bfloat16)
    return high, mid, low


def z_weights(nz):
    circulant = np.zeros((nz, nz), np.float32)
    at = np.arange(nz)
    for offset in range(1, REACH + 1):
        circulant[at, (at + offset) % nz] += np.float32(-0.5 * COEFFS[offset])
        circulant[at, (at - offset) % nz] += np.float32(-0.5 * COEFFS[offset])
    high = circulant.astype(ml_dtypes.bfloat16)
    rest = circulant - high.astype(np.float32)
    mid = rest.astype(ml_dtypes.bfloat16)
    low = (rest - mid.astype(np.float32)).astype(ml_dtypes.bfloat16)
    first = np.block([[high, mid], [high, mid]])
    second = np.concatenate([high, low], 0)
    return first, second


def filter_kernel(dims, core_ref, own_ref, other_ref, w1_ref, w2_ref, out_ref, pot, buf_a, buf_b, zbuf):
    gx, gy, own, nx, ny, nz, pieces = dims
    width = gx * nx
    height = gy * ny
    cells = nx * ny
    half = cells // 2
    rows = cells // pieces
    middle, first, others = filter_weights(DEGREE)
    shift = -middle - 1.5 * COEFFS[0]
    pad = TILE

    def place(buf, k, x, tile, value):
        buf[k, x, pl.ds(pad + tile * TILE, TILE), :] = value
        if tile == 0:
            buf[k, x, pl.ds(pad + height, TILE), :] = value
        if tile == height // TILE - 1:
            buf[k, x, pl.ds(0, TILE), :] = value

    core = core_ref[0]
    for g in range(gx * gy):
        at_x, at_y = (g // gy) * nx, (g % gy) * ny
        for k in range(own):
            for i in range(nx):
                for t in range(ny // TILE):
                    value = own_ref[g, pl.ds(k * cells + i * ny + t * TILE, TILE), :]
                    place(buf_a, k, at_x + i, at_y // TILE + t, value)
        mine = pl.ds(pl.multiple_of(core * half, TILE), half)
        theirs = pl.ds(pl.multiple_of((1 - core) * half, TILE), half)
        pot[g, mine, :] = own_ref[g, own * cells :, :] + shift
        pot[g, theirs, :] = other_ref[g] + shift

    buffers = (buf_a, buf_b)
    steps = [(first, None)] + others
    for step, (scale, back) in enumerate(steps):
        src, dst = buffers[step % 2], buffers[(step + 1) % 2]
        last = step == len(steps) - 1
        field = src[:, :, pl.ds(pad, height), :].reshape(own * width * height, nz)
        high, mid, low = split3(field)
        part = jnp.dot(jnp.concatenate([high, mid], 1), w1_ref[...], preferred_element_type=jnp.float32)
        rest = jnp.dot(jnp.concatenate([low, high], 1), w2_ref[...], preferred_element_type=jnp.float32)
        zbuf[...] = (part[:, :nz] + part[:, nz:] + rest).reshape(own, width, height, nz)
        for k in range(own):
            for x in range(width):
                for tile in range(height // TILE):
                    g = (x // nx) * gy + tile * TILE // ny
                    in_pencil = (x % nx) * ny + (tile * TILE) % ny
                    at = pad + tile * TILE
                    centre = src[k, x, pl.ds(at, TILE), :]
                    total = zbuf[k, x, pl.ds(tile * TILE, TILE), :] + pot[g, pl.ds(in_pencil, TILE), :] * centre
                    for j in range(1, REACH + 1):
                        near = src[k, (x + j) % width, pl.ds(at, TILE), :] + src[k, (x - j) % width, pl.ds(at, TILE), :]
                        near = near + src[k, x, pl.ds(at + j, TILE), :] + src[k, x, pl.ds(at - j, TILE), :]
                        total = total + (-0.5 * COEFFS[j]) * near
                    value = scale * total
                    if back is not None:
                        value = value - back * dst[k, x, pl.ds(at, TILE), :]
                    if not last:
                        place(dst, k, x, tile, value)
                        continue
                    for r in range(0, TILE, TILE // 2):
                        piece, row = divmod(in_pencil + r, rows)
                        to = piece_owner(piece, pieces) * gx * gy + g
                        out_ref[to, pl.ds(k * rows + row, TILE // 2), :] = value[r : r + TILE // 2]


def piece_owner(piece, pieces):
    chips = pieces // 2
    return (piece % chips) * 2 + piece // chips


def apply_filter(core, own, other, dims):
    gx, gy, bands, nx, ny, nz, pieces = dims
    width, height = gx * nx, gy * ny
    w1, w2 = z_weights(nz)
    padded = (bands, width, height + 2 * TILE, nz)
    vmem = pl.BlockSpec(memory_space=pltpu.VMEM)
    return pl.pallas_call(
        functools.partial(filter_kernel, dims),
        out_shape=jax.ShapeDtypeStruct((pieces * gx * gy, bands * nx * ny // pieces, nz), jnp.float32),
        in_specs=[pl.BlockSpec(memory_space=pltpu.SMEM)] + [vmem] * 4,
        out_specs=vmem,
        scratch_shapes=[
            pltpu.VMEM((gx * gy, nx * ny, nz), jnp.float32),
            pltpu.VMEM(padded, jnp.float32),
            pltpu.VMEM(padded, jnp.float32),
            pltpu.VMEM((bands, width, height, nz), jnp.float32),
        ],
        compiler_params=pltpu.CompilerParams(vmem_limit_bytes=40 * 1024 * 1024),
        name="filter",
    )(core, own, other, w1, w2)


def margin_kernel(rows, bands, scale, x_ref, out_ref):
    total = jnp.zeros((bands, bands), jnp.float32)
    for r in range(rows):
        block = x_ref[pl.ds(r, bands, stride=rows), :]
        total = total + lax.dot_general(
            block, block, (((1,), (1,)), ((), ())), precision=lax.Precision.HIGHEST, preferred_element_type=jnp.float32
        )
    total = total * scale
    out_ref[:, pl.ds(0, bands)] = total[: bands // 2]
    out_ref[:, pl.ds(bands, bands)] = total[bands // 2 :]


def partial_margin(blocks, bands, scale):
    rows = blocks.shape[0] // bands
    return pl.pallas_call(
        functools.partial(margin_kernel, rows, bands, scale),
        out_shape=jax.ShapeDtypeStruct((bands // 2, 2 * bands), jnp.float32),
        in_specs=[pl.BlockSpec(memory_space=pltpu.VMEM)],
        out_specs=pl.BlockSpec(memory_space=pltpu.VMEM),
        name="margin",
    )(blocks)


def sum_over(value, axes, masks, count):
    total = value
    for mask in masks:
        total = total + lax.ppermute(value, axes, [(i, i ^ mask) for i in range(count)])
    return total


def inverse_kernel(bands, m_ref, out_ref):
    folded = m_ref[...]
    margin = jnp.concatenate([folded[:, :bands], folded[:, bands:]], 0)
    row_at = lax.broadcasted_iota(jnp.int32, (bands, bands), 0)
    col_at = lax.broadcasted_iota(jnp.int32, (bands, bands), 1)
    both = jnp.concatenate([margin, jnp.where(row_at == col_at, 1.0, 0.0)], 1)
    lines = lax.broadcasted_iota(jnp.int32, (bands, 1), 0)
    pivots = jnp.ones((bands, 1), jnp.float32)
    for j in range(bands):
        row = both[j : j + 1, :]
        column = both[:, j : j + 1]
        pivot = row[:, j : j + 1]
        pivots = jnp.where(lines == j, pivot, pivots)
        factor = jnp.where(lines > j, column, 0.0)
        both = both - factor * (row * (1.0 / pivot))
    out_ref[...] = both[:, bands:] * lax.rsqrt(pivots)


def inverse_factor(folded, bands):
    return pl.pallas_call(
        functools.partial(inverse_kernel, bands),
        out_shape=jax.ShapeDtypeStruct((bands, bands), jnp.float32),
        in_specs=[pl.BlockSpec(memory_space=pltpu.VMEM)],
        out_specs=pl.BlockSpec(memory_space=pltpu.VMEM),
        name="inverse",
    )(folded)


def rotate_kernel(dims, place_ref, inv_ref, *refs):
    rows, bands, own, pieces = dims
    parts, out_ref = refs[:-1], refs[-1]
    first = pl.multiple_of(place_ref[0], TILE)
    inverse = inv_ref[pl.ds(first, own), :]
    for index, part in enumerate(parts):
        at = place_ref[1 + index]
        for r in range(rows):
            block = part[pl.ds(r, bands, stride=rows), :]
            value = jnp.dot(inverse, block, precision=lax.Precision.HIGHEST, preferred_element_type=jnp.float32)
            out_ref[pl.ds(at + r, own, stride=rows * pieces), :] = value


def rotate(place, inverse, parts, own):
    bands = inverse.shape[0]
    pieces = len(parts)
    rows = parts[0].shape[0] // bands
    nz = parts[0].shape[1]
    vmem = pl.BlockSpec(memory_space=pltpu.VMEM)
    return pl.pallas_call(
        functools.partial(rotate_kernel, (rows, bands, own, pieces)),
        out_shape=jax.ShapeDtypeStruct((own * rows * pieces, nz), jnp.float32),
        in_specs=[pl.BlockSpec(memory_space=pltpu.SMEM)] + [vmem] * (1 + pieces),
        out_specs=vmem,
        compiler_params=pltpu.CompilerParams(vmem_limit_bytes=32 * 1024 * 1024),
        name="rotate",
    )(place, inverse, *parts)


def on_device_fields(start_bands, potential):
    own_bands, nx, ny, nz = start_bands.shape
    gx, gy, pieces = lax.axis_size("gx"), lax.axis_size("gy"), lax.axis_size("band")
    grid = gx * gy
    own = own_bands // grid
    cells = nx * ny
    bands = own_bands * pieces
    rows = cells // pieces
    band = lax.axis_index("band")
    core = band % 2
    swap = [(i, i ^ 1) for i in range(pieces)]

    fields = start_bands.reshape(grid, own * cells, nz)
    flat_potential = potential.reshape(cells, nz)
    half = cells // 2
    own_half = lax.dynamic_slice_in_dim(flat_potential, core * half, half, 0)
    packed = jnp.concatenate([fields, jnp.broadcast_to(own_half[None], (grid, half, nz))], 1)
    packed = lax.all_to_all(packed, ("gx", "gy"), 0, 0)
    other = lax.ppermute(packed[:, own * cells :, :], "band", swap)
    dims = (gx, gy, own, nx, ny, nz, pieces)
    filtered = apply_filter(core.reshape(1), packed, other, dims)
    blocks = lax.all_to_all(filtered, ("band", "gx", "gy"), 0, 0).reshape(bands * rows, nz)

    parts, offsets = [blocks], [band]
    for mask in range(2, pieces, 2):
        parts.append(lax.ppermute(blocks, "band", [(i, i ^ mask) for i in range(pieces)]))
        offsets.append(band ^ mask)
    for index in range(len(parts)):
        parts.append(lax.ppermute(parts[index], "band", swap))
        offsets.append(offsets[index] ^ 1)
    chips = pieces // 2
    offsets = [((at % 2) * chips + at // 2) * rows for at in offsets]

    margin = partial_margin(blocks, bands, 1.0 / (cells * nz * grid))
    margin = sum_over(margin, "band", [1], pieces)
    masks = [chip * 2 * gy + y for chip in range(chips) for y in range(gy)][1:]
    margin = sum_over(margin, ("band", "gy"), masks, pieces * gy)
    margin = sum_over(margin, "gx", range(1, gx), gx)
    inverse = inverse_factor(margin, bands)
    place = jnp.stack([band * own_bands] + offsets).astype(jnp.int32)
    rotated = rotate(place, inverse, parts, own_bands)
    return rotated.reshape(start_bands.shape)


def power_of_two(count):
    return count & (count - 1) == 0


def on_device(start_bands, potential):
    own_bands, nx, ny, nz = start_bands.shape
    gx, gy, pieces = lax.axis_size("gx"), lax.axis_size("gy"), lax.axis_size("band")
    cells = nx * ny
    whole_fields = (
        own_bands % (gx * gy) == 0
        and own_bands % TILE == 0
        and all(power_of_two(count) for count in (gx, gy, pieces))
        and pieces > 1
        and ny % TILE == 0
        and nz % 128 == 0
        and cells % (2 * TILE) == 0
        and cells % (pieces * TILE // 2) == 0
        and (own_bands // (gx * gy)) * (cells // pieces) % TILE == 0
        and gx * nx > 2 * REACH
    )
    if whole_fields:
        return on_device_fields(start_bands, potential)
    return on_device_halo(start_bands, potential)


def solution(mesh):
    in_specs = (P("band", "gx", "gy", None), P("gx", "gy", None))
    out_specs = P("band", "gx", "gy", None)
    return jax.shard_map(
        on_device, mesh=mesh, in_specs=in_specs, out_specs=out_specs, check_vma=False
    )
```

```python
import functools

import jax
import jax.numpy as jnp
import ml_dtypes
import numpy as np
from jax import lax
from jax.experimental import pallas as pl
from jax.experimental.pallas import tpu as pltpu
from jax.sharding import Mesh, PartitionSpec as P

DEGREE = 4


COEFFS = (
    -5369.0 / 1800.0,
    12.0 / 7.0,
    -15.0 / 56.0,
    10.0 / 189.0,
    -1.0 / 112.0,
    2.0 / 1925.0,
    -1.0 / 16632.0,
)
REACH = len(COEFFS) - 1
LOWER_END = -0.5
CUT_LOW = 3.0
CUT_HIGH = 12.7
TILE = 8


def filter_weights(degree):
    half_width = (CUT_HIGH - CUT_LOW) / 2.0
    middle = (CUT_HIGH + CUT_LOW) / 2.0
    sigma = half_width / (LOWER_END - middle)
    tau = 2.0 / sigma
    first = sigma / half_width
    others = []
    for index in range(degree - 1):
        sigma_new = 1.0 / (tau - sigma)
        others.append((2.0 * sigma_new / half_width, sigma * sigma_new))
        sigma = sigma_new
    return (middle, first, others)


def padded_2(block, sides, width):
    for axis, dim in sides:
        count = lax.axis_size(axis)
        forward = [(i, i + 1) for i in range(count - 1)]
        forward.append((count - 1, 0))
        backward = [(target, source) for source, target in forward]
        low = lax.ppermute(
            lax.slice_in_dim(block, block.shape[dim] - width, None, axis=dim), axis, forward
        )
        high = lax.ppermute(lax.slice_in_dim(block, 0, width, axis=dim), axis, backward)
        block = jnp.concatenate([low, block, high], axis=dim)
    return block


def hamiltonian(field, potential):
    width_x = field.shape[1]
    width_y = field.shape[2]
    padded = padded_2(field, (("gx", 1), ("gy", 2)), REACH)
    laplace = 3.0 * COEFFS[0] * field
    for offset in range(1, REACH + 1):
        ahead_x = padded[:, REACH + offset : REACH + offset + width_x, REACH : REACH + width_y]
        behind_x = padded[:, REACH - offset : REACH - offset + width_x, REACH : REACH + width_y]
        ahead_y = padded[:, REACH : REACH + width_x, REACH + offset : REACH + offset + width_y]
        behind_y = padded[:, REACH : REACH + width_x, REACH - offset : REACH - offset + width_y]
        neighbours = ahead_x + behind_x
        neighbours = neighbours + ahead_y + behind_y
        neighbours = neighbours + jnp.roll(field, -offset, 3) + jnp.roll(field, offset, 3)
        laplace = laplace + COEFFS[offset] * neighbours
    return -0.5 * laplace + potential * field


def chebyshev(field, potential):
    middle, first, others = filter_weights(DEGREE)
    current = (hamiltonian(field, potential) - middle * field) * first
    previous = field
    for scale_now, scale_back in others:
        following = (
            hamiltonian(current, potential) - middle * current
        ) * scale_now - scale_back * previous
        previous = current
        current = following
    return current


def invert_factor(margin, identity):
    lower_factor = jnp.linalg.cholesky(margin)
    return jax.scipy.linalg.solve_triangular(lower_factor, identity, lower=True)


def on_device_halo(start_bands, potential):
    filtered = chebyshev(start_bands, potential)
    own_bands = filtered.shape[0]
    flattened = filtered.reshape(own_bands, -1)
    total_cells = flattened.shape[1] * lax.axis_size("gx") * lax.axis_size("gy")
    all_bands = own_bands * lax.axis_size("band")
    identity = jnp.eye(all_bands, dtype=jnp.float32)
    products = jnp.dot(
        flattened,
        lax.all_gather(flattened, "band", axis=0, tiled=True).T,
        precision=lax.Precision.HIGHEST,
        preferred_element_type=jnp.float32,
    )
    first_row = lax.axis_index("band") * own_bands
    summed = lax.psum(products, ("gx", "gy"))
    margin = lax.all_gather(summed, "band", axis=0, tiled=True) * (1.0 / total_cells)
    inverse = invert_factor(margin, identity)
    own_rows = lax.dynamic_slice_in_dim(inverse, first_row, own_bands, 0)
    rotated = jnp.dot(
        own_rows,
        lax.all_gather(flattened, "band", axis=0, tiled=True),
        precision=lax.Precision.HIGHEST,
        preferred_element_type=jnp.float32,
    )
    return rotated.reshape(filtered.shape)


def split3(value):
    high = value.astype(jnp.bfloat16)
    rest = value - high.astype(jnp.float32)
    mid = rest.astype(jnp.bfloat16)
    low = (rest - mid.astype(jnp.float32)).astype(jnp.bfloat16)
    return high, mid, low


def z_weights(nz):
    circulant = np.zeros((nz, nz), np.float32)
    at = np.arange(nz)
    for offset in range(1, REACH + 1):
        circulant[at, (at + offset) % nz] += np.float32(-0.5 * COEFFS[offset])
        circulant[at, (at - offset) % nz] += np.float32(-0.5 * COEFFS[offset])
    high = circulant.astype(ml_dtypes.bfloat16)
    rest = circulant - high.astype(np.float32)
    mid = rest.astype(ml_dtypes.bfloat16)
    low = (rest - mid.astype(np.float32)).astype(ml_dtypes.bfloat16)
    first = np.block([[high, mid], [high, mid]])
    second = np.concatenate([high, low], 0)
    return first, second


def filter_kernel(dims, core_ref, own_ref, other_ref, w1_ref, w2_ref, out_ref, pot, buf_a, buf_b, zbuf):
    gx, gy, own, nx, ny, nz, pieces = dims
    width = gx * nx
    height = gy * ny
    cells = nx * ny
    half = cells // 2
    rows = cells // pieces
    middle, first, others = filter_weights(DEGREE)
    shift = -middle - 1.5 * COEFFS[0]
    pad = TILE

    def place(buf, k, x, tile, value):
        buf[k, x, pl.ds(pad + tile * TILE, TILE), :] = value
        if tile == 0:
            buf[k, x, pl.ds(pad + height, TILE), :] = value
        if tile == height // TILE - 1:
            buf[k, x, pl.ds(0, TILE), :] = value

    core = core_ref[0]
    for g in range(gx * gy):
        at_x, at_y = (g // gy) * nx, (g % gy) * ny
        for k in range(own):
            for i in range(nx):
                for t in range(ny // TILE):
                    value = own_ref[g, pl.ds(k * cells + i * ny + t * TILE, TILE), :]
                    place(buf_a, k, at_x + i, at_y // TILE + t, value)
        mine = pl.ds(pl.multiple_of(core * half, TILE), half)
        theirs = pl.ds(pl.multiple_of((1 - core) * half, TILE), half)
        pot[g, mine, :] = own_ref[g, own * cells :, :] + shift
        pot[g, theirs, :] = other_ref[g] + shift

    buffers = (buf_a, buf_b)
    steps = [(first, None)] + others
    for step, (scale, back) in enumerate(steps):
        src, dst = buffers[step % 2], buffers[(step + 1) % 2]
        last = step == len(steps) - 1
        field = src[:, :, pl.ds(pad, height), :].reshape(own * width * height, nz)
        high, mid, low = split3(field)
        part = jnp.dot(jnp.concatenate([high, mid], 1), w1_ref[...], preferred_element_type=jnp.float32)
        rest = jnp.dot(jnp.concatenate([low, high], 1), w2_ref[...], preferred_element_type=jnp.float32)
        zbuf[...] = (part[:, :nz] + part[:, nz:] + rest).reshape(own, width, height, nz)
        for k in range(own):
            for x in range(width):
                for tile in range(height // TILE):
                    g = (x // nx) * gy + tile * TILE // ny
                    in_pencil = (x % nx) * ny + (tile * TILE) % ny
                    at = pad + tile * TILE
                    centre = src[k, x, pl.ds(at, TILE), :]
                    total = zbuf[k, x, pl.ds(tile * TILE, TILE), :] + pot[g, pl.ds(in_pencil, TILE), :] * centre
                    for j in range(1, REACH + 1):
                        near = src[k, (x + j) % width, pl.ds(at, TILE), :] + src[k, (x - j) % width, pl.ds(at, TILE), :]
                        near = near + src[k, x, pl.ds(at + j, TILE), :] + src[k, x, pl.ds(at - j, TILE), :]
                        total = total + (-0.5 * COEFFS[j]) * near
                    value = scale * total
                    if back is not None:
                        value = value - back * dst[k, x, pl.ds(at, TILE), :]
                    if not last:
                        place(dst, k, x, tile, value)
                        continue
                    for r in range(0, TILE, TILE // 2):
                        piece, row = divmod(in_pencil + r, rows)
                        to = piece_owner(piece, pieces) * gx * gy + g
                        out_ref[to, pl.ds(k * rows + row, TILE // 2), :] = value[r : r + TILE // 2]


def piece_owner(piece, pieces):
    chips = pieces // 2
    return (piece % chips) * 2 + piece // chips


def apply_filter(core, own, other, dims):
    gx, gy, bands, nx, ny, nz, pieces = dims
    width, height = gx * nx, gy * ny
    w1, w2 = z_weights(nz)
    padded = (bands, width, height + 2 * TILE, nz)
    vmem = pl.BlockSpec(memory_space=pltpu.VMEM)
    return pl.pallas_call(
        functools.partial(filter_kernel, dims),
        out_shape=jax.ShapeDtypeStruct((pieces * gx * gy, bands * nx * ny // pieces, nz), jnp.float32),
        in_specs=[pl.BlockSpec(memory_space=pltpu.SMEM)] + [vmem] * 4,
        out_specs=vmem,
        scratch_shapes=[
            pltpu.VMEM((gx * gy, nx * ny, nz), jnp.float32),
            pltpu.VMEM(padded, jnp.float32),
            pltpu.VMEM(padded, jnp.float32),
            pltpu.VMEM((bands, width, height, nz), jnp.float32),
        ],
        compiler_params=pltpu.CompilerParams(vmem_limit_bytes=16 * 1024 * 1024),
        name="filter",
    )(core, own, other, w1, w2)


def margin_kernel(rows, bands, scale, x_ref, out_ref):
    highs, mids, lows = [], [], []
    for r in range(rows):
        high, mid, low = split3(x_ref[pl.ds(r, bands, stride=rows), :])
        highs.append(high)
        mids.append(mid)
        lows.append(low)
    terms = [jnp.concatenate(term, 1) for term in (highs, mids, lows)]
    stacked = jnp.concatenate(terms, 0)
    products = lax.dot_general(stacked, stacked, (((1,), (1,)), ((), ())), preferred_element_type=jnp.float32)

    def block(i, j):
        return products[i * bands : (i + 1) * bands, j * bands : (j + 1) * bands]

    small = block(0, 2) + block(2, 0) + block(1, 1)
    total = (small + (block(0, 1) + block(1, 0)) + block(0, 0)) * scale
    half = bands // 2
    for at, (i, j) in enumerate(((0, 0), (1, 0), (1, 1))):
        part = total[i * half : (i + 1) * half, j * half : (j + 1) * half]
        folds = [part[t * TILE : (t + 1) * TILE] for t in range(half // TILE)]
        out_ref[pl.ds(at * TILE, TILE), :] = jnp.concatenate(folds, 1)


def partial_margin(blocks, bands, scale):
    rows = blocks.shape[0] // bands
    return pl.pallas_call(
        functools.partial(margin_kernel, rows, bands, scale),
        out_shape=jax.ShapeDtypeStruct((3 * TILE, bands // 2 * (bands // 2) // TILE), jnp.float32),
        in_specs=[pl.BlockSpec(memory_space=pltpu.VMEM)],
        out_specs=pl.BlockSpec(memory_space=pltpu.VMEM),
        compiler_params=pltpu.CompilerParams(vmem_limit_bytes=8 * 1024 * 1024),
        name="margin",
    )(blocks)


def eliminate(margin, between):
    bands = margin.shape[0]
    tiles = bands // TILE
    row_at = lax.broadcasted_iota(jnp.int32, (bands, bands), 0)
    col_at = lax.broadcasted_iota(jnp.int32, (bands, bands), 1)
    both = jnp.concatenate([margin, jnp.where(row_at == col_at, 1.0, 0.0)], 1)
    width = 2 * bands
    lines = lax.broadcasted_iota(jnp.int32, (TILE, width), 0)
    both = [both[t * TILE : (t + 1) * TILE] for t in range(tiles)]
    for p in range(tiles):
        between(p)
        spread = [
            [
                jnp.broadcast_to(both[t][:, p * TILE + c : p * TILE + c + 1], (TILE, width)) if t >= p else None
                for t in range(tiles)
            ]
            for c in range(TILE)
        ]
        pivots = None
        for j in range(TILE):
            pivot = jnp.broadcast_to(spread[j][p][j : j + 1, :], (TILE, width))
            pivots = pivot if j == 0 else jnp.where(lines == j, pivot, pivots)
            ratio = 1.0 / pivot
            factor = [spread[j][t] * ratio if t >= p else None for t in range(tiles)]
            factor[p] = jnp.where(lines > j, factor[p], 0.0)
            for c in range(j + 1, TILE):
                entry = jnp.broadcast_to(spread[j][p][c : c + 1, :], (TILE, width))
                for t in range(p, tiles):
                    spread[c][t] = spread[c][t] - factor[t] * entry
            line = jnp.broadcast_to(both[p][j : j + 1, :], (TILE, width))
            for t in range(p, tiles):
                both[t] = both[t] - factor[t] * line
        both[p] = both[p] * lax.rsqrt(pivots)
    return jnp.concatenate(both, 0)[:, bands:]


def rotate_kernel(dims, place_ref, margins_ref, *refs):
    rows, bands, own, pieces, tiles = dims
    parts = refs[:pieces]
    out_ref, inv_ref, split_ref = refs[pieces:]
    folded = margins_ref[0]
    for term in range(1, margins_ref.shape[0]):
        folded = folded + margins_ref[term]
    half = bands // 2
    quarters = []
    for at in range(3):
        part = folded[at * TILE : (at + 1) * TILE]
        quarters.append(jnp.concatenate([part[:, t * half : (t + 1) * half] for t in range(half // TILE)], 0))
    low, cross, high = quarters
    margin = jnp.concatenate(
        [jnp.concatenate([low, cross.T], 1), jnp.concatenate([cross, high], 1)], 0
    )
    jobs = [(part, r) for part in range(pieces) for r in range(rows)]
    nz = parts[0].shape[1]

    def split_some(step):
        share = -(-len(jobs) // tiles)
        for at in range(step * share, min(len(jobs), (step + 1) * share)):
            part, r = jobs[at]
            terms_of = split3(parts[part][pl.ds(r, bands, stride=rows), :])
            for i, term in enumerate(terms_of):
                split_ref[at // 2, pl.ds(i * bands, bands), pl.ds((at % 2) * nz, nz)] = term

    inv_ref[...] = eliminate(margin, split_some)
    first = pl.multiple_of(place_ref[0], TILE)
    high, mid, low = split3(inv_ref[pl.ds(first, own), :])
    zero = jnp.zeros_like(high)
    left = jnp.concatenate(
        [
            jnp.concatenate([high, high, high], 1),
            jnp.concatenate([mid, mid, zero], 1),
            jnp.concatenate([low, zero, zero], 1),
        ],
        0,
    )
    for pair in range(len(jobs) // 2):
        product = jnp.dot(left, split_ref[pair], preferred_element_type=jnp.float32)
        value = product[:own] + (product[own : 2 * own] + product[2 * own :])
        for i in range(2):
            part, r = jobs[2 * pair + i]
            start = place_ref[1 + part] + r
            out_ref[pl.ds(start, own, stride=rows * pieces), :] = value[:, i * nz : (i + 1) * nz]


def rotate(place, margins, parts, own, bands):
    pieces = len(parts)
    rows = parts[0].shape[0] // bands
    nz = parts[0].shape[1]
    vmem = pl.BlockSpec(memory_space=pltpu.VMEM)
    dims = (rows, bands, own, pieces, bands // TILE)
    return pl.pallas_call(
        functools.partial(rotate_kernel, dims),
        out_shape=jax.ShapeDtypeStruct((own * rows * pieces, nz), jnp.float32),
        in_specs=[pl.BlockSpec(memory_space=pltpu.SMEM)] + [vmem] * (1 + pieces),
        out_specs=vmem,
        scratch_shapes=[
            pltpu.VMEM((bands, bands), jnp.float32),
            pltpu.VMEM((rows * pieces // 2, 3 * bands, 2 * nz), jnp.bfloat16),
        ],
        compiler_params=pltpu.CompilerParams(vmem_limit_bytes=12 * 1024 * 1024),
        name="rotate",
    )(place, margins, *parts)


def on_device_fields(start_bands, potential):
    own_bands, nx, ny, nz = start_bands.shape
    gx, gy, chips = lax.axis_size("gx"), lax.axis_size("gy"), lax.axis_size("chip")
    pieces = 2 * chips
    grid = gx * gy
    own = own_bands // grid
    cells = nx * ny
    bands = own_bands * pieces
    rows = cells // pieces
    chip, core = lax.axis_index("chip"), lax.axis_index("core")
    swap = [(0, 1), (1, 0)]

    fields = start_bands.reshape(grid, own * cells, nz)
    flat_potential = potential.reshape(cells, nz)
    half = cells // 2
    own_half = lax.dynamic_slice_in_dim(flat_potential, core * half, half, 0)
    packed = jnp.concatenate([fields, jnp.broadcast_to(own_half[None], (grid, half, nz))], 1)
    packed = lax.all_to_all(packed, ("gx", "gy"), 0, 0)
    other = lax.ppermute(packed[:, own * cells :, :], "core", swap)
    dims = (gx, gy, own, nx, ny, nz, pieces)
    filtered = apply_filter(core.reshape(1), packed, other, dims)
    blocks = lax.all_to_all(filtered, ("chip", "core", "gx", "gy"), 0, 0).reshape(bands * rows, nz)

    margin = partial_margin(blocks, bands, 1.0 / (cells * nz * grid))
    margin = margin + lax.ppermute(margin, "core", swap)
    margins = jnp.broadcast_to(margin[None], (chips * grid,) + margin.shape)
    margins = lax.all_to_all(margins, ("chip", "gx", "gy"), 0, 0)

    parts, offsets = [blocks], [(core * chips + chip) * rows]
    for mask in range(1, chips):
        parts.append(lax.ppermute(blocks, "chip", [(i, i ^ mask) for i in range(chips)]))
        offsets.append((core * chips + (chip ^ mask)) * rows)
    for index in range(chips):
        source = parts[index]
        if index:
            source, margins = lax.optimization_barrier((source, margins))
        parts.append(lax.ppermute(source, "core", swap))
        offsets.append((1 - core) * chips * rows + offsets[index] - core * chips * rows)
    place = jnp.stack([(chip * 2 + core) * own_bands] + offsets).astype(jnp.int32)
    rotated = rotate(place, margins, parts, own_bands, bands)
    return rotated.reshape(start_bands.shape)


def power_of_two(count):
    return count & (count - 1) == 0


def whole_fields(mesh, shape):
    gx, gy, pieces = mesh.shape["gx"], mesh.shape["gy"], mesh.shape["band"]
    bands, nx, ny, nz = shape[0], shape[1] // gx, shape[2] // gy, shape[3]
    own_bands, cells = bands // pieces, nx * ny
    return (
        own_bands % (gx * gy) == 0
        and own_bands % (2 * TILE) == 0
        and pieces % 2 == 0
        and power_of_two(pieces)
        and ny % TILE == 0
        and nz % 128 == 0
        and bands // 2 * (bands // 2) // TILE % 128 == 0
        and cells % (2 * TILE) == 0
        and cells % (pieces * TILE // 2) == 0
        and (own_bands // (gx * gy)) * (cells // pieces) % TILE == 0
        and shape[1] > 2 * REACH
    )


def solution(mesh):
    def step(start_bands, potential):
        if whole_fields(mesh, start_bands.shape):
            chips = mesh.shape["band"] // 2
            rest = mesh.devices.shape[1:]
            split = Mesh(mesh.devices.reshape((chips, 2) + rest), ("chip", "core") + mesh.axis_names[1:])
            program, band = on_device_fields, ("chip", "core")
        else:
            split, program, band = mesh, on_device_halo, "band"
        return jax.shard_map(
            program,
            mesh=split,
            in_specs=(P(band, "gx", "gy", None), P("gx", "gy", None)),
            out_specs=P(band, "gx", "gy", None),
            check_vma=False,
        )(start_bands, potential)

    return step
```

```python
import functools

import jax
import jax.numpy as jnp
from jax import lax
from jax.experimental import pallas as pl
from jax.experimental.pallas import tpu as pltpu
from jax.sharding import Mesh, PartitionSpec as P

DEGREE = 4


COEFFS = (
    -5369.0 / 1800.0,
    12.0 / 7.0,
    -15.0 / 56.0,
    10.0 / 189.0,
    -1.0 / 112.0,
    2.0 / 1925.0,
    -1.0 / 16632.0,
)
REACH = len(COEFFS) - 1
LOWER_END = -0.5
CUT_LOW = 3.0
CUT_HIGH = 12.7
TILE = 8


def filter_weights(degree):
    half_width = (CUT_HIGH - CUT_LOW) / 2.0
    middle = (CUT_HIGH + CUT_LOW) / 2.0
    sigma = half_width / (LOWER_END - middle)
    tau = 2.0 / sigma
    first = sigma / half_width
    others = []
    for index in range(degree - 1):
        sigma_new = 1.0 / (tau - sigma)
        others.append((2.0 * sigma_new / half_width, sigma * sigma_new))
        sigma = sigma_new
    return (middle, first, others)


def padded_2(block, sides, width):
    for axis, dim in sides:
        count = lax.axis_size(axis)
        forward = [(i, i + 1) for i in range(count - 1)]
        forward.append((count - 1, 0))
        backward = [(target, source) for source, target in forward]
        low = lax.ppermute(
            lax.slice_in_dim(block, block.shape[dim] - width, None, axis=dim), axis, forward
        )
        high = lax.ppermute(lax.slice_in_dim(block, 0, width, axis=dim), axis, backward)
        block = jnp.concatenate([low, block, high], axis=dim)
    return block


def hamiltonian(field, potential):
    width_x = field.shape[1]
    width_y = field.shape[2]
    padded = padded_2(field, (("gx", 1), ("gy", 2)), REACH)
    laplace = 3.0 * COEFFS[0] * field
    for offset in range(1, REACH + 1):
        ahead_x = padded[:, REACH + offset : REACH + offset + width_x, REACH : REACH + width_y]
        behind_x = padded[:, REACH - offset : REACH - offset + width_x, REACH : REACH + width_y]
        ahead_y = padded[:, REACH : REACH + width_x, REACH + offset : REACH + offset + width_y]
        behind_y = padded[:, REACH : REACH + width_x, REACH - offset : REACH - offset + width_y]
        neighbours = ahead_x + behind_x
        neighbours = neighbours + ahead_y + behind_y
        neighbours = neighbours + jnp.roll(field, -offset, 3) + jnp.roll(field, offset, 3)
        laplace = laplace + COEFFS[offset] * neighbours
    return -0.5 * laplace + potential * field


def chebyshev(field, potential):
    middle, first, others = filter_weights(DEGREE)
    current = (hamiltonian(field, potential) - middle * field) * first
    previous = field
    for scale_now, scale_back in others:
        following = (
            hamiltonian(current, potential) - middle * current
        ) * scale_now - scale_back * previous
        previous = current
        current = following
    return current


def invert_factor(margin, identity):
    lower_factor = jnp.linalg.cholesky(margin)
    return jax.scipy.linalg.solve_triangular(lower_factor, identity, lower=True)


def on_device_halo(start_bands, potential):
    filtered = chebyshev(start_bands, potential)
    own_bands = filtered.shape[0]
    flattened = filtered.reshape(own_bands, -1)
    total_cells = flattened.shape[1] * lax.axis_size("gx") * lax.axis_size("gy")
    all_bands = own_bands * lax.axis_size("band")
    identity = jnp.eye(all_bands, dtype=jnp.float32)
    products = jnp.dot(
        flattened,
        lax.all_gather(flattened, "band", axis=0, tiled=True).T,
        precision=lax.Precision.HIGHEST,
        preferred_element_type=jnp.float32,
    )
    first_row = lax.axis_index("band") * own_bands
    summed = lax.psum(products, ("gx", "gy"))
    margin = lax.all_gather(summed, "band", axis=0, tiled=True) * (1.0 / total_cells)
    inverse = invert_factor(margin, identity)
    own_rows = lax.dynamic_slice_in_dim(inverse, first_row, own_bands, 0)
    rotated = jnp.dot(
        own_rows,
        lax.all_gather(flattened, "band", axis=0, tiled=True),
        precision=lax.Precision.HIGHEST,
        preferred_element_type=jnp.float32,
    )
    return rotated.reshape(filtered.shape)


def split3(value):
    high = value.astype(jnp.bfloat16)
    rest = value - high.astype(jnp.float32)
    mid = rest.astype(jnp.bfloat16)
    low = (rest - mid.astype(jnp.float32)).astype(jnp.bfloat16)
    return high, mid, low


def z_weights(nz):
    row = lax.broadcasted_iota(jnp.int32, (nz, nz), 0)
    col = lax.broadcasted_iota(jnp.int32, (nz, nz), 1)
    apart = jnp.abs(row - col)
    apart = jnp.minimum(apart, nz - apart)
    circulant = jnp.zeros((nz, nz), jnp.float32)
    for offset in range(1, REACH + 1):
        circulant = jnp.where(apart == offset, -0.5 * COEFFS[offset], circulant)
    return split3(circulant)


PAD = TILE


def place(buf, k, x, tile, height, value):
    buf[k, x, pl.ds(PAD + tile * TILE, TILE), :] = value
    if tile == 0:
        buf[k, x, pl.ds(PAD + height, TILE), :] = value
    if tile == height // TILE - 1:
        buf[k, x, pl.ds(0, TILE), :] = value


def along_z(field, w1_ref, w2_ref):
    nz = field.shape[1]
    high, mid, low = split3(field)
    part = jnp.dot(jnp.concatenate([high, mid], 1), w1_ref[...], preferred_element_type=jnp.float32)
    rest = jnp.dot(jnp.concatenate([low, high], 1), w2_ref[...], preferred_element_type=jnp.float32)
    return part[:, :nz] + part[:, nz:] + rest


def add_xy(src, k, x, tile, total):
    width = src.shape[1]
    at = PAD + tile * TILE
    for j in range(1, REACH + 1):
        near = src[k, (x + j) % width, pl.ds(at, TILE), :] + src[k, (x - j) % width, pl.ds(at, TILE), :]
        near = near + src[k, x, pl.ds(at + j, TILE), :] + src[k, x, pl.ds(at - j, TILE), :]
        total = total + (-0.5 * COEFFS[j]) * near
    return total


def laplace_kernel(dims, in_ref, field_ref, lap_ref, w1_ref, w2_ref):
    gx, gy, own, nx, ny, nz, pieces, skip = dims
    width, height, cells = gx * nx, gy * ny, nx * ny
    high, mid, low = z_weights(nz)
    for at in (0, nz):
        w1_ref[pl.ds(at, nz), pl.ds(0, nz)] = high
        w1_ref[pl.ds(at, nz), pl.ds(nz, nz)] = mid
    w2_ref[pl.ds(0, nz), :] = high
    w2_ref[pl.ds(nz, nz), :] = low
    for g in range(gx * gy):
        at_x, at_y = (g // gy) * nx, (g % gy) * ny
        for k in range(own):
            for i in range(nx):
                for t in range(ny // TILE):
                    value = in_ref[g, pl.ds(k * cells + i * ny + t * TILE, TILE), :]
                    place(field_ref, k, at_x + i, at_y // TILE + t, height, value)
    field = field_ref[:, :, pl.ds(PAD, height), :].reshape(own * width * height, nz)
    lap_ref[...] = along_z(field, w1_ref, w2_ref).reshape(own, width, height, nz)
    for k in range(own):
        for x in range(width):
            for tile in range(height // TILE):
                rows = pl.ds(tile * TILE, TILE)
                lap_ref[k, x, rows, :] = add_xy(field_ref, k, x, tile, lap_ref[k, x, rows, :])


def filter_kernel(dims, core_ref, field_ref, lap_ref, half_ref, other_ref, w1_ref, w2_ref, out_ref, pot, buf_a, buf_b, zbuf):
    gx, gy, own, nx, ny, nz, pieces, skip = dims
    width, height, cells = gx * nx, gy * ny, nx * ny
    half = cells // 2
    rows = cells // pieces
    middle, first, others = filter_weights(DEGREE)
    shift = -middle - 1.5 * COEFFS[0]

    core = core_ref[0]
    for g in range(gx * gy):
        mine = pl.ds(pl.multiple_of(core * half, TILE), half)
        theirs = pl.ds(pl.multiple_of((1 - core) * half, TILE), half)
        pot[g, mine, :] = half_ref[g, pl.ds(skip, half), :] + shift
        pot[g, theirs, :] = other_ref[g] + shift

    chain = (field_ref, buf_a, buf_b, buf_a)
    steps = [(first, None)] + others
    for step, (scale, back) in enumerate(steps):
        src, dst, old = chain[step], buf_b if step % 2 else buf_a, chain[step - 1]
        last = step == len(steps) - 1
        if step:
            field = src[:, :, pl.ds(PAD, height), :].reshape(own * width * height, nz)
            zbuf[...] = along_z(field, w1_ref, w2_ref).reshape(own, width, height, nz)
        for k in range(own):
            for x in range(width):
                for tile in range(height // TILE):
                    g = (x // nx) * gy + tile * TILE // ny
                    in_pencil = (x % nx) * ny + (tile * TILE) % ny
                    inner = pl.ds(PAD + tile * TILE, TILE)
                    plain = pl.ds(tile * TILE, TILE)
                    if step:
                        total = add_xy(src, k, x, tile, zbuf[k, x, plain, :])
                    else:
                        total = lap_ref[k, x, plain, :]
                    total = total + pot[g, pl.ds(in_pencil, TILE), :] * src[k, x, inner, :]
                    value = scale * total
                    if step:
                        value = value - back * old[k, x, inner, :]
                    if not last:
                        place(dst, k, x, tile, height, value)
                        continue
                    for r in range(0, TILE, TILE // 2):
                        piece, row = divmod(in_pencil + r, rows)
                        to = piece_owner(piece, pieces) * gx * gy + g
                        out_ref[to, pl.ds(k * rows + row, TILE // 2), :] = value[r : r + TILE // 2]


def piece_owner(piece, pieces):
    chips = pieces // 2
    return (piece % chips) * 2 + piece // chips


def first_laplace(packed, dims):
    gx, gy, bands, nx, ny, nz, pieces, skip = dims
    width, height = gx * nx, gy * ny
    vmem = pl.BlockSpec(memory_space=pltpu.VMEM)
    cells = bands * width * height * nz
    return pl.pallas_call(
        functools.partial(laplace_kernel, dims),
        out_shape=(
            jax.ShapeDtypeStruct((bands, width, height + 2 * PAD, nz), jnp.float32),
            jax.ShapeDtypeStruct((bands, width, height, nz), jnp.float32),
            jax.ShapeDtypeStruct((2 * nz, 2 * nz), jnp.bfloat16),
            jax.ShapeDtypeStruct((2 * nz, nz), jnp.bfloat16),
        ),
        in_specs=[vmem],
        out_specs=(vmem,) * 4,
        compiler_params=pltpu.CompilerParams(vmem_limit_bytes=12 * 1024 * 1024),
        cost_estimate=pl.CostEstimate(flops=44 * cells, bytes_accessed=16 * cells, transcendentals=0),
        name="laplace",
    )(packed)


def apply_filter(core, field, laplace, packed, other, weights, dims):
    gx, gy, bands, nx, ny, nz, pieces, skip = dims
    vmem = pl.BlockSpec(memory_space=pltpu.VMEM)
    return pl.pallas_call(
        functools.partial(filter_kernel, dims),
        out_shape=jax.ShapeDtypeStruct((pieces * gx * gy, bands * nx * ny // pieces, nz), jnp.float32),
        in_specs=[pl.BlockSpec(memory_space=pltpu.SMEM)] + [vmem] * 6,
        out_specs=vmem,
        scratch_shapes=[
            pltpu.VMEM((gx * gy, nx * ny, nz), jnp.float32),
            pltpu.VMEM(field.shape, jnp.float32),
            pltpu.VMEM(field.shape, jnp.float32),
            pltpu.VMEM(laplace.shape, jnp.float32),
        ],
        compiler_params=pltpu.CompilerParams(vmem_limit_bytes=12 * 1024 * 1024),
        name="filter",
    )(core, field, laplace, packed, other, *weights)


def margin_kernel(rows, bands, scale, x_ref, out_ref):
    highs, mids, lows = [], [], []
    for r in range(rows):
        high, mid, low = split3(x_ref[pl.ds(r, bands, stride=rows), :])
        highs.append(high)
        mids.append(mid)
        lows.append(low)
    terms = [jnp.concatenate(term, 1) for term in (highs, mids, lows)]
    stacked = jnp.concatenate(terms, 0)
    products = lax.dot_general(stacked, stacked, (((1,), (1,)), ((), ())), preferred_element_type=jnp.float32)

    def block(i, j):
        return products[i * bands : (i + 1) * bands, j * bands : (j + 1) * bands]

    small = block(0, 2) + block(2, 0) + block(1, 1)
    total = (small + (block(0, 1) + block(1, 0)) + block(0, 0)) * scale
    half = bands // 2
    for at, (i, j) in enumerate(((0, 0), (1, 0), (1, 1))):
        part = total[i * half : (i + 1) * half, j * half : (j + 1) * half]
        folds = [part[t * TILE : (t + 1) * TILE] for t in range(half // TILE)]
        out_ref[pl.ds(at * TILE, TILE), :] = jnp.concatenate(folds, 1)


def partial_margin(blocks, bands, scale):
    rows = blocks.shape[0] // bands
    return pl.pallas_call(
        functools.partial(margin_kernel, rows, bands, scale),
        out_shape=jax.ShapeDtypeStruct((3 * TILE, bands // 2 * (bands // 2) // TILE), jnp.float32),
        in_specs=[pl.BlockSpec(memory_space=pltpu.VMEM)],
        out_specs=pl.BlockSpec(memory_space=pltpu.VMEM),
        compiler_params=pltpu.CompilerParams(vmem_limit_bytes=8 * 1024 * 1024),
        name="margin",
    )(blocks)


def eliminate(margin, between):
    bands = margin.shape[0]
    tiles = bands // TILE
    row_at = lax.broadcasted_iota(jnp.int32, (bands, bands), 0)
    col_at = lax.broadcasted_iota(jnp.int32, (bands, bands), 1)
    both = jnp.concatenate([margin, jnp.where(row_at == col_at, 1.0, 0.0)], 1)
    width = 2 * bands
    lines = lax.broadcasted_iota(jnp.int32, (TILE, width), 0)
    both = [both[t * TILE : (t + 1) * TILE] for t in range(tiles)]

    def spread(t, at):
        return jnp.broadcast_to(both[t][:, at : at + 1], (TILE, width))

    def line_of(value, at):
        return jnp.broadcast_to(value[at : at + 1, :], (TILE, width))

    heads = [spread(0, c) for c in range(TILE)]
    for p in range(tiles):
        between(p)
        here = range(p * TILE, (p + 1) * TILE)
        panel = [{t: spread(t, at) for t in range(p + 1, tiles)} for at in here]
        later = [spread(p + 1, at + TILE) for at in here] if p + 1 < tiles else []
        square = [[line_of(heads[c], d) if d >= c else None for d in range(TILE)] for c in range(TILE)]
        pivots = None
        for j in range(TILE):
            pivot = square[j][j]
            pivots = pivot if j == 0 else jnp.where(lines == j, pivot, pivots)
            ratio = pl.reciprocal(pivot, approx=True)
            for c in range(j + 1, TILE):
                for d in range(c, TILE):
                    square[c][d] = square[c][d] - (square[j][c] * square[j][d]) * ratio
            factor = {t: panel[j][t] * ratio for t in range(p + 1, tiles)}
            factor[p] = jnp.where(lines > j, heads[j] * ratio, 0.0)
            for c in range(j + 1, TILE):
                heads[c] = heads[c] - factor[p] * square[j][c]
                for t in range(p + 1, tiles):
                    panel[c][t] = panel[c][t] - factor[t] * square[j][c]
            for c, column in enumerate(later):
                later[c] = column - factor[p + 1] * line_of(panel[j][p + 1], c)
            line = line_of(both[p], j)
            for t in range(p, tiles):
                both[t] = both[t] - factor[t] * line
        heads = later
        both[p] = both[p] * lax.rsqrt(pivots)
    return jnp.concatenate(both, 0)[:, bands:]


def rotate_kernel(dims, place_ref, *refs):
    rows, bands, own, pieces, tiles = dims
    margins, parts = refs[: pieces // 2], refs[pieces // 2 : -3]
    out_ref, inv_ref, split_ref = refs[-3:]
    folded = margins[0][...]
    for term in margins[1:]:
        folded = folded + term[...]
    half = bands // 2
    quarters = []
    for at in range(3):
        part = folded[at * TILE : (at + 1) * TILE]
        quarters.append(jnp.concatenate([part[:, t * half : (t + 1) * half] for t in range(half // TILE)], 0))
    low, cross, high = quarters
    margin = jnp.concatenate(
        [jnp.concatenate([low, cross.T], 1), jnp.concatenate([cross, high], 1)], 0
    )
    jobs = [(part, r) for part in range(pieces) for r in range(rows)]
    nz = parts[0].shape[1]

    def split_some(step):
        share = -(-len(jobs) // tiles)
        for at in range(step * share, min(len(jobs), (step + 1) * share)):
            part, r = jobs[at]
            terms_of = split3(parts[part][pl.ds(r, bands, stride=rows), :])
            for i, term in enumerate(terms_of):
                split_ref[at // 2, pl.ds(i * bands, bands), pl.ds((at % 2) * nz, nz)] = term

    inv_ref[...] = eliminate(margin, split_some)
    first = pl.multiple_of(place_ref[0], TILE)
    high, mid, low = split3(inv_ref[pl.ds(first, own), :])
    zero = jnp.zeros_like(high)
    left = jnp.concatenate(
        [
            jnp.concatenate([high, high, high], 1),
            jnp.concatenate([mid, mid, zero], 1),
            jnp.concatenate([low, zero, zero], 1),
        ],
        0,
    )
    for pair in range(len(jobs) // 2):
        product = jnp.dot(left, split_ref[pair], preferred_element_type=jnp.float32)
        value = product[:own] + (product[own : 2 * own] + product[2 * own :])
        for i in range(2):
            part, r = jobs[2 * pair + i]
            start = place_ref[1 + part] + r
            out_ref[pl.ds(start, own, stride=rows * pieces), :] = value[:, i * nz : (i + 1) * nz]


def rotate(place, margins, parts, own, bands):
    pieces = len(parts)
    rows = parts[0].shape[0] // bands
    nz = parts[0].shape[1]
    vmem = pl.BlockSpec(memory_space=pltpu.VMEM)
    dims = (rows, bands, own, pieces, bands // TILE)
    return pl.pallas_call(
        functools.partial(rotate_kernel, dims),
        out_shape=jax.ShapeDtypeStruct((own * rows * pieces, nz), jnp.float32),
        in_specs=[pl.BlockSpec(memory_space=pltpu.SMEM)] + [vmem] * (len(margins) + pieces),
        out_specs=vmem,
        scratch_shapes=[
            pltpu.VMEM((bands, bands), jnp.float32),
            pltpu.VMEM((rows * pieces // 2, 3 * bands, 2 * nz), jnp.bfloat16),
        ],
        compiler_params=pltpu.CompilerParams(vmem_limit_bytes=12 * 1024 * 1024),
        name="rotate",
    )(place, *margins, *parts)


def on_device_fields(start_bands, potential):
    own_bands, nx, ny, nz = start_bands.shape
    gx, gy, chips = lax.axis_size("gx"), lax.axis_size("gy"), lax.axis_size("chip")
    pieces = 2 * chips
    grid = gx * gy
    own = own_bands // grid
    cells = nx * ny
    bands = own_bands * pieces
    rows = cells // pieces
    chip, core = lax.axis_index("chip"), lax.axis_index("core")
    swap = [(0, 1), (1, 0)]

    fields = start_bands.reshape(grid, own * cells, nz)
    flat_potential = potential.reshape(cells, nz)
    half = cells // 2
    own_half = lax.dynamic_slice_in_dim(flat_potential, core * half, half, 0)
    packed = jnp.concatenate([fields, jnp.broadcast_to(own_half[None], (grid, half, nz))], 1)
    packed = lax.all_to_all(packed, ("gx", "gy"), 0, 0)
    other = lax.ppermute(packed[:, own * cells :, :], "core", swap)
    dims = (gx, gy, own, nx, ny, nz, pieces, own * cells)
    field, laplace, *weights = first_laplace(packed, dims)
    filtered = apply_filter(core.reshape(1), field, laplace, packed, other, weights, dims)
    blocks = lax.all_to_all(filtered, ("chip", "core", "gx", "gy"), 0, 0).reshape(bands * rows, nz)

    def tied(value, first):
        return lax.optimization_barrier((value, first))[0]

    def copies(value, axis):
        count = lax.axis_size(axis)
        pairs = [[(i, i ^ mask) for i in range(count)] for mask in range(1, count)]
        return [value] + [lax.ppermute(value, axis, pair) for pair in pairs]

    margin = partial_margin(blocks, bands, 1.0 / (cells * nz * grid))
    parts = copies(tied(blocks, margin), "chip")
    margin = sum(copies(margin, "core"))
    crossed = [lax.ppermute(tied(blocks, margin), "core", swap)]
    for axis in ("gx", "gy"):
        margin = sum(copies(margin, axis))
    margins = copies(margin, "chip")
    crossed += [lax.ppermute(tied(part, margin), "core", swap) for part in parts[1:]]
    parts += crossed
    offsets = [(core * chips + (chip ^ mask)) * rows for mask in range(chips)]
    offsets += [at + (1 - 2 * core) * chips * rows for at in offsets]
    place = jnp.stack([(chip * 2 + core) * own_bands] + offsets).astype(jnp.int32)
    rotated = rotate(place, margins, parts, own_bands, bands)
    return rotated.reshape(start_bands.shape)


def power_of_two(count):
    return count & (count - 1) == 0


def whole_fields(mesh, shape):
    gx, gy, pieces = mesh.shape["gx"], mesh.shape["gy"], mesh.shape["band"]
    bands, nx, ny, nz = shape[0], shape[1] // gx, shape[2] // gy, shape[3]
    own_bands, cells = bands // pieces, nx * ny
    return (
        own_bands % (gx * gy) == 0
        and own_bands % (2 * TILE) == 0
        and pieces % 2 == 0
        and power_of_two(pieces)
        and ny % TILE == 0
        and nz % 128 == 0
        and bands // 2 * (bands // 2) // TILE % 128 == 0
        and cells % (2 * TILE) == 0
        and cells % (pieces * TILE // 2) == 0
        and (own_bands // (gx * gy)) * (cells // pieces) % TILE == 0
        and shape[1] > 2 * REACH
    )


def solution(mesh):
    def step(start_bands, potential):
        if whole_fields(mesh, start_bands.shape):
            chips = mesh.shape["band"] // 2
            rest = mesh.devices.shape[1:]
            split = Mesh(mesh.devices.reshape((chips, 2) + rest), ("chip", "core") + mesh.axis_names[1:])
            program, band = on_device_fields, ("chip", "core")
        else:
            split, program, band = mesh, on_device_halo, "band"
        return jax.shard_map(
            program,
            mesh=split,
            in_specs=(P(band, "gx", "gy", None), P("gx", "gy", None)),
            out_specs=P(band, "gx", "gy", None),
            check_vma=False,
        )(start_bands, potential)

    return step
```

```python
import functools
import math

import jax
import jax.numpy as jnp
from jax import lax
from jax.experimental import pallas as pl
from jax.experimental.pallas import tpu as pltpu
from jax.sharding import Mesh, PartitionSpec as P

DEGREE = 4


COEFFS = (
    -5369.0 / 1800.0,
    12.0 / 7.0,
    -15.0 / 56.0,
    10.0 / 189.0,
    -1.0 / 112.0,
    2.0 / 1925.0,
    -1.0 / 16632.0,
)
REACH = len(COEFFS) - 1
LOWER_END = -0.5
CUT_LOW = 3.0
CUT_HIGH = 12.7
TILE = 8


def filter_weights(degree):
    half_width = (CUT_HIGH - CUT_LOW) / 2.0
    middle = (CUT_HIGH + CUT_LOW) / 2.0
    sigma = half_width / (LOWER_END - middle)
    tau = 2.0 / sigma
    first = sigma / half_width
    others = []
    for index in range(degree - 1):
        sigma_new = 1.0 / (tau - sigma)
        others.append((2.0 * sigma_new / half_width, sigma * sigma_new))
        sigma = sigma_new
    return (middle, first, others)


def padded_2(block, sides, width):
    for axis, dim in sides:
        count = lax.axis_size(axis)
        forward = [(i, i + 1) for i in range(count - 1)]
        forward.append((count - 1, 0))
        backward = [(target, source) for source, target in forward]
        low = lax.ppermute(
            lax.slice_in_dim(block, block.shape[dim] - width, None, axis=dim), axis, forward
        )
        high = lax.ppermute(lax.slice_in_dim(block, 0, width, axis=dim), axis, backward)
        block = jnp.concatenate([low, block, high], axis=dim)
    return block


def hamiltonian(field, potential):
    width_x = field.shape[1]
    width_y = field.shape[2]
    padded = padded_2(field, (("gx", 1), ("gy", 2)), REACH)
    laplace = 3.0 * COEFFS[0] * field
    for offset in range(1, REACH + 1):
        ahead_x = padded[:, REACH + offset : REACH + offset + width_x, REACH : REACH + width_y]
        behind_x = padded[:, REACH - offset : REACH - offset + width_x, REACH : REACH + width_y]
        ahead_y = padded[:, REACH : REACH + width_x, REACH + offset : REACH + offset + width_y]
        behind_y = padded[:, REACH : REACH + width_x, REACH - offset : REACH - offset + width_y]
        neighbours = ahead_x + behind_x
        neighbours = neighbours + ahead_y + behind_y
        neighbours = neighbours + jnp.roll(field, -offset, 3) + jnp.roll(field, offset, 3)
        laplace = laplace + COEFFS[offset] * neighbours
    return -0.5 * laplace + potential * field


def chebyshev(field, potential):
    middle, first, others = filter_weights(DEGREE)
    current = (hamiltonian(field, potential) - middle * field) * first
    previous = field
    for scale_now, scale_back in others:
        following = (
            hamiltonian(current, potential) - middle * current
        ) * scale_now - scale_back * previous
        previous = current
        current = following
    return current


def invert_factor(margin, identity):
    lower_factor = jnp.linalg.cholesky(margin)
    return jax.scipy.linalg.solve_triangular(lower_factor, identity, lower=True)


def on_device_halo(start_bands, potential):
    filtered = chebyshev(start_bands, potential)
    own_bands = filtered.shape[0]
    flattened = filtered.reshape(own_bands, -1)
    total_cells = flattened.shape[1] * lax.axis_size("gx") * lax.axis_size("gy")
    all_bands = own_bands * lax.axis_size("band")
    identity = jnp.eye(all_bands, dtype=jnp.float32)
    products = jnp.dot(
        flattened,
        lax.all_gather(flattened, "band", axis=0, tiled=True).T,
        precision=lax.Precision.HIGHEST,
        preferred_element_type=jnp.float32,
    )
    first_row = lax.axis_index("band") * own_bands
    summed = lax.psum(products, ("gx", "gy"))
    margin = lax.all_gather(summed, "band", axis=0, tiled=True) * (1.0 / total_cells)
    inverse = invert_factor(margin, identity)
    own_rows = lax.dynamic_slice_in_dim(inverse, first_row, own_bands, 0)
    rotated = jnp.dot(
        own_rows,
        lax.all_gather(flattened, "band", axis=0, tiled=True),
        precision=lax.Precision.HIGHEST,
        preferred_element_type=jnp.float32,
    )
    return rotated.reshape(filtered.shape)


def split3(value):
    high = value.astype(jnp.bfloat16)
    rest = value - high.astype(jnp.float32)
    mid = rest.astype(jnp.bfloat16)
    low = (rest - mid.astype(jnp.float32)).astype(jnp.bfloat16)
    return high, mid, low


def z_weights(nz):
    row = lax.broadcasted_iota(jnp.int32, (nz, nz), 0)
    col = lax.broadcasted_iota(jnp.int32, (nz, nz), 1)
    apart = jnp.abs(row - col)
    apart = jnp.minimum(apart, nz - apart)
    circulant = jnp.zeros((nz, nz), jnp.float32)
    for offset in range(1, REACH + 1):
        circulant = jnp.where(apart == offset, -0.5 * COEFFS[offset], circulant)
    return split3(circulant)


PAD = TILE


def place(buf, k, x, tile, height, value):
    buf[k, x, pl.ds(PAD + tile * TILE, TILE), :] = value
    if tile == 0:
        buf[k, x, pl.ds(PAD + height, TILE), :] = value
    if tile == height // TILE - 1:
        buf[k, x, pl.ds(0, TILE), :] = value


def along_z(field, w1_ref, w2_ref):
    nz = field.shape[1]
    high, mid, low = split3(field)
    part = jnp.dot(jnp.concatenate([high, mid], 1), w1_ref[...], preferred_element_type=jnp.float32)
    rest = jnp.dot(jnp.concatenate([low, high], 1), w2_ref[...], preferred_element_type=jnp.float32)
    return part[:, :nz] + part[:, nz:] + rest


def add_xy(src, k, x, tile, total):
    width = src.shape[1]
    at = PAD + tile * TILE
    for j in range(1, REACH + 1):
        near = src[k, (x + j) % width, pl.ds(at, TILE), :] + src[k, (x - j) % width, pl.ds(at, TILE), :]
        near = near + src[k, x, pl.ds(at + j, TILE), :] + src[k, x, pl.ds(at - j, TILE), :]
        total = total + (-0.5 * COEFFS[j]) * near
    return total


def laplace_kernel(dims, in_ref, field_ref, lap_ref, w1_ref, w2_ref):
    gx, gy, own, nx, ny, nz, pieces, skip = dims
    width, height, cells = gx * nx, gy * ny, nx * ny
    high, mid, low = z_weights(nz)
    for at in (0, nz):
        w1_ref[pl.ds(at, nz), pl.ds(0, nz)] = high
        w1_ref[pl.ds(at, nz), pl.ds(nz, nz)] = mid
    w2_ref[pl.ds(0, nz), :] = high
    w2_ref[pl.ds(nz, nz), :] = low
    for g in range(gx * gy):
        at_x, at_y = (g // gy) * nx, (g % gy) * ny
        for k in range(own):
            for i in range(nx):
                for t in range(ny // TILE):
                    value = in_ref[g, pl.ds(k * cells + i * ny + t * TILE, TILE), :]
                    place(field_ref, k, at_x + i, at_y // TILE + t, height, value)
    field = field_ref[:, :, pl.ds(PAD, height), :].reshape(own * width * height, nz)
    lap_ref[...] = along_z(field, w1_ref, w2_ref).reshape(own, width, height, nz)
    for k in range(own):
        for x in range(width):
            for tile in range(height // TILE):
                rows = pl.ds(tile * TILE, TILE)
                lap_ref[k, x, rows, :] = add_xy(field_ref, k, x, tile, lap_ref[k, x, rows, :])


def filter_kernel(dims, field_ref, lap_ref, half_ref, other_ref, w1_ref, w2_ref, out_ref, pot, buf_a, buf_b, zbuf):
    gx, gy, own, nx, ny, nz, pieces, skip = dims
    width, height, cells = gx * nx, gy * ny, nx * ny
    half = cells // 2
    rows = cells // pieces
    middle, first, others = filter_weights(DEGREE)
    shift = -middle - 1.5 * COEFFS[0]

    core = lax.axis_index("core")
    for g in range(gx * gy):
        mine = pl.ds(pl.multiple_of(core * half, TILE), half)
        theirs = pl.ds(pl.multiple_of((1 - core) * half, TILE), half)
        pot[g, mine, :] = half_ref[g, pl.ds(skip, half), :] + shift
        pot[g, theirs, :] = other_ref[g] + shift

    chain = (field_ref, buf_a, buf_b, buf_a)
    steps = [(first, None)] + others
    for step, (scale, back) in enumerate(steps):
        src, dst, old = chain[step], buf_b if step % 2 else buf_a, chain[step - 1]
        last = step == len(steps) - 1
        if step:
            field = src[:, :, pl.ds(PAD, height), :].reshape(own * width * height, nz)
            zbuf[...] = along_z(field, w1_ref, w2_ref).reshape(own, width, height, nz)
        for k in range(own):
            for x in range(width):
                for tile in range(height // TILE):
                    g = (x // nx) * gy + tile * TILE // ny
                    in_pencil = (x % nx) * ny + (tile * TILE) % ny
                    inner = pl.ds(PAD + tile * TILE, TILE)
                    plain = pl.ds(tile * TILE, TILE)
                    if step:
                        total = add_xy(src, k, x, tile, zbuf[k, x, plain, :])
                    else:
                        total = lap_ref[k, x, plain, :]
                    total = total + pot[g, pl.ds(in_pencil, TILE), :] * src[k, x, inner, :]
                    value = scale * total
                    if step:
                        value = value - back * old[k, x, inner, :]
                    if not last:
                        place(dst, k, x, tile, height, value)
                        continue
                    for r in range(0, TILE, TILE // 2):
                        piece, row = divmod(in_pencil + r, rows)
                        to = piece_owner(piece, pieces) * gx * gy + g
                        out_ref[to, pl.ds(k * rows + row, TILE // 2), :] = value[r : r + TILE // 2]


def piece_owner(piece, pieces):
    chips = pieces // 2
    return (piece % chips) * 2 + piece // chips


def first_laplace(packed, dims):
    gx, gy, bands, nx, ny, nz, pieces, skip = dims
    width, height = gx * nx, gy * ny
    vmem = pl.BlockSpec(memory_space=pltpu.VMEM)
    cells = bands * width * height * nz
    return pl.pallas_call(
        functools.partial(laplace_kernel, dims),
        out_shape=(
            jax.ShapeDtypeStruct((bands, width, height + 2 * PAD, nz), jnp.float32),
            jax.ShapeDtypeStruct((bands, width, height, nz), jnp.float32),
            jax.ShapeDtypeStruct((2 * nz, 2 * nz), jnp.bfloat16),
            jax.ShapeDtypeStruct((2 * nz, nz), jnp.bfloat16),
        ),
        in_specs=[vmem],
        out_specs=(vmem,) * 4,
        compiler_params=pltpu.CompilerParams(vmem_limit_bytes=12 * 1024 * 1024),
        cost_estimate=pl.CostEstimate(flops=44 * cells, bytes_accessed=16 * cells, transcendentals=0),
        name="laplace",
    )(packed)


def apply_filter(field, laplace, packed, other, weights, dims):
    gx, gy, bands, nx, ny, nz, pieces, skip = dims
    vmem = pl.BlockSpec(memory_space=pltpu.VMEM)
    return pl.pallas_call(
        functools.partial(filter_kernel, dims),
        out_shape=jax.ShapeDtypeStruct((pieces * gx * gy, bands * nx * ny // pieces, nz), jnp.float32),
        in_specs=[vmem] * 6,
        out_specs=vmem,
        scratch_shapes=[
            pltpu.VMEM((gx * gy, nx * ny, nz), jnp.float32),
            pltpu.VMEM(field.shape, jnp.float32),
            pltpu.VMEM(field.shape, jnp.float32),
            pltpu.VMEM(laplace.shape, jnp.float32),
        ],
        compiler_params=pltpu.CompilerParams(vmem_limit_bytes=12 * 1024 * 1024),
        name="filter",
    )(field, laplace, packed, other, *weights)


def margin_kernel(rows, bands, scale, x_ref, out_ref):
    highs, mids, lows = [], [], []
    for r in range(rows):
        high, mid, low = split3(x_ref[pl.ds(r, bands, stride=rows), :])
        highs.append(high)
        mids.append(mid)
        lows.append(low)
    terms = [jnp.concatenate(term, 1) for term in (highs, mids, lows)]
    stacked = jnp.concatenate(terms, 0)
    products = lax.dot_general(stacked, stacked, (((1,), (1,)), ((), ())), preferred_element_type=jnp.float32)

    def block(i, j):
        return products[i * bands : (i + 1) * bands, j * bands : (j + 1) * bands]

    small = block(0, 2) + block(2, 0) + block(1, 1)
    total = (small + (block(0, 1) + block(1, 0)) + block(0, 0)) * scale
    out_ref[:, pl.ds(0, bands)] = total[: bands // 2]
    out_ref[:, pl.ds(bands, bands)] = total[bands // 2 :]


def partial_margin(blocks, bands, scale):
    rows = blocks.shape[0] // bands
    return pl.pallas_call(
        functools.partial(margin_kernel, rows, bands, scale),
        out_shape=jax.ShapeDtypeStruct((bands // 2, 2 * bands), jnp.float32),
        in_specs=[pl.BlockSpec(memory_space=pltpu.VMEM)],
        out_specs=pl.BlockSpec(memory_space=pltpu.VMEM),
        compiler_params=pltpu.CompilerParams(vmem_limit_bytes=8 * 1024 * 1024),
        name="margin",
    )(blocks)


def eliminate(folded):
    bands = folded.shape[1] // 2
    tiles = bands // TILE
    width = 2 * bands
    lines = lax.broadcasted_iota(jnp.int32, (TILE, width), 0)
    lanes = lax.broadcasted_iota(jnp.int32, (TILE, width), 1)
    swapped = jnp.concatenate([folded[:, bands:], folded[:, :bands]], 1)
    both = []
    for t in range(tiles):
        at = t * TILE % (bands // 2)
        right = (swapped if t < tiles // 2 else folded)[at : at + TILE]
        eye = jnp.where(lines + t * TILE == lanes % bands, 1.0, 0.0)
        both.append([eye, jnp.where(lanes < bands, eye, right)])

    def spread(t, at):
        return jnp.broadcast_to(both[t][1][:, bands + at : bands + at + 1], (TILE, width))

    def line_of(value, at):
        return jnp.broadcast_to(value[at : at + 1, :], (TILE, width))

    heads = [spread(0, c) for c in range(TILE)]
    for p in range(tiles):
        here = range(p * TILE, (p + 1) * TILE)
        panel = [{t: spread(t, at) for t in range(p + 1, tiles)} for at in here]
        later = [spread(p + 1, at + TILE) for at in here] if p + 1 < tiles else []
        square = [[line_of(heads[c], d) if d >= c else None for d in range(TILE)] for c in range(TILE)]
        pivots = None
        for j in range(TILE):
            pivot = square[j][j]
            pivots = pivot if j == 0 else jnp.where(lines == j, pivot, pivots)
            ratio = pl.reciprocal(pivot, approx=True)
            for c in range(j + 1, TILE):
                for d in range(c, TILE):
                    square[c][d] = square[c][d] - (square[j][c] * square[j][d]) * ratio
            factor = {t: panel[j][t] * ratio for t in range(p + 1, tiles)}
            factor[p] = jnp.where(lines > j, heads[j] * ratio, 0.0)
            for c in range(j + 1, TILE):
                heads[c] = heads[c] - factor[p] * square[j][c]
                for t in range(p + 1, tiles):
                    panel[c][t] = panel[c][t] - factor[t] * square[j][c]
            for c, column in enumerate(later):
                later[c] = column - factor[p + 1] * line_of(panel[j][p + 1], c)
            pair = [line_of(value, j) for value in both[p]]
            for t in range(p, tiles):
                both[t] = [value - factor[t] * line for value, line in zip(both[t], pair)]
        heads = later
        scale = lax.rsqrt(pivots)
        both[p] = [value * scale for value in both[p]]
    return [jnp.concatenate(value, 1) for value in both]


def split_pair(split_ref, at, part, pair, bands):
    rows = part.shape[0] // bands
    nz = part.shape[1]
    for i in range(2):
        terms = split3(part[pl.ds(2 * pair + i, bands, stride=rows), :])
        for j, term in enumerate(terms):
            split_ref[at, pl.ds(j * bands, bands), pl.ds(i * nz, nz)] = term


def inverse_kernel(dims, *refs):
    bands, own = dims
    margins, left_ref, inv_ref = refs[:-2], refs[-2], refs[-1]
    folded = margins[0][...]
    for term in margins[1:]:
        folded = folded + term[...]
    for t, value in enumerate(eliminate(folded)):
        inv_ref[pl.ds(t * TILE, TILE), :] = value
    first = pl.multiple_of((lax.axis_index("chip") * 2 + lax.axis_index("core")) * own, TILE)
    rows = inv_ref[pl.ds(first, own), pl.ds(0, 3 * bands)]
    lanes = lax.broadcasted_iota(jnp.int32, rows.shape, 1)
    high = rows.astype(jnp.bfloat16)
    rest = rows - high.astype(jnp.float32)
    mid = rest.astype(jnp.bfloat16)
    low = rest - mid.astype(jnp.float32)
    left_ref[pl.ds(0, own), :] = high
    left_ref[pl.ds(own, own), :] = jnp.where(lanes < 2 * bands, rest, 0.0).astype(jnp.bfloat16)
    left_ref[pl.ds(2 * own, own), :] = jnp.where(lanes < bands, low, 0.0).astype(jnp.bfloat16)


def inverse_rows(margins, own, bands):
    vmem = pl.BlockSpec(memory_space=pltpu.VMEM)
    return pl.pallas_call(
        functools.partial(inverse_kernel, (bands, own)),
        out_shape=jax.ShapeDtypeStruct((3 * own, 3 * bands), jnp.bfloat16),
        in_specs=[vmem] * len(margins),
        out_specs=vmem,
        scratch_shapes=[pltpu.VMEM((bands, 4 * bands), jnp.float32)],
        compiler_params=pltpu.CompilerParams(vmem_limit_bytes=4 * 1024 * 1024),
        name="inverse",
    )(*margins)


def rotate_kernel(dims, left_ref, *refs):
    bands, own = dims
    parts, out_ref = refs[:-1], refs[-1]
    rows = parts[0].shape[0] // bands
    nz = parts[0].shape[1]
    left = left_ref[...]
    chips = len(parts) // 2
    chip, core = lax.axis_index("chip"), lax.axis_index("core")
    for index, part in enumerate(parts):
        piece = (core ^ (index // chips)) * chips + (chip ^ (index % chips))
        for r in range(0, rows, 2):
            terms = [split3(part[pl.ds(r + i, bands, stride=rows), :]) for i in range(2)]
            block = jnp.concatenate([jnp.concatenate(term, 1) for term in zip(*terms)], 0)
            product = jnp.dot(left, block, preferred_element_type=jnp.float32)
            value = product[:own] + (product[own : 2 * own] + product[2 * own :])
            for i in range(2):
                start = piece * rows + r + i
                out_ref[pl.ds(start, own, stride=rows * len(parts)), :] = value[:, i * nz : (i + 1) * nz]


def rotate(left, parts, bands):
    rows = parts[0].shape[0] // bands
    own = left.shape[0] // 3
    nz = parts[0].shape[1]
    vmem = pl.BlockSpec(memory_space=pltpu.VMEM)
    return pl.pallas_call(
        functools.partial(rotate_kernel, (bands, own)),
        out_shape=jax.ShapeDtypeStruct((own * rows * len(parts), nz), jnp.float32),
        in_specs=[vmem] * (1 + len(parts)),
        out_specs=vmem,
        compiler_params=pltpu.CompilerParams(vmem_limit_bytes=6 * 1024 * 1024),
        name="rotate",
    )(left, *parts)


def on_device_fields(start_bands, potential):
    own_bands, nx, ny, nz = start_bands.shape
    gx, gy, chips = lax.axis_size("gx"), lax.axis_size("gy"), lax.axis_size("chip")
    pieces = 2 * chips
    grid = gx * gy
    own = own_bands // grid
    cells = nx * ny
    bands = own_bands * pieces
    rows = cells // pieces
    core = lax.axis_index("core")
    swap = [(0, 1), (1, 0)]

    fields = start_bands.reshape(grid, own * cells, nz)
    flat_potential = potential.reshape(cells, nz)
    half = cells // 2
    own_half = lax.dynamic_slice_in_dim(flat_potential, core * half, half, 0)
    packed = jnp.concatenate([fields, jnp.broadcast_to(own_half[None], (grid, half, nz))], 1)
    packed = lax.all_to_all(packed, ("gx", "gy"), 0, 0)
    other = lax.ppermute(packed[:, own * cells :, :], "core", swap)
    dims = (gx, gy, own, nx, ny, nz, pieces, own * cells)
    field, laplace, *weights = first_laplace(packed, dims)
    filtered = apply_filter(field, laplace, packed, other, weights, dims)
    blocks = lax.all_to_all(filtered, ("chip", "core", "gx", "gy"), 0, 0).reshape(bands * rows, nz)

    def tied(value, first):
        return lax.optimization_barrier((value, first))[0]

    def copies(value, *axes):
        count = math.prod(lax.axis_size(axis) for axis in axes)
        pairs = [[(i, i ^ mask) for i in range(count)] for mask in range(1, count)]
        return [value] + [lax.ppermute(value, axes, pair) for pair in pairs]

    margin = partial_margin(blocks, bands, 1.0 / (cells * nz * grid))
    margin = sum(copies(margin, "chip", "core"))
    parts = copies(tied(blocks, margin), "chip")
    crossed = [lax.ppermute(tied(blocks, margin), "core", swap)]
    margin = sum(copies(margin, "gx"))
    margins = copies(margin, "gy")
    far, margins = lax.optimization_barrier((parts[1:], margins))
    parts += crossed + [lax.ppermute(part, "core", swap) for part in far]
    left = inverse_rows(margins, own_bands, bands)
    rotated = rotate(left, parts, bands)
    return rotated.reshape(start_bands.shape)


def power_of_two(count):
    return count & (count - 1) == 0


def whole_fields(mesh, shape):
    gx, gy, pieces = mesh.shape["gx"], mesh.shape["gy"], mesh.shape["band"]
    bands, nx, ny, nz = shape[0], shape[1] // gx, shape[2] // gy, shape[3]
    own_bands, cells = bands // pieces, nx * ny
    return (
        own_bands % (gx * gy) == 0
        and own_bands % (2 * TILE) == 0
        and pieces % 2 == 0
        and power_of_two(pieces)
        and ny % TILE == 0
        and nz % 128 == 0
        and bands % 64 == 0
        and cells % (2 * TILE) == 0
        and cells % (pieces * TILE // 2) == 0
        and pieces > 2
        and (own_bands // (gx * gy)) * (cells // pieces) % TILE == 0
        and shape[1] > 2 * REACH
    )


def solution(mesh):
    def step(start_bands, potential):
        if whole_fields(mesh, start_bands.shape):
            chips = mesh.shape["band"] // 2
            rest = mesh.devices.shape[1:]
            split = Mesh(mesh.devices.reshape((chips, 2) + rest), ("chip", "core") + mesh.axis_names[1:])
            program, band = on_device_fields, ("chip", "core")
        else:
            split, program, band = mesh, on_device_halo, "band"
        return jax.shard_map(
            program,
            mesh=split,
            in_specs=(P(band, "gx", "gy", None), P("gx", "gy", None)),
            out_specs=P(band, "gx", "gy", None),
            check_vma=False,
        )(start_bands, potential)

    return step
```

```python
import functools
import math

import jax
import jax.numpy as jnp
from jax import lax
from jax.experimental import pallas as pl
from jax.experimental.pallas import tpu as pltpu
from jax.sharding import Mesh, PartitionSpec as P

DEGREE = 4


COEFFS = (
    -5369.0 / 1800.0,
    12.0 / 7.0,
    -15.0 / 56.0,
    10.0 / 189.0,
    -1.0 / 112.0,
    2.0 / 1925.0,
    -1.0 / 16632.0,
)
REACH = len(COEFFS) - 1
LOWER_END = -0.5
CUT_LOW = 3.0
CUT_HIGH = 12.7
TILE = 8


def filter_weights(degree):
    half_width = (CUT_HIGH - CUT_LOW) / 2.0
    middle = (CUT_HIGH + CUT_LOW) / 2.0
    sigma = half_width / (LOWER_END - middle)
    tau = 2.0 / sigma
    first = sigma / half_width
    others = []
    for index in range(degree - 1):
        sigma_new = 1.0 / (tau - sigma)
        others.append((2.0 * sigma_new / half_width, sigma * sigma_new))
        sigma = sigma_new
    return (middle, first, others)


def padded_2(block, sides, width):
    for axis, dim in sides:
        count = lax.axis_size(axis)
        forward = [(i, i + 1) for i in range(count - 1)]
        forward.append((count - 1, 0))
        backward = [(target, source) for source, target in forward]
        low = lax.ppermute(
            lax.slice_in_dim(block, block.shape[dim] - width, None, axis=dim), axis, forward
        )
        high = lax.ppermute(lax.slice_in_dim(block, 0, width, axis=dim), axis, backward)
        block = jnp.concatenate([low, block, high], axis=dim)
    return block


def hamiltonian(field, potential):
    width_x = field.shape[1]
    width_y = field.shape[2]
    padded = padded_2(field, (("gx", 1), ("gy", 2)), REACH)
    laplace = 3.0 * COEFFS[0] * field
    for offset in range(1, REACH + 1):
        ahead_x = padded[:, REACH + offset : REACH + offset + width_x, REACH : REACH + width_y]
        behind_x = padded[:, REACH - offset : REACH - offset + width_x, REACH : REACH + width_y]
        ahead_y = padded[:, REACH : REACH + width_x, REACH + offset : REACH + offset + width_y]
        behind_y = padded[:, REACH : REACH + width_x, REACH - offset : REACH - offset + width_y]
        neighbours = ahead_x + behind_x
        neighbours = neighbours + ahead_y + behind_y
        neighbours = neighbours + jnp.roll(field, -offset, 3) + jnp.roll(field, offset, 3)
        laplace = laplace + COEFFS[offset] * neighbours
    return -0.5 * laplace + potential * field


def chebyshev(field, potential):
    middle, first, others = filter_weights(DEGREE)
    current = (hamiltonian(field, potential) - middle * field) * first
    previous = field
    for scale_now, scale_back in others:
        following = (
            hamiltonian(current, potential) - middle * current
        ) * scale_now - scale_back * previous
        previous = current
        current = following
    return current


def invert_factor(margin, identity):
    lower_factor = jnp.linalg.cholesky(margin)
    return jax.scipy.linalg.solve_triangular(lower_factor, identity, lower=True)


def on_device_halo(start_bands, potential):
    filtered = chebyshev(start_bands, potential)
    own_bands = filtered.shape[0]
    flattened = filtered.reshape(own_bands, -1)
    total_cells = flattened.shape[1] * lax.axis_size("gx") * lax.axis_size("gy")
    all_bands = own_bands * lax.axis_size("band")
    identity = jnp.eye(all_bands, dtype=jnp.float32)
    products = jnp.dot(
        flattened,
        lax.all_gather(flattened, "band", axis=0, tiled=True).T,
        precision=lax.Precision.HIGHEST,
        preferred_element_type=jnp.float32,
    )
    first_row = lax.axis_index("band") * own_bands
    summed = lax.psum(products, ("gx", "gy"))
    margin = lax.all_gather(summed, "band", axis=0, tiled=True) * (1.0 / total_cells)
    inverse = invert_factor(margin, identity)
    own_rows = lax.dynamic_slice_in_dim(inverse, first_row, own_bands, 0)
    rotated = jnp.dot(
        own_rows,
        lax.all_gather(flattened, "band", axis=0, tiled=True),
        precision=lax.Precision.HIGHEST,
        preferred_element_type=jnp.float32,
    )
    return rotated.reshape(filtered.shape)


def split3(value):
    high = value.astype(jnp.bfloat16)
    rest = value - high.astype(jnp.float32)
    mid = rest.astype(jnp.bfloat16)
    low = (rest - mid.astype(jnp.float32)).astype(jnp.bfloat16)
    return high, mid, low


def z_weights(nz):
    row = lax.broadcasted_iota(jnp.int32, (nz, nz), 0)
    col = lax.broadcasted_iota(jnp.int32, (nz, nz), 1)
    apart = jnp.abs(row - col)
    apart = jnp.minimum(apart, nz - apart)
    circulant = jnp.zeros((nz, nz), jnp.float32)
    for offset in range(1, REACH + 1):
        circulant = jnp.where(apart == offset, -0.5 * COEFFS[offset], circulant)
    return split3(circulant)


PAD = TILE


def place(buf, k, x, tile, height, value):
    buf[k, x, pl.ds(PAD + tile * TILE, TILE), :] = value
    if tile == 0:
        buf[k, x, pl.ds(PAD + height, TILE), :] = value
    if tile == height // TILE - 1:
        buf[k, x, pl.ds(0, TILE), :] = value


def along_z(field, w1_ref, w2_ref):
    nz = field.shape[1]
    high, mid, low = split3(field)
    part = jnp.dot(jnp.concatenate([high, mid], 1), w1_ref[...], preferred_element_type=jnp.float32)
    rest = jnp.dot(jnp.concatenate([low, high], 1), w2_ref[...], preferred_element_type=jnp.float32)
    return part[:, :nz] + part[:, nz:] + rest


def add_xy(src, k, x, tile, total):
    width = src.shape[1]
    at = PAD + tile * TILE
    for j in range(1, REACH + 1):
        near = src[k, (x + j) % width, pl.ds(at, TILE), :] + src[k, (x - j) % width, pl.ds(at, TILE), :]
        near = near + src[k, x, pl.ds(at + j, TILE), :] + src[k, x, pl.ds(at - j, TILE), :]
        total = total + (-0.5 * COEFFS[j]) * near
    return total


def laplace_kernel(dims, in_ref, field_ref, lap_ref, w1_ref, w2_ref):
    gx, gy, own, nx, ny, nz, pieces, skip = dims
    width, height, cells = gx * nx, gy * ny, nx * ny
    high, mid, low = z_weights(nz)
    for at in (0, nz):
        w1_ref[pl.ds(at, nz), pl.ds(0, nz)] = high
        w1_ref[pl.ds(at, nz), pl.ds(nz, nz)] = mid
    w2_ref[pl.ds(0, nz), :] = high
    w2_ref[pl.ds(nz, nz), :] = low
    for g in range(gx * gy):
        at_x, at_y = (g // gy) * nx, (g % gy) * ny
        for k in range(own):
            for i in range(nx):
                for t in range(ny // TILE):
                    value = in_ref[g, pl.ds(k * cells + i * ny + t * TILE, TILE), :]
                    place(field_ref, k, at_x + i, at_y // TILE + t, height, value)
    field = field_ref[:, :, pl.ds(PAD, height), :].reshape(own * width * height, nz)
    lap_ref[...] = along_z(field, w1_ref, w2_ref).reshape(own, width, height, nz)
    for k in range(own):
        for x in range(width):
            for tile in range(height // TILE):
                rows = pl.ds(tile * TILE, TILE)
                lap_ref[k, x, rows, :] = add_xy(field_ref, k, x, tile, lap_ref[k, x, rows, :])


def filter_kernel(dims, field_ref, lap_ref, half_ref, other_ref, w1_ref, w2_ref, out_ref, pot, buf_a, buf_b, zbuf):
    gx, gy, own, nx, ny, nz, pieces, skip = dims
    width, height, cells = gx * nx, gy * ny, nx * ny
    half = cells // 2
    rows = cells // pieces
    middle, first, others = filter_weights(DEGREE)
    shift = -middle - 1.5 * COEFFS[0]

    core = lax.axis_index("core")
    for g in range(gx * gy):
        mine = pl.ds(pl.multiple_of(core * half, TILE), half)
        theirs = pl.ds(pl.multiple_of((1 - core) * half, TILE), half)
        pot[g, mine, :] = half_ref[g, pl.ds(skip, half), :] + shift
        pot[g, theirs, :] = other_ref[g] + shift

    chain = (field_ref, buf_a, buf_b, buf_a)
    steps = [(first, None)] + others
    for step, (scale, back) in enumerate(steps):
        src, dst, old = chain[step], buf_b if step % 2 else buf_a, chain[step - 1]
        last = step == len(steps) - 1
        if step:
            field = src[:, :, pl.ds(PAD, height), :].reshape(own * width * height, nz)
            zbuf[...] = along_z(field, w1_ref, w2_ref).reshape(own, width, height, nz)
        squares = [jnp.zeros((TILE, nz), jnp.float32) for _ in range(own)]
        for k in range(own):
            for x in range(width):
                for tile in range(height // TILE):
                    g = (x // nx) * gy + tile * TILE // ny
                    in_pencil = (x % nx) * ny + (tile * TILE) % ny
                    inner = pl.ds(PAD + tile * TILE, TILE)
                    plain = pl.ds(tile * TILE, TILE)
                    if step:
                        total = add_xy(src, k, x, tile, zbuf[k, x, plain, :])
                    else:
                        total = lap_ref[k, x, plain, :]
                    total = total + pot[g, pl.ds(in_pencil, TILE), :] * src[k, x, inner, :]
                    value = scale * total
                    if step:
                        value = value - back * old[k, x, inner, :]
                    if not last:
                        place(dst, k, x, tile, height, value)
                        continue
                    squares[k] = squares[k] + value * value
                    for r in range(0, TILE, TILE // 2):
                        piece, row = divmod(in_pencil + r, rows)
                        to = piece_owner(piece, pieces) * gx * gy + g
                        out_ref[to, pl.ds(k * rows + row, TILE // 2), :] = value[r : r + TILE // 2]
    line = lax.broadcasted_iota(jnp.int32, out_ref.shape[1:], 0)
    factor = jnp.zeros(out_ref.shape[1:], jnp.float32)
    for k in range(own):
        mean = jnp.sum(squares[k], keepdims=True) * (1.0 / (width * height * nz))
        factor = jnp.where(line // rows == k, lax.rsqrt(mean), factor)
    for to in range(out_ref.shape[0]):
        out_ref[to] = out_ref[to] * factor


def piece_owner(piece, pieces):
    chips = pieces // 2
    return (piece % chips) * 2 + piece // chips


def first_laplace(packed, dims):
    gx, gy, bands, nx, ny, nz, pieces, skip = dims
    width, height = gx * nx, gy * ny
    vmem = pl.BlockSpec(memory_space=pltpu.VMEM)
    cells = bands * width * height * nz
    return pl.pallas_call(
        functools.partial(laplace_kernel, dims),
        out_shape=(
            jax.ShapeDtypeStruct((bands, width, height + 2 * PAD, nz), jnp.float32),
            jax.ShapeDtypeStruct((bands, width, height, nz), jnp.float32),
            jax.ShapeDtypeStruct((2 * nz, 2 * nz), jnp.bfloat16),
            jax.ShapeDtypeStruct((2 * nz, nz), jnp.bfloat16),
        ),
        in_specs=[vmem],
        out_specs=(vmem,) * 4,
        compiler_params=pltpu.CompilerParams(vmem_limit_bytes=12 * 1024 * 1024),
        cost_estimate=pl.CostEstimate(flops=44 * cells, bytes_accessed=16 * cells, transcendentals=0),
        name="laplace",
    )(packed)


def apply_filter(field, laplace, packed, other, weights, dims):
    gx, gy, bands, nx, ny, nz, pieces, skip = dims
    vmem = pl.BlockSpec(memory_space=pltpu.VMEM)
    return pl.pallas_call(
        functools.partial(filter_kernel, dims),
        out_shape=jax.ShapeDtypeStruct((pieces * gx * gy, bands * nx * ny // pieces, nz), jnp.float32),
        in_specs=[vmem] * 6,
        out_specs=vmem,
        scratch_shapes=[
            pltpu.VMEM((gx * gy, nx * ny, nz), jnp.float32),
            pltpu.VMEM(field.shape, jnp.float32),
            pltpu.VMEM(field.shape, jnp.float32),
            pltpu.VMEM(laplace.shape, jnp.float32),
        ],
        compiler_params=pltpu.CompilerParams(vmem_limit_bytes=12 * 1024 * 1024),
        name="filter",
    )(field, laplace, packed, other, *weights)


def margin_kernel(rows, bands, scale, grid, x_ref, out_ref):
    highs, mids, lows = [], [], []
    for r in range(rows):
        high, mid, low = split3(x_ref[pl.ds(r, bands, stride=rows), :])
        highs.append(high)
        mids.append(mid)
        lows.append(low)
    terms = [jnp.concatenate(term, 1) for term in (highs, mids, lows)]
    stacked = jnp.concatenate(terms, 0)
    products = lax.dot_general(stacked, stacked, (((1,), (1,)), ((), ())), preferred_element_type=jnp.float32)

    def block(i, j):
        return products[i * bands : (i + 1) * bands, j * bands : (j + 1) * bands]

    small = block(0, 2) + block(2, 0) + block(1, 1)
    total = (small + (block(0, 1) + block(1, 0)) + block(0, 0)) * scale
    half = bands // 2
    row = lax.broadcasted_iota(jnp.int32, (half, half), 0)
    col = lax.broadcasted_iota(jnp.int32, (half, half), 1)
    strict = jnp.where(row > col, total[:half, :half], total[half:, half:])
    for core, part in enumerate((total[half:, :half], strict)):
        folded = jnp.concatenate([part[at : at + TILE] for at in range(0, half, TILE)], 1)
        for to in range(out_ref.shape[0]):
            if to // grid % 2 == core:
                out_ref[to] = folded


def partial_margin(blocks, bands, scale, pieces, grid):
    rows = blocks.shape[0] // bands
    return pl.pallas_call(
        functools.partial(margin_kernel, rows, bands, scale, grid),
        out_shape=jax.ShapeDtypeStruct((pieces * grid, TILE, (bands // 2) ** 2 // TILE), jnp.float32),
        in_specs=[pl.BlockSpec(memory_space=pltpu.VMEM)],
        out_specs=pl.BlockSpec(memory_space=pltpu.VMEM),
        compiler_params=pltpu.CompilerParams(vmem_limit_bytes=8 * 1024 * 1024),
        name="margin",
    )(blocks)


def sum_kernel(in_ref, out_ref):
    total = in_ref[0]
    for term in range(1, in_ref.shape[0]):
        total = total + in_ref[term]
    out_ref[...] = total


def sum_first(value):
    return pl.pallas_call(
        sum_kernel,
        out_shape=jax.ShapeDtypeStruct(value.shape[1:], value.dtype),
        in_specs=[pl.BlockSpec(memory_space=pltpu.VMEM)],
        out_specs=pl.BlockSpec(memory_space=pltpu.VMEM),
        compiler_params=pltpu.CompilerParams(vmem_limit_bytes=4 * 1024 * 1024),
        name="sum",
    )(value)


def eliminate(margin):
    bands = margin.shape[0]
    tiles = bands // TILE
    margin = jnp.concatenate([margin, margin], 1)
    width = 2 * bands
    lines = lax.broadcasted_iota(jnp.int32, (TILE, width), 0)
    lanes = lax.broadcasted_iota(jnp.int32, (TILE, width), 1)
    both = []
    for t in range(tiles):
        right = margin[t * TILE : (t + 1) * TILE]
        eye = jnp.where(lines + t * TILE == lanes % bands, 1.0, 0.0)
        both.append([eye, jnp.where(lanes < bands, eye, right)])

    def spread(t, at):
        return jnp.broadcast_to(both[t][1][:, bands + at : bands + at + 1], (TILE, width))

    def line_of(value, at):
        return jnp.broadcast_to(value[at : at + 1, :], (TILE, width))

    heads = [spread(0, c) for c in range(TILE)]
    for p in range(tiles):
        here = range(p * TILE, (p + 1) * TILE)
        panel = [{t: spread(t, at) for t in range(p + 1, tiles)} for at in here]
        later = [spread(p + 1, at + TILE) for at in here] if p + 1 < tiles else []
        square = [[line_of(heads[c], d) if d >= c else None for d in range(TILE)] for c in range(TILE)]
        pivots = None
        for j in range(TILE):
            pivot = square[j][j]
            pivots = pivot if j == 0 else jnp.where(lines == j, pivot, pivots)
            ratio = pl.reciprocal(pivot, approx=True)
            for c in range(j + 1, TILE):
                for d in range(c, TILE):
                    square[c][d] = square[c][d] - (square[j][c] * square[j][d]) * ratio
            factor = {t: panel[j][t] * ratio for t in range(p + 1, tiles)}
            factor[p] = jnp.where(lines > j, heads[j] * ratio, 0.0)
            for c in range(j + 1, TILE):
                heads[c] = heads[c] - factor[p] * square[j][c]
                for t in range(p + 1, tiles):
                    panel[c][t] = panel[c][t] - factor[t] * square[j][c]
            for c, column in enumerate(later):
                later[c] = column - factor[p + 1] * line_of(panel[j][p + 1], c)
            pair = [line_of(value, j) for value in both[p]]
            for t in range(p, tiles):
                both[t] = [value - factor[t] * line for value, line in zip(both[t], pair)]
        heads = later
        scale = lax.rsqrt(pivots)
        both[p] = [value * scale for value in both[p]]
    return [jnp.concatenate(value, 1) for value in both]


def split_pair(split_ref, at, part, pair, bands):
    rows = part.shape[0] // bands
    nz = part.shape[1]
    for i in range(2):
        terms = split3(part[pl.ds(2 * pair + i, bands, stride=rows), :])
        for j, term in enumerate(terms):
            split_ref[at, pl.ds(j * bands, bands), pl.ds(i * nz, nz)] = term


def inverse_kernel(dims, *refs):
    bands, own = dims
    own_ref, other_ref, left_ref, inv_ref = refs
    half = bands // 2
    here, there = own_ref[...], other_ref[...]
    first = lax.axis_index("core") == 0
    cross, strict = [
        jnp.concatenate([value[:, at : at + half] for at in range(0, half * half // TILE, half)], 0)
        for value in (jnp.where(first, here, there), jnp.where(first, there, here))
    ]
    row = lax.broadcasted_iota(jnp.int32, (half, half), 0)
    col = lax.broadcasted_iota(jnp.int32, (half, half), 1)
    turned = strict.T
    low = jnp.where(row == col, 1.0, jnp.where(row > col, strict, turned))
    high = jnp.where(row == col, 1.0, jnp.where(row < col, strict, turned))
    margin = jnp.concatenate(
        [jnp.concatenate([low, cross.T], 1), jnp.concatenate([cross, high], 1)], 0
    )
    for t, value in enumerate(eliminate(margin)):
        inv_ref[pl.ds(t * TILE, TILE), :] = value
    first = pl.multiple_of((lax.axis_index("chip") * 2 + lax.axis_index("core")) * own, TILE)
    rows = inv_ref[pl.ds(first, own), pl.ds(0, 3 * bands)]
    lanes = lax.broadcasted_iota(jnp.int32, rows.shape, 1)
    high = rows.astype(jnp.bfloat16)
    rest = rows - high.astype(jnp.float32)
    mid = rest.astype(jnp.bfloat16)
    low = rest - mid.astype(jnp.float32)
    left_ref[pl.ds(0, own), :] = high
    left_ref[pl.ds(own, own), :] = jnp.where(lanes < 2 * bands, rest, 0.0).astype(jnp.bfloat16)
    left_ref[pl.ds(2 * own, own), :] = jnp.where(lanes < bands, low, 0.0).astype(jnp.bfloat16)


def inverse_rows(margins, own, bands):
    vmem = pl.BlockSpec(memory_space=pltpu.VMEM)
    return pl.pallas_call(
        functools.partial(inverse_kernel, (bands, own)),
        out_shape=jax.ShapeDtypeStruct((3 * own, 3 * bands), jnp.bfloat16),
        in_specs=[vmem] * len(margins),
        out_specs=vmem,
        scratch_shapes=[pltpu.VMEM((bands, 4 * bands), jnp.float32)],
        compiler_params=pltpu.CompilerParams(vmem_limit_bytes=4 * 1024 * 1024),
        name="inverse",
    )(*margins)


def rotate_kernel(dims, left_ref, *refs):
    bands, own = dims
    parts, out_ref = refs[:-1], refs[-1]
    rows = parts[0].shape[0] // bands
    nz = parts[0].shape[1]
    left = left_ref[...]
    chips = len(parts) // 2
    chip, core = lax.axis_index("chip"), lax.axis_index("core")
    for index, part in enumerate(parts):
        piece = (core ^ (index // chips)) * chips + (chip ^ (index % chips))
        for r in range(0, rows, 2):
            terms = [split3(part[pl.ds(r + i, bands, stride=rows), :]) for i in range(2)]
            block = jnp.concatenate([jnp.concatenate(term, 1) for term in zip(*terms)], 0)
            product = jnp.dot(left, block, preferred_element_type=jnp.float32)
            value = product[:own] + (product[own : 2 * own] + product[2 * own :])
            for i in range(2):
                start = piece * rows + r + i
                out_ref[pl.ds(start, own, stride=rows * len(parts)), :] = value[:, i * nz : (i + 1) * nz]


def rotate(left, parts, bands):
    rows = parts[0].shape[0] // bands
    own = left.shape[0] // 3
    nz = parts[0].shape[1]
    vmem = pl.BlockSpec(memory_space=pltpu.VMEM)
    return pl.pallas_call(
        functools.partial(rotate_kernel, (bands, own)),
        out_shape=jax.ShapeDtypeStruct((own * rows * len(parts), nz), jnp.float32),
        in_specs=[vmem] * (1 + len(parts)),
        out_specs=vmem,
        compiler_params=pltpu.CompilerParams(vmem_limit_bytes=6 * 1024 * 1024),
        name="rotate",
    )(left, *parts)


def on_device_fields(start_bands, potential):
    own_bands, nx, ny, nz = start_bands.shape
    gx, gy, chips = lax.axis_size("gx"), lax.axis_size("gy"), lax.axis_size("chip")
    pieces = 2 * chips
    grid = gx * gy
    own = own_bands // grid
    cells = nx * ny
    bands = own_bands * pieces
    rows = cells // pieces
    core = lax.axis_index("core")
    swap = [(0, 1), (1, 0)]

    fields = start_bands.reshape(grid, own * cells, nz)
    flat_potential = potential.reshape(cells, nz)
    half = cells // 2
    own_half = lax.dynamic_slice_in_dim(flat_potential, core * half, half, 0)
    packed = jnp.concatenate([fields, jnp.broadcast_to(own_half[None], (grid, half, nz))], 1)
    packed = lax.all_to_all(packed, ("gx", "gy"), 0, 0)
    other = lax.ppermute(packed[:, own * cells :, :], "core", swap)
    dims = (gx, gy, own, nx, ny, nz, pieces, own * cells)
    field, laplace, *weights = first_laplace(packed, dims)
    filtered = apply_filter(field, laplace, packed, other, weights, dims)
    blocks = lax.all_to_all(filtered, ("chip", "core", "gx", "gy"), 0, 0).reshape(bands * rows, nz)

    def tied(value, first):
        return lax.optimization_barrier((value, first))[0]

    def copies(value, *axes):
        count = math.prod(lax.axis_size(axis) for axis in axes)
        pairs = [[(i, i ^ mask) for i in range(count)] for mask in range(1, count)]
        return [value] + [lax.ppermute(value, axes, pair) for pair in pairs]

    spread = partial_margin(blocks, bands, 1.0 / (cells * nz * grid), pieces, grid)
    parts = copies(blocks, "chip")
    crossed = [lax.ppermute(blocks, "core", swap)]
    crossed, spread = lax.optimization_barrier((crossed, spread))
    margins = lax.all_to_all(spread, ("chip", "core", "gx", "gy"), 0, 0)
    margins = copies(sum_first(margins), "core")
    far, margins = lax.optimization_barrier((parts[1:], margins))
    parts += crossed + [lax.ppermute(part, "core", swap) for part in far]
    left = inverse_rows(margins, own_bands, bands)
    rotated = rotate(left, parts, bands)
    return rotated.reshape(start_bands.shape)


def power_of_two(count):
    return count & (count - 1) == 0


def whole_fields(mesh, shape):
    gx, gy, pieces = mesh.shape["gx"], mesh.shape["gy"], mesh.shape["band"]
    bands, nx, ny, nz = shape[0], shape[1] // gx, shape[2] // gy, shape[3]
    own_bands, cells = bands // pieces, nx * ny
    return (
        own_bands % (gx * gy) == 0
        and own_bands % (2 * TILE) == 0
        and pieces % 2 == 0
        and power_of_two(pieces)
        and ny % TILE == 0
        and nz % 128 == 0
        and bands % 64 == 0
        and cells % (2 * TILE) == 0
        and cells % (pieces * TILE // 2) == 0
        and pieces > 2
        and (own_bands // (gx * gy)) * (cells // pieces) % TILE == 0
        and shape[1] > 2 * REACH
    )


def solution(mesh):
    def step(start_bands, potential):
        if whole_fields(mesh, start_bands.shape):
            chips = mesh.shape["band"] // 2
            rest = mesh.devices.shape[1:]
            split = Mesh(mesh.devices.reshape((chips, 2) + rest), ("chip", "core") + mesh.axis_names[1:])
            program, band = on_device_fields, ("chip", "core")
        else:
            split, program, band = mesh, on_device_halo, "band"
        return jax.shard_map(
            program,
            mesh=split,
            in_specs=(P(band, "gx", "gy", None), P("gx", "gy", None)),
            out_specs=P(band, "gx", "gy", None),
            check_vma=False,
        )(start_bands, potential)

    return step
```

```python
import functools
import math

import jax
import jax.numpy as jnp
from jax import lax
from jax.experimental import pallas as pl
from jax.experimental.pallas import tpu as pltpu
from jax.sharding import Mesh, PartitionSpec as P

DEGREE = 4


COEFFS = (
    -5369.0 / 1800.0,
    12.0 / 7.0,
    -15.0 / 56.0,
    10.0 / 189.0,
    -1.0 / 112.0,
    2.0 / 1925.0,
    -1.0 / 16632.0,
)
REACH = len(COEFFS) - 1
LOWER_END = -0.5
CUT_LOW = 3.0
CUT_HIGH = 12.7
TILE = 8


def filter_weights(degree):
    half_width = (CUT_HIGH - CUT_LOW) / 2.0
    middle = (CUT_HIGH + CUT_LOW) / 2.0
    sigma = half_width / (LOWER_END - middle)
    tau = 2.0 / sigma
    first = sigma / half_width
    others = []
    for index in range(degree - 1):
        sigma_new = 1.0 / (tau - sigma)
        others.append((2.0 * sigma_new / half_width, sigma * sigma_new))
        sigma = sigma_new
    return (middle, first, others)


def padded_2(block, sides, width):
    for axis, dim in sides:
        count = lax.axis_size(axis)
        forward = [(i, i + 1) for i in range(count - 1)]
        forward.append((count - 1, 0))
        backward = [(target, source) for source, target in forward]
        low = lax.ppermute(
            lax.slice_in_dim(block, block.shape[dim] - width, None, axis=dim), axis, forward
        )
        high = lax.ppermute(lax.slice_in_dim(block, 0, width, axis=dim), axis, backward)
        block = jnp.concatenate([low, block, high], axis=dim)
    return block


def hamiltonian(field, potential):
    width_x = field.shape[1]
    width_y = field.shape[2]
    padded = padded_2(field, (("gx", 1), ("gy", 2)), REACH)
    laplace = 3.0 * COEFFS[0] * field
    for offset in range(1, REACH + 1):
        ahead_x = padded[:, REACH + offset : REACH + offset + width_x, REACH : REACH + width_y]
        behind_x = padded[:, REACH - offset : REACH - offset + width_x, REACH : REACH + width_y]
        ahead_y = padded[:, REACH : REACH + width_x, REACH + offset : REACH + offset + width_y]
        behind_y = padded[:, REACH : REACH + width_x, REACH - offset : REACH - offset + width_y]
        neighbours = ahead_x + behind_x
        neighbours = neighbours + ahead_y + behind_y
        neighbours = neighbours + jnp.roll(field, -offset, 3) + jnp.roll(field, offset, 3)
        laplace = laplace + COEFFS[offset] * neighbours
    return -0.5 * laplace + potential * field


def chebyshev(field, potential):
    middle, first, others = filter_weights(DEGREE)
    current = (hamiltonian(field, potential) - middle * field) * first
    previous = field
    for scale_now, scale_back in others:
        following = (
            hamiltonian(current, potential) - middle * current
        ) * scale_now - scale_back * previous
        previous = current
        current = following
    return current


def invert_factor(margin, identity):
    lower_factor = jnp.linalg.cholesky(margin)
    return jax.scipy.linalg.solve_triangular(lower_factor, identity, lower=True)


def on_device_halo(start_bands, potential):
    filtered = chebyshev(start_bands, potential)
    own_bands = filtered.shape[0]
    flattened = filtered.reshape(own_bands, -1)
    total_cells = flattened.shape[1] * lax.axis_size("gx") * lax.axis_size("gy")
    all_bands = own_bands * lax.axis_size("band")
    identity = jnp.eye(all_bands, dtype=jnp.float32)
    products = jnp.dot(
        flattened,
        lax.all_gather(flattened, "band", axis=0, tiled=True).T,
        precision=lax.Precision.HIGHEST,
        preferred_element_type=jnp.float32,
    )
    first_row = lax.axis_index("band") * own_bands
    summed = lax.psum(products, ("gx", "gy"))
    margin = lax.all_gather(summed, "band", axis=0, tiled=True) * (1.0 / total_cells)
    inverse = invert_factor(margin, identity)
    own_rows = lax.dynamic_slice_in_dim(inverse, first_row, own_bands, 0)
    rotated = jnp.dot(
        own_rows,
        lax.all_gather(flattened, "band", axis=0, tiled=True),
        precision=lax.Precision.HIGHEST,
        preferred_element_type=jnp.float32,
    )
    return rotated.reshape(filtered.shape)


def split3(value):
    high = value.astype(jnp.bfloat16)
    rest = value - high.astype(jnp.float32)
    mid = rest.astype(jnp.bfloat16)
    low = (rest - mid.astype(jnp.float32)).astype(jnp.bfloat16)
    return high, mid, low


def z_weights(nz):
    row = lax.broadcasted_iota(jnp.int32, (nz, nz), 0)
    col = lax.broadcasted_iota(jnp.int32, (nz, nz), 1)
    apart = jnp.abs(row - col)
    apart = jnp.minimum(apart, nz - apart)
    circulant = jnp.zeros((nz, nz), jnp.float32)
    for offset in range(1, REACH + 1):
        circulant = jnp.where(apart == offset, -0.5 * COEFFS[offset], circulant)
    return split3(circulant)


def place(buf, k, x, tile, height, value):
    buf[k, x, pl.ds(tile * TILE, TILE), :] = value
    if tile == 0:
        buf[k, x, pl.ds(height, TILE), :] = value


def along_z(field, w1_ref, w2_ref):
    nz = field.shape[1]
    high, mid, low = split3(field)
    part = jnp.dot(jnp.concatenate([high, mid], 1), w1_ref[...], preferred_element_type=jnp.float32)
    rest = jnp.dot(jnp.concatenate([low, high], 1), w2_ref[...], preferred_element_type=jnp.float32)
    return part[:, :nz] + part[:, nz:] + rest


def along_xy(src, k, height, wanted):
    width = src.shape[1]
    tiles = range(height // TILE)
    window = {}

    def plane(x, t):
        if (x, t) not in window:
            window[x, t] = src[k, x % width, pl.ds(t * TILE, TILE), :]
        return window[x, t]

    for x in range(width):
        rows, pairs = {}, {}

        def shifted(at):
            if at not in rows:
                rows[at] = src[k, x, pl.ds(at, TILE), :]
            return rows[at]

        def pair(*ends):
            ends = tuple(sorted(at % height for at in ends))
            if ends not in pairs:
                pairs[ends] = shifted(ends[0]) + shifted(ends[1])
            return pairs[ends]

        totals = []
        for t in tiles if wanted else ():
            total = None
            for j in range(1, REACH + 1):
                near = plane(x + j, t) + plane(x - j, t)
                near = near + pair(t * TILE + j, t * TILE - j)
                near = (-0.5 * COEFFS[j]) * near
                total = near if total is None else total + near
            totals.append(total)
        yield x, [plane(x, t) for t in tiles], totals


def laplace_kernel(dims, in_ref, field_ref, lap_ref, w1_ref, w2_ref):
    gx, gy, own, nx, ny, nz, pieces, skip = dims
    width, height, cells = gx * nx, gy * ny, nx * ny
    high, mid, low = z_weights(nz)
    for at in (0, nz):
        w1_ref[pl.ds(at, nz), pl.ds(0, nz)] = high
        w1_ref[pl.ds(at, nz), pl.ds(nz, nz)] = mid
    w2_ref[pl.ds(0, nz), :] = high
    w2_ref[pl.ds(nz, nz), :] = low
    for g in range(gx * gy):
        at_x, at_y = (g // gy) * nx, (g % gy) * ny
        for k in range(own):
            for i in range(nx):
                for t in range(ny // TILE):
                    value = in_ref[g, pl.ds(k * cells + i * ny + t * TILE, TILE), :]
                    place(field_ref, k, at_x + i, at_y // TILE + t, height, value)
    field = field_ref[:, :, pl.ds(0, height), :].reshape(own * width * height, nz)
    lap_ref[...] = along_z(field, w1_ref, w2_ref).reshape(own, width, height, nz)
    for k in range(own):
        for x, _, totals in along_xy(field_ref, k, height, True):
            for tile, total in enumerate(totals):
                rows = pl.ds(tile * TILE, TILE)
                lap_ref[k, x, rows, :] = lap_ref[k, x, rows, :] + total


def filter_kernel(dims, field_ref, lap_ref, half_ref, other_ref, w1_ref, w2_ref, out_ref, pot, buf_a, buf_b, zbuf):
    gx, gy, own, nx, ny, nz, pieces, skip = dims
    width, height, cells = gx * nx, gy * ny, nx * ny
    half = cells // 2
    rows = cells // pieces
    middle, first, others = filter_weights(DEGREE)
    shift = -middle - 1.5 * COEFFS[0]

    core = lax.axis_index("core")
    for g in range(gx * gy):
        mine = pl.ds(pl.multiple_of(core * half, TILE), half)
        theirs = pl.ds(pl.multiple_of((1 - core) * half, TILE), half)
        pot[g, mine, :] = half_ref[g, pl.ds(skip, half), :] + shift
        pot[g, theirs, :] = other_ref[g] + shift

    chain = (field_ref, buf_a, buf_b, buf_a)
    steps = [(first, None)] + others
    for step, (scale, back) in enumerate(steps):
        src, dst, old = chain[step], buf_b if step % 2 else buf_a, chain[step - 1]
        last = step == len(steps) - 1
        if step:
            field = src[:, :, pl.ds(0, height), :].reshape(own * width * height, nz)
            zbuf[...] = along_z(field, w1_ref, w2_ref).reshape(own, width, height, nz)
        squares = [jnp.zeros((TILE, nz), jnp.float32) for _ in range(own)]
        for k in range(own):
            for x, centres, totals in along_xy(src, k, height, bool(step)):
                for tile in range(height // TILE):
                    g = (x // nx) * gy + tile * TILE // ny
                    in_pencil = (x % nx) * ny + (tile * TILE) % ny
                    plain = pl.ds(tile * TILE, TILE)
                    if step:
                        total = zbuf[k, x, plain, :] + totals[tile]
                    else:
                        total = lap_ref[k, x, plain, :]
                    total = total + pot[g, pl.ds(in_pencil, TILE), :] * centres[tile]
                    value = scale * total
                    if step:
                        value = value - back * old[k, x, plain, :]
                    if not last:
                        place(dst, k, x, tile, height, value)
                        continue
                    squares[k] = squares[k] + value * value
                    for r in range(0, TILE, TILE // 2):
                        piece, row = divmod(in_pencil + r, rows)
                        to = piece_owner(piece, pieces) * gx * gy + g
                        out_ref[to, pl.ds(k * rows + row, TILE // 2), :] = value[r : r + TILE // 2]
    line = lax.broadcasted_iota(jnp.int32, out_ref.shape[1:], 0)
    factor = jnp.zeros(out_ref.shape[1:], jnp.float32)
    for k in range(own):
        mean = jnp.sum(squares[k], keepdims=True) * (1.0 / (width * height * nz))
        factor = jnp.where(line // rows == k, lax.rsqrt(mean), factor)
    for to in range(out_ref.shape[0]):
        out_ref[to] = out_ref[to] * factor


def piece_owner(piece, pieces):
    chips = pieces // 2
    return (piece % chips) * 2 + piece // chips


def first_laplace(packed, dims):
    gx, gy, bands, nx, ny, nz, pieces, skip = dims
    width, height = gx * nx, gy * ny
    vmem = pl.BlockSpec(memory_space=pltpu.VMEM)
    cells = bands * width * height * nz
    return pl.pallas_call(
        functools.partial(laplace_kernel, dims),
        out_shape=(
            jax.ShapeDtypeStruct((bands, width, height + TILE, nz), jnp.float32),
            jax.ShapeDtypeStruct((bands, width, height, nz), jnp.float32),
            jax.ShapeDtypeStruct((2 * nz, 2 * nz), jnp.bfloat16),
            jax.ShapeDtypeStruct((2 * nz, nz), jnp.bfloat16),
        ),
        in_specs=[vmem],
        out_specs=(vmem,) * 4,
        compiler_params=pltpu.CompilerParams(vmem_limit_bytes=12 * 1024 * 1024),
        cost_estimate=pl.CostEstimate(flops=44 * cells, bytes_accessed=16 * cells, transcendentals=0),
        name="laplace",
    )(packed)


def apply_filter(field, laplace, packed, other, weights, dims):
    gx, gy, bands, nx, ny, nz, pieces, skip = dims
    vmem = pl.BlockSpec(memory_space=pltpu.VMEM)
    return pl.pallas_call(
        functools.partial(filter_kernel, dims),
        out_shape=jax.ShapeDtypeStruct((pieces * gx * gy, bands * nx * ny // pieces, nz), jnp.float32),
        in_specs=[vmem] * 6,
        out_specs=vmem,
        scratch_shapes=[
            pltpu.VMEM((gx * gy, nx * ny, nz), jnp.float32),
            pltpu.VMEM(field.shape, jnp.float32),
            pltpu.VMEM(field.shape, jnp.float32),
            pltpu.VMEM(laplace.shape, jnp.float32),
        ],
        compiler_params=pltpu.CompilerParams(vmem_limit_bytes=12 * 1024 * 1024),
        name="filter",
    )(field, laplace, packed, other, *weights)


def margin_kernel(rows, bands, scale, grid, x_ref, out_ref):
    highs, mids, lows = [], [], []
    for r in range(rows):
        high, mid, low = split3(x_ref[pl.ds(r, bands, stride=rows), :])
        highs.append(high)
        mids.append(mid)
        lows.append(low)
    terms = [jnp.concatenate(term, 1) for term in (highs, mids, lows)]
    stacked = jnp.concatenate(terms, 0)
    products = lax.dot_general(stacked, stacked, (((1,), (1,)), ((), ())), preferred_element_type=jnp.float32)

    def block(i, j):
        return products[i * bands : (i + 1) * bands, j * bands : (j + 1) * bands]

    small = block(0, 2) + block(2, 0) + block(1, 1)
    total = (small + (block(0, 1) + block(1, 0)) + block(0, 0)) * scale
    half = bands // 2
    row = lax.broadcasted_iota(jnp.int32, (half, half), 0)
    col = lax.broadcasted_iota(jnp.int32, (half, half), 1)
    strict = jnp.where(row > col, total[:half, :half], total[half:, half:])
    for core, part in enumerate((total[half:, :half], strict)):
        folded = jnp.concatenate([part[at : at + TILE] for at in range(0, half, TILE)], 1)
        for to in range(out_ref.shape[0]):
            if to // grid % 2 == core:
                out_ref[to] = folded


def partial_margin(blocks, bands, scale, pieces, grid):
    rows = blocks.shape[0] // bands
    return pl.pallas_call(
        functools.partial(margin_kernel, rows, bands, scale, grid),
        out_shape=jax.ShapeDtypeStruct((pieces * grid, TILE, (bands // 2) ** 2 // TILE), jnp.float32),
        in_specs=[pl.BlockSpec(memory_space=pltpu.VMEM)],
        out_specs=pl.BlockSpec(memory_space=pltpu.VMEM),
        compiler_params=pltpu.CompilerParams(vmem_limit_bytes=8 * 1024 * 1024),
        name="margin",
    )(blocks)


def sum_kernel(in_ref, out_ref):
    total = in_ref[0]
    for term in range(1, in_ref.shape[0]):
        total = total + in_ref[term]
    out_ref[...] = total


def sum_first(value):
    return pl.pallas_call(
        sum_kernel,
        out_shape=jax.ShapeDtypeStruct(value.shape[1:], value.dtype),
        in_specs=[pl.BlockSpec(memory_space=pltpu.VMEM)],
        out_specs=pl.BlockSpec(memory_space=pltpu.VMEM),
        compiler_params=pltpu.CompilerParams(vmem_limit_bytes=4 * 1024 * 1024),
        name="sum",
    )(value)


def eliminate(margin):
    bands = margin.shape[0]
    tiles = bands // TILE
    margin = jnp.concatenate([margin, margin], 1)
    width = 2 * bands
    lines = lax.broadcasted_iota(jnp.int32, (TILE, width), 0)
    lanes = lax.broadcasted_iota(jnp.int32, (TILE, width), 1)
    both = []
    for t in range(tiles):
        right = margin[t * TILE : (t + 1) * TILE]
        eye = jnp.where(lines + t * TILE == lanes % bands, 1.0, 0.0)
        both.append([eye, jnp.where(lanes < bands, eye, right)])

    def spread(t, at):
        return jnp.broadcast_to(both[t][1][:, bands + at : bands + at + 1], (TILE, width))

    def line_of(value, at):
        return jnp.broadcast_to(value[at : at + 1, :], (TILE, width))

    heads = [spread(0, c) for c in range(TILE)]
    for p in range(tiles):
        here = range(p * TILE, (p + 1) * TILE)
        panel = [{t: spread(t, at) for t in range(p + 1, tiles)} for at in here]
        later = [spread(p + 1, at + TILE) for at in here] if p + 1 < tiles else []
        square = [[line_of(heads[c], d) if d >= c else None for d in range(TILE)] for c in range(TILE)]
        pivots = None
        for j in range(TILE):
            pivot = square[j][j]
            pivots = pivot if j == 0 else jnp.where(lines == j, pivot, pivots)
            ratio = pl.reciprocal(pivot, approx=True)
            for c in range(j + 1, TILE):
                for d in range(c, TILE):
                    square[c][d] = square[c][d] - (square[j][c] * square[j][d]) * ratio
            factor = {t: panel[j][t] * ratio for t in range(p + 1, tiles)}
            factor[p] = jnp.where(lines > j, heads[j] * ratio, 0.0)
            for c in range(j + 1, TILE):
                heads[c] = heads[c] - factor[p] * square[j][c]
                for t in range(p + 1, tiles):
                    panel[c][t] = panel[c][t] - factor[t] * square[j][c]
            for c, column in enumerate(later):
                later[c] = column - factor[p + 1] * line_of(panel[j][p + 1], c)
            pair = [line_of(value, j) for value in both[p]]
            for t in range(p, tiles):
                both[t] = [value - factor[t] * line for value, line in zip(both[t], pair)]
        heads = later
        scale = lax.rsqrt(pivots)
        both[p] = [value * scale for value in both[p]]
    return [jnp.concatenate(value, 1) for value in both]


def split_pair(split_ref, at, part, pair, bands):
    rows = part.shape[0] // bands
    nz = part.shape[1]
    for i in range(2):
        terms = split3(part[pl.ds(2 * pair + i, bands, stride=rows), :])
        for j, term in enumerate(terms):
            split_ref[at, pl.ds(j * bands, bands), pl.ds(i * nz, nz)] = term


def inverse_kernel(dims, *refs):
    bands, own = dims
    own_ref, other_ref, left_ref, inv_ref = refs
    half = bands // 2
    here, there = own_ref[...], other_ref[...]
    first = lax.axis_index("core") == 0
    cross, strict = [
        jnp.concatenate([value[:, at : at + half] for at in range(0, half * half // TILE, half)], 0)
        for value in (jnp.where(first, here, there), jnp.where(first, there, here))
    ]
    row = lax.broadcasted_iota(jnp.int32, (half, half), 0)
    col = lax.broadcasted_iota(jnp.int32, (half, half), 1)
    turned = strict.T
    low = jnp.where(row == col, 1.0, jnp.where(row > col, strict, turned))
    high = jnp.where(row == col, 1.0, jnp.where(row < col, strict, turned))
    margin = jnp.concatenate(
        [jnp.concatenate([low, cross.T], 1), jnp.concatenate([cross, high], 1)], 0
    )
    for t, value in enumerate(eliminate(margin)):
        inv_ref[pl.ds(t * TILE, TILE), :] = value
    first = pl.multiple_of((lax.axis_index("chip") * 2 + lax.axis_index("core")) * own, TILE)
    rows = inv_ref[pl.ds(first, own), pl.ds(0, 3 * bands)]
    lanes = lax.broadcasted_iota(jnp.int32, rows.shape, 1)
    high = rows.astype(jnp.bfloat16)
    rest = rows - high.astype(jnp.float32)
    mid = rest.astype(jnp.bfloat16)
    low = rest - mid.astype(jnp.float32)
    left_ref[pl.ds(0, own), :] = high
    left_ref[pl.ds(own, own), :] = jnp.where(lanes < 2 * bands, rest, 0.0).astype(jnp.bfloat16)
    left_ref[pl.ds(2 * own, own), :] = jnp.where(lanes < bands, low, 0.0).astype(jnp.bfloat16)


def inverse_rows(margins, own, bands):
    vmem = pl.BlockSpec(memory_space=pltpu.VMEM)
    return pl.pallas_call(
        functools.partial(inverse_kernel, (bands, own)),
        out_shape=jax.ShapeDtypeStruct((3 * own, 3 * bands), jnp.bfloat16),
        in_specs=[vmem] * len(margins),
        out_specs=vmem,
        scratch_shapes=[pltpu.VMEM((bands, 4 * bands), jnp.float32)],
        compiler_params=pltpu.CompilerParams(vmem_limit_bytes=4 * 1024 * 1024),
        name="inverse",
    )(*margins)


def rotate_kernel(dims, left_ref, *refs):
    bands, own = dims
    parts, out_ref = refs[:-1], refs[-1]
    rows = parts[0].shape[0] // bands
    nz = parts[0].shape[1]
    left = left_ref[...]
    chips = len(parts) // 2
    chip, core = lax.axis_index("chip"), lax.axis_index("core")
    for index, part in enumerate(parts):
        piece = (core ^ (index // chips)) * chips + (chip ^ (index % chips))
        for r in range(0, rows, 2):
            terms = [split3(part[pl.ds(r + i, bands, stride=rows), :]) for i in range(2)]
            block = jnp.concatenate([jnp.concatenate(term, 1) for term in zip(*terms)], 0)
            product = jnp.dot(left, block, preferred_element_type=jnp.float32)
            value = product[:own] + (product[own : 2 * own] + product[2 * own :])
            for i in range(2):
                start = piece * rows + r + i
                out_ref[pl.ds(start, own, stride=rows * len(parts)), :] = value[:, i * nz : (i + 1) * nz]


def rotate(left, parts, bands):
    rows = parts[0].shape[0] // bands
    own = left.shape[0] // 3
    nz = parts[0].shape[1]
    vmem = pl.BlockSpec(memory_space=pltpu.VMEM)
    return pl.pallas_call(
        functools.partial(rotate_kernel, (bands, own)),
        out_shape=jax.ShapeDtypeStruct((own * rows * len(parts), nz), jnp.float32),
        in_specs=[vmem] * (1 + len(parts)),
        out_specs=vmem,
        compiler_params=pltpu.CompilerParams(vmem_limit_bytes=6 * 1024 * 1024),
        name="rotate",
    )(left, *parts)


def on_device_fields(start_bands, potential):
    own_bands, nx, ny, nz = start_bands.shape
    gx, gy, chips = lax.axis_size("gx"), lax.axis_size("gy"), lax.axis_size("chip")
    pieces = 2 * chips
    grid = gx * gy
    own = own_bands // grid
    cells = nx * ny
    bands = own_bands * pieces
    rows = cells // pieces
    core = lax.axis_index("core")
    swap = [(0, 1), (1, 0)]

    fields = start_bands.reshape(grid, own * cells, nz)
    flat_potential = potential.reshape(cells, nz)
    half = cells // 2
    own_half = lax.dynamic_slice_in_dim(flat_potential, core * half, half, 0)
    packed = jnp.concatenate([fields, jnp.broadcast_to(own_half[None], (grid, half, nz))], 1)
    packed = lax.all_to_all(packed, ("gx", "gy"), 0, 0)
    other = lax.ppermute(packed[:, own * cells :, :], "core", swap)
    dims = (gx, gy, own, nx, ny, nz, pieces, own * cells)
    field, laplace, *weights = first_laplace(packed, dims)
    filtered = apply_filter(field, laplace, packed, other, weights, dims)
    blocks = lax.all_to_all(filtered, ("chip", "core", "gx", "gy"), 0, 0).reshape(bands * rows, nz)

    def tied(value, first):
        return lax.optimization_barrier((value, first))[0]

    def copies(value, *axes):
        count = math.prod(lax.axis_size(axis) for axis in axes)
        pairs = [[(i, i ^ mask) for i in range(count)] for mask in range(1, count)]
        return [value] + [lax.ppermute(value, axes, pair) for pair in pairs]

    spread = partial_margin(blocks, bands, 1.0 / (cells * nz * grid), pieces, grid)
    parts = copies(blocks, "chip")
    crossed = [lax.ppermute(blocks, "core", swap)]
    crossed, spread = lax.optimization_barrier((crossed, spread))
    margins = lax.all_to_all(spread, ("chip", "core", "gx", "gy"), 0, 0)
    margins = copies(sum_first(margins), "core")
    far, margins = lax.optimization_barrier((parts[1:], margins))
    parts += crossed + [lax.ppermute(part, "core", swap) for part in far]
    left = inverse_rows(margins, own_bands, bands)
    rotated = rotate(left, parts, bands)
    return rotated.reshape(start_bands.shape)


def power_of_two(count):
    return count & (count - 1) == 0


def whole_fields(mesh, shape):
    gx, gy, pieces = mesh.shape["gx"], mesh.shape["gy"], mesh.shape["band"]
    bands, nx, ny, nz = shape[0], shape[1] // gx, shape[2] // gy, shape[3]
    own_bands, cells = bands // pieces, nx * ny
    return (
        own_bands % (gx * gy) == 0
        and own_bands % (2 * TILE) == 0
        and pieces % 2 == 0
        and power_of_two(pieces)
        and ny % TILE == 0
        and nz % 128 == 0
        and bands % 64 == 0
        and cells % (2 * TILE) == 0
        and cells % (pieces * TILE // 2) == 0
        and pieces > 2
        and (own_bands // (gx * gy)) * (cells // pieces) % TILE == 0
        and shape[1] > 2 * REACH
    )


def solution(mesh):
    def step(start_bands, potential):
        if whole_fields(mesh, start_bands.shape):
            chips = mesh.shape["band"] // 2
            rest = mesh.devices.shape[1:]
            split = Mesh(mesh.devices.reshape((chips, 2) + rest), ("chip", "core") + mesh.axis_names[1:])
            program, band = on_device_fields, ("chip", "core")
        else:
            split, program, band = mesh, on_device_halo, "band"
        return jax.shard_map(
            program,
            mesh=split,
            in_specs=(P(band, "gx", "gy", None), P("gx", "gy", None)),
            out_specs=P(band, "gx", "gy", None),
            check_vma=False,
        )(start_bands, potential)

    return step
```

```python
import functools
import math

import jax
import jax.numpy as jnp
from jax import lax
from jax.experimental import pallas as pl
from jax.experimental.pallas import tpu as pltpu
from jax.sharding import Mesh, PartitionSpec as P

DEGREE = 4


COEFFS = (
    -5369.0 / 1800.0,
    12.0 / 7.0,
    -15.0 / 56.0,
    10.0 / 189.0,
    -1.0 / 112.0,
    2.0 / 1925.0,
    -1.0 / 16632.0,
)
REACH = len(COEFFS) - 1
LOWER_END = -0.5
CUT_LOW = 3.0
CUT_HIGH = 12.7
TILE = 8


def filter_weights(degree):
    half_width = (CUT_HIGH - CUT_LOW) / 2.0
    middle = (CUT_HIGH + CUT_LOW) / 2.0
    sigma = half_width / (LOWER_END - middle)
    tau = 2.0 / sigma
    first = sigma / half_width
    others = []
    for index in range(degree - 1):
        sigma_new = 1.0 / (tau - sigma)
        others.append((2.0 * sigma_new / half_width, sigma * sigma_new))
        sigma = sigma_new
    return (middle, first, others)


def padded_2(block, sides, width):
    for axis, dim in sides:
        count = lax.axis_size(axis)
        forward = [(i, i + 1) for i in range(count - 1)]
        forward.append((count - 1, 0))
        backward = [(target, source) for source, target in forward]
        low = lax.ppermute(
            lax.slice_in_dim(block, block.shape[dim] - width, None, axis=dim), axis, forward
        )
        high = lax.ppermute(lax.slice_in_dim(block, 0, width, axis=dim), axis, backward)
        block = jnp.concatenate([low, block, high], axis=dim)
    return block


def hamiltonian(field, potential):
    width_x = field.shape[1]
    width_y = field.shape[2]
    padded = padded_2(field, (("gx", 1), ("gy", 2)), REACH)
    laplace = 3.0 * COEFFS[0] * field
    for offset in range(1, REACH + 1):
        ahead_x = padded[:, REACH + offset : REACH + offset + width_x, REACH : REACH + width_y]
        behind_x = padded[:, REACH - offset : REACH - offset + width_x, REACH : REACH + width_y]
        ahead_y = padded[:, REACH : REACH + width_x, REACH + offset : REACH + offset + width_y]
        behind_y = padded[:, REACH : REACH + width_x, REACH - offset : REACH - offset + width_y]
        neighbours = ahead_x + behind_x
        neighbours = neighbours + ahead_y + behind_y
        neighbours = neighbours + jnp.roll(field, -offset, 3) + jnp.roll(field, offset, 3)
        laplace = laplace + COEFFS[offset] * neighbours
    return -0.5 * laplace + potential * field


def chebyshev(field, potential):
    middle, first, others = filter_weights(DEGREE)
    current = (hamiltonian(field, potential) - middle * field) * first
    previous = field
    for scale_now, scale_back in others:
        following = (
            hamiltonian(current, potential) - middle * current
        ) * scale_now - scale_back * previous
        previous = current
        current = following
    return current


def invert_factor(margin, identity):
    lower_factor = jnp.linalg.cholesky(margin)
    return jax.scipy.linalg.solve_triangular(lower_factor, identity, lower=True)


def on_device_halo(start_bands, potential):
    filtered = chebyshev(start_bands, potential)
    own_bands = filtered.shape[0]
    flattened = filtered.reshape(own_bands, -1)
    total_cells = flattened.shape[1] * lax.axis_size("gx") * lax.axis_size("gy")
    all_bands = own_bands * lax.axis_size("band")
    identity = jnp.eye(all_bands, dtype=jnp.float32)
    products = jnp.dot(
        flattened,
        lax.all_gather(flattened, "band", axis=0, tiled=True).T,
        precision=lax.Precision.HIGHEST,
        preferred_element_type=jnp.float32,
    )
    first_row = lax.axis_index("band") * own_bands
    summed = lax.psum(products, ("gx", "gy"))
    margin = lax.all_gather(summed, "band", axis=0, tiled=True) * (1.0 / total_cells)
    inverse = invert_factor(margin, identity)
    own_rows = lax.dynamic_slice_in_dim(inverse, first_row, own_bands, 0)
    rotated = jnp.dot(
        own_rows,
        lax.all_gather(flattened, "band", axis=0, tiled=True),
        precision=lax.Precision.HIGHEST,
        preferred_element_type=jnp.float32,
    )
    return rotated.reshape(filtered.shape)


def split3(value):
    high = value.astype(jnp.bfloat16)
    rest = value - high.astype(jnp.float32)
    mid = rest.astype(jnp.bfloat16)
    low = (rest - mid.astype(jnp.float32)).astype(jnp.bfloat16)
    return high, mid, low


def z_weights(nz):
    row = lax.broadcasted_iota(jnp.int32, (nz, nz), 0)
    col = lax.broadcasted_iota(jnp.int32, (nz, nz), 1)
    apart = jnp.abs(row - col)
    apart = jnp.minimum(apart, nz - apart)
    circulant = jnp.zeros((nz, nz), jnp.float32)
    for offset in range(1, REACH + 1):
        circulant = jnp.where(apart == offset, -0.5 * COEFFS[offset], circulant)
    return split3(circulant)


def place(buf, k, x, tile, height, value):
    buf[k, x, pl.ds(tile * TILE, TILE), :] = value
    if tile == 0:
        buf[k, x, pl.ds(height, TILE), :] = value


def along_z(field, w1_ref, w2_ref):
    nz = field.shape[1]
    high, mid, low = split3(field)
    part = jnp.dot(jnp.concatenate([high, mid], 1), w1_ref[...], preferred_element_type=jnp.float32)
    rest = jnp.dot(jnp.concatenate([low, high], 1), w2_ref[...], preferred_element_type=jnp.float32)
    return part[:, :nz] + part[:, nz:] + rest


def along_xy(src, k, height, wanted):
    width = src.shape[1]
    tiles = range(height // TILE)
    window = {}

    def plane(x, t):
        if (x, t) not in window:
            window[x, t] = src[k, x % width, pl.ds(t * TILE, TILE), :]
        return window[x, t]

    for x in range(width):
        rows, pairs = {}, {}

        def shifted(at):
            if at not in rows:
                rows[at] = src[k, x, pl.ds(at, TILE), :]
            return rows[at]

        def pair(*ends):
            ends = tuple(sorted(at % height for at in ends))
            if ends not in pairs:
                pairs[ends] = shifted(ends[0]) + shifted(ends[1])
            return pairs[ends]

        totals = []
        for t in tiles if wanted else ():
            total = None
            for j in range(1, REACH + 1):
                near = plane(x + j, t) + plane(x - j, t)
                near = near + pair(t * TILE + j, t * TILE - j)
                near = (-0.5 * COEFFS[j]) * near
                total = near if total is None else total + near
            totals.append(total)
        yield x, [plane(x, t) for t in tiles], totals


def laplace_kernel(dims, in_ref, field_ref, lap_ref, w1_ref, w2_ref):
    gx, gy, own, nx, ny, nz, pieces, skip = dims
    width, height, cells = gx * nx, gy * ny, nx * ny
    high, mid, low = z_weights(nz)
    for at in (0, nz):
        w1_ref[pl.ds(at, nz), pl.ds(0, nz)] = high
        w1_ref[pl.ds(at, nz), pl.ds(nz, nz)] = mid
    w2_ref[pl.ds(0, nz), :] = high
    w2_ref[pl.ds(nz, nz), :] = low
    for g in range(gx * gy):
        at_x, at_y = (g // gy) * nx, (g % gy) * ny
        for k in range(own):
            for i in range(nx):
                for t in range(ny // TILE):
                    value = in_ref[g, pl.ds(k * cells + i * ny + t * TILE, TILE), :]
                    place(field_ref, k, at_x + i, at_y // TILE + t, height, value)
    field = field_ref[:, :, pl.ds(0, height), :].reshape(own * width * height, nz)
    lap_ref[...] = along_z(field, w1_ref, w2_ref).reshape(own, width, height, nz)
    for k in range(own):
        for x, _, totals in along_xy(field_ref, k, height, True):
            for tile, total in enumerate(totals):
                rows = pl.ds(tile * TILE, TILE)
                lap_ref[k, x, rows, :] = lap_ref[k, x, rows, :] + total


def filter_kernel(dims, field_ref, lap_ref, half_ref, other_ref, w1_ref, w2_ref, out_ref, pot, buf_a, buf_b, zbuf):
    gx, gy, own, nx, ny, nz, pieces, skip = dims
    width, height, cells = gx * nx, gy * ny, nx * ny
    half = cells // 2
    rows = cells // pieces
    middle, first, others = filter_weights(DEGREE)
    shift = -middle - 1.5 * COEFFS[0]

    core = lax.axis_index("core")
    for g in range(gx * gy):
        mine = pl.ds(pl.multiple_of(core * half, TILE), half)
        theirs = pl.ds(pl.multiple_of((1 - core) * half, TILE), half)
        pot[g, mine, :] = half_ref[g, pl.ds(skip, half), :] + shift
        pot[g, theirs, :] = other_ref[g] + shift

    chain = (field_ref, buf_a, buf_b, buf_a)
    steps = [(first, None)] + others
    for step, (scale, back) in enumerate(steps):
        src, dst, old = chain[step], buf_b if step % 2 else buf_a, chain[step - 1]
        last = step == len(steps) - 1
        if step:
            field = src[:, :, pl.ds(0, height), :].reshape(own * width * height, nz)
            zbuf[...] = along_z(field, w1_ref, w2_ref).reshape(own, width, height, nz)
        squares = [jnp.zeros((TILE, nz), jnp.float32) for _ in range(own)]
        for k in range(own):
            for x, centres, totals in along_xy(src, k, height, bool(step)):
                for tile in range(height // TILE):
                    g = (x // nx) * gy + tile * TILE // ny
                    in_pencil = (x % nx) * ny + (tile * TILE) % ny
                    plain = pl.ds(tile * TILE, TILE)
                    if step:
                        total = zbuf[k, x, plain, :] + totals[tile]
                    else:
                        total = lap_ref[k, x, plain, :]
                    total = total + pot[g, pl.ds(in_pencil, TILE), :] * centres[tile]
                    value = scale * total
                    if step:
                        value = value - back * old[k, x, plain, :]
                    if not last:
                        place(dst, k, x, tile, height, value)
                        continue
                    squares[k] = squares[k] + value * value
                    for r in range(0, TILE, TILE // 2):
                        piece, row = divmod(in_pencil + r, rows)
                        to = piece_owner(piece, pieces) * gx * gy + g
                        out_ref[to, pl.ds(k * rows + row, TILE // 2), :] = value[r : r + TILE // 2]
    scales = []
    for k in range(own):
        mean = jnp.sum(squares[k], keepdims=True) * (1.0 / (width * height * nz))
        scales.append(jnp.broadcast_to(lax.rsqrt(mean), (TILE, nz)))
    line = lax.broadcasted_iota(jnp.int32, (TILE, nz), 0)
    for at in range(0, own * rows, TILE):
        factor = scales[at // rows]
        for k in range(at // rows + 1, (at + TILE - 1) // rows + 1):
            factor = jnp.where(line + at < k * rows, factor, scales[k])
        for to in range(out_ref.shape[0]):
            out_ref[to, pl.ds(at, TILE), :] = out_ref[to, pl.ds(at, TILE), :] * factor


def piece_owner(piece, pieces):
    chips = pieces // 2
    return (piece % chips) * 2 + piece // chips


def first_laplace(packed, dims):
    gx, gy, bands, nx, ny, nz, pieces, skip = dims
    width, height = gx * nx, gy * ny
    vmem = pl.BlockSpec(memory_space=pltpu.VMEM)
    cells = bands * width * height * nz
    return pl.pallas_call(
        functools.partial(laplace_kernel, dims),
        out_shape=(
            jax.ShapeDtypeStruct((bands, width, height + TILE, nz), jnp.float32),
            jax.ShapeDtypeStruct((bands, width, height, nz), jnp.float32),
            jax.ShapeDtypeStruct((2 * nz, 2 * nz), jnp.bfloat16),
            jax.ShapeDtypeStruct((2 * nz, nz), jnp.bfloat16),
        ),
        in_specs=[vmem],
        out_specs=(vmem,) * 4,
        compiler_params=pltpu.CompilerParams(vmem_limit_bytes=12 * 1024 * 1024),
        cost_estimate=pl.CostEstimate(flops=44 * cells, bytes_accessed=16 * cells, transcendentals=0),
        name="laplace",
    )(packed)


def apply_filter(field, laplace, packed, other, weights, dims):
    gx, gy, bands, nx, ny, nz, pieces, skip = dims
    vmem = pl.BlockSpec(memory_space=pltpu.VMEM)
    return pl.pallas_call(
        functools.partial(filter_kernel, dims),
        out_shape=jax.ShapeDtypeStruct((pieces * gx * gy, bands * nx * ny // pieces, nz), jnp.float32),
        in_specs=[vmem] * 6,
        out_specs=vmem,
        scratch_shapes=[
            pltpu.VMEM((gx * gy, nx * ny, nz), jnp.float32),
            pltpu.VMEM(field.shape, jnp.float32),
            pltpu.VMEM(field.shape, jnp.float32),
            pltpu.VMEM(laplace.shape, jnp.float32),
        ],
        compiler_params=pltpu.CompilerParams(vmem_limit_bytes=12 * 1024 * 1024),
        name="filter",
    )(field, laplace, packed, other, *weights)


def margin_kernel(rows, bands, scale, grid, x_ref, out_ref):
    highs, mids, lows = [], [], []
    for r in range(rows):
        high, mid, low = split3(x_ref[pl.ds(r, bands, stride=rows), :])
        highs.append(high)
        mids.append(mid)
        lows.append(low)
    terms = [jnp.concatenate(term, 1) for term in (highs, mids, lows)]
    stacked = jnp.concatenate(terms, 0)
    products = lax.dot_general(stacked, stacked, (((1,), (1,)), ((), ())), preferred_element_type=jnp.float32)

    def block(i, j):
        return products[i * bands : (i + 1) * bands, j * bands : (j + 1) * bands]

    small = block(0, 2) + block(2, 0) + block(1, 1)
    total = (small + (block(0, 1) + block(1, 0)) + block(0, 0)) * scale
    half = bands // 2
    row = lax.broadcasted_iota(jnp.int32, (half, half), 0)
    col = lax.broadcasted_iota(jnp.int32, (half, half), 1)
    strict = jnp.where(row > col, total[:half, :half], total[half:, half:])
    for core, part in enumerate((total[half:, :half], strict)):
        folded = jnp.concatenate([part[at : at + TILE] for at in range(0, half, TILE)], 1)
        for to in range(out_ref.shape[0]):
            if to // grid % 2 == core:
                out_ref[to] = folded


def partial_margin(blocks, bands, scale, pieces, grid):
    rows = blocks.shape[0] // bands
    return pl.pallas_call(
        functools.partial(margin_kernel, rows, bands, scale, grid),
        out_shape=jax.ShapeDtypeStruct((pieces * grid, TILE, (bands // 2) ** 2 // TILE), jnp.float32),
        in_specs=[pl.BlockSpec(memory_space=pltpu.VMEM)],
        out_specs=pl.BlockSpec(memory_space=pltpu.VMEM),
        compiler_params=pltpu.CompilerParams(vmem_limit_bytes=8 * 1024 * 1024),
        name="margin",
    )(blocks)


def sum_kernel(in_ref, out_ref):
    total = in_ref[0]
    for term in range(1, in_ref.shape[0]):
        total = total + in_ref[term]
    out_ref[...] = total


def sum_first(value):
    return pl.pallas_call(
        sum_kernel,
        out_shape=jax.ShapeDtypeStruct(value.shape[1:], value.dtype),
        in_specs=[pl.BlockSpec(memory_space=pltpu.VMEM)],
        out_specs=pl.BlockSpec(memory_space=pltpu.VMEM),
        compiler_params=pltpu.CompilerParams(vmem_limit_bytes=4 * 1024 * 1024),
        name="sum",
    )(value)


def eliminate(margin):
    bands = margin.shape[0]
    tiles = bands // TILE
    margin = jnp.concatenate([margin, margin], 1)
    width = 2 * bands
    lines = lax.broadcasted_iota(jnp.int32, (TILE, width), 0)
    lanes = lax.broadcasted_iota(jnp.int32, (TILE, width), 1)
    both = []
    for t in range(tiles):
        right = margin[t * TILE : (t + 1) * TILE]
        eye = jnp.where(lines + t * TILE == lanes % bands, 1.0, 0.0)
        both.append([eye, jnp.where(lanes < bands, eye, right)])

    def spread(t, at):
        return jnp.broadcast_to(both[t][1][:, bands + at : bands + at + 1], (TILE, width))

    def line_of(value, at):
        return jnp.broadcast_to(value[at : at + 1, :], (TILE, width))

    heads = [spread(0, c) for c in range(TILE)]
    for p in range(tiles):
        here = range(p * TILE, (p + 1) * TILE)
        panel = [{t: spread(t, at) for t in range(p + 1, tiles)} for at in here]
        later = [spread(p + 1, at + TILE) for at in here] if p + 1 < tiles else []
        square = [[line_of(heads[c], d) if d >= c else None for d in range(TILE)] for c in range(TILE)]
        pivots = None
        for j in range(TILE):
            pivot = square[j][j]
            pivots = pivot if j == 0 else jnp.where(lines == j, pivot, pivots)
            ratio = pl.reciprocal(pivot, approx=True)
            for c in range(j + 1, TILE):
                for d in range(c, TILE):
                    square[c][d] = square[c][d] - (square[j][c] * square[j][d]) * ratio
            factor = {t: panel[j][t] * ratio for t in range(p + 1, tiles)}
            factor[p] = jnp.where(lines > j, heads[j] * ratio, 0.0)
            for c in range(j + 1, TILE):
                heads[c] = heads[c] - factor[p] * square[j][c]
                for t in range(p + 1, tiles):
                    panel[c][t] = panel[c][t] - factor[t] * square[j][c]
            for c, column in enumerate(later):
                later[c] = column - factor[p + 1] * line_of(panel[j][p + 1], c)
            pair = [line_of(value, j) for value in both[p]]
            for t in range(p, tiles):
                both[t] = [value - factor[t] * line for value, line in zip(both[t], pair)]
        heads = later
        scale = lax.rsqrt(pivots)
        both[p] = [value * scale for value in both[p]]
    return [jnp.concatenate(value, 1) for value in both]


def split_pair(split_ref, at, part, pair, bands):
    rows = part.shape[0] // bands
    nz = part.shape[1]
    for i in range(2):
        terms = split3(part[pl.ds(2 * pair + i, bands, stride=rows), :])
        for j, term in enumerate(terms):
            split_ref[at, pl.ds(j * bands, bands), pl.ds(i * nz, nz)] = term


def inverse_kernel(dims, *refs):
    bands, own = dims
    own_ref, other_ref, left_ref, inv_ref = refs
    half = bands // 2
    here, there = own_ref[...], other_ref[...]
    first = lax.axis_index("core") == 0
    cross, strict = [
        jnp.concatenate([value[:, at : at + half] for at in range(0, half * half // TILE, half)], 0)
        for value in (jnp.where(first, here, there), jnp.where(first, there, here))
    ]
    row = lax.broadcasted_iota(jnp.int32, (half, half), 0)
    col = lax.broadcasted_iota(jnp.int32, (half, half), 1)
    turned = strict.T
    low = jnp.where(row == col, 1.0, jnp.where(row > col, strict, turned))
    high = jnp.where(row == col, 1.0, jnp.where(row < col, strict, turned))
    margin = jnp.concatenate(
        [jnp.concatenate([low, cross.T], 1), jnp.concatenate([cross, high], 1)], 0
    )
    for t, value in enumerate(eliminate(margin)):
        inv_ref[pl.ds(t * TILE, TILE), :] = value
    first = pl.multiple_of((lax.axis_index("chip") * 2 + lax.axis_index("core")) * own, TILE)
    rows = inv_ref[pl.ds(first, own), pl.ds(0, 3 * bands)]
    lanes = lax.broadcasted_iota(jnp.int32, rows.shape, 1)
    high = rows.astype(jnp.bfloat16)
    rest = rows - high.astype(jnp.float32)
    mid = rest.astype(jnp.bfloat16)
    low = rest - mid.astype(jnp.float32)
    left_ref[pl.ds(0, own), :] = high
    left_ref[pl.ds(own, own), :] = jnp.where(lanes < 2 * bands, rest, 0.0).astype(jnp.bfloat16)
    left_ref[pl.ds(2 * own, own), :] = jnp.where(lanes < bands, low, 0.0).astype(jnp.bfloat16)


def inverse_rows(margins, own, bands):
    vmem = pl.BlockSpec(memory_space=pltpu.VMEM)
    return pl.pallas_call(
        functools.partial(inverse_kernel, (bands, own)),
        out_shape=jax.ShapeDtypeStruct((3 * own, 3 * bands), jnp.bfloat16),
        in_specs=[vmem] * len(margins),
        out_specs=vmem,
        scratch_shapes=[pltpu.VMEM((bands, 4 * bands), jnp.float32)],
        compiler_params=pltpu.CompilerParams(vmem_limit_bytes=4 * 1024 * 1024),
        name="inverse",
    )(*margins)


def rotate_kernel(dims, left_ref, *refs):
    bands, own = dims
    parts, out_ref = refs[:-1], refs[-1]
    rows = parts[0].shape[0] // bands
    nz = parts[0].shape[1]
    left = left_ref[...]
    chips = len(parts) // 2
    chip, core = lax.axis_index("chip"), lax.axis_index("core")
    for index, part in enumerate(parts):
        piece = (core ^ (index // chips)) * chips + (chip ^ (index % chips))
        for r in range(0, rows, 2):
            terms = [split3(part[pl.ds(r + i, bands, stride=rows), :]) for i in range(2)]
            block = jnp.concatenate([jnp.concatenate(term, 1) for term in zip(*terms)], 0)
            product = jnp.dot(left, block, preferred_element_type=jnp.float32)
            value = product[:own] + (product[own : 2 * own] + product[2 * own :])
            for i in range(2):
                start = piece * rows + r + i
                out_ref[pl.ds(start, own, stride=rows * len(parts)), :] = value[:, i * nz : (i + 1) * nz]


def rotate(left, parts, bands):
    rows = parts[0].shape[0] // bands
    own = left.shape[0] // 3
    nz = parts[0].shape[1]
    vmem = pl.BlockSpec(memory_space=pltpu.VMEM)
    return pl.pallas_call(
        functools.partial(rotate_kernel, (bands, own)),
        out_shape=jax.ShapeDtypeStruct((own * rows * len(parts), nz), jnp.float32),
        in_specs=[vmem] * (1 + len(parts)),
        out_specs=vmem,
        compiler_params=pltpu.CompilerParams(vmem_limit_bytes=6 * 1024 * 1024),
        name="rotate",
    )(left, *parts)


def on_device_fields(start_bands, potential):
    own_bands, nx, ny, nz = start_bands.shape
    gx, gy, chips = lax.axis_size("gx"), lax.axis_size("gy"), lax.axis_size("chip")
    pieces = 2 * chips
    grid = gx * gy
    own = own_bands // grid
    cells = nx * ny
    bands = own_bands * pieces
    rows = cells // pieces
    core = lax.axis_index("core")
    swap = [(0, 1), (1, 0)]

    fields = start_bands.reshape(grid, own * cells, nz)
    flat_potential = potential.reshape(cells, nz)
    half = cells // 2
    own_half = lax.dynamic_slice_in_dim(flat_potential, core * half, half, 0)
    packed = lax.optimization_barrier(jnp.pad(fields, ((0, 0), (0, half), (0, 0))))
    packed = packed.at[:, own * cells :, :].set(own_half[None])
    packed = lax.all_to_all(packed, ("gx", "gy"), 0, 0)
    other = lax.ppermute(packed[:, own * cells :, :], "core", swap)
    dims = (gx, gy, own, nx, ny, nz, pieces, own * cells)
    field, laplace, *weights = first_laplace(packed, dims)
    filtered = apply_filter(field, laplace, packed, other, weights, dims)
    blocks = lax.all_to_all(filtered, ("chip", "core", "gx", "gy"), 0, 0).reshape(bands * rows, nz)

    def tied(value, first):
        return lax.optimization_barrier((value, first))[0]

    def copies(value, *axes):
        count = math.prod(lax.axis_size(axis) for axis in axes)
        pairs = [[(i, i ^ mask) for i in range(count)] for mask in range(1, count)]
        return [value] + [lax.ppermute(value, axes, pair) for pair in pairs]

    spread = partial_margin(blocks, bands, 1.0 / (cells * nz * grid), pieces, grid)
    parts = copies(blocks, "chip")
    crossed = [lax.ppermute(blocks, "core", swap)]
    crossed, spread = lax.optimization_barrier((crossed, spread))
    margins = lax.all_to_all(spread, ("chip", "core", "gx", "gy"), 0, 0)
    margins = copies(sum_first(margins), "core")
    far, margins = lax.optimization_barrier((parts[1:], margins))
    parts += crossed + [lax.ppermute(part, "core", swap) for part in far]
    left = inverse_rows(margins, own_bands, bands)
    rotated = rotate(left, parts, bands)
    return rotated.reshape(start_bands.shape)


def power_of_two(count):
    return count & (count - 1) == 0


def whole_fields(mesh, shape):
    gx, gy, pieces = mesh.shape["gx"], mesh.shape["gy"], mesh.shape["band"]
    bands, nx, ny, nz = shape[0], shape[1] // gx, shape[2] // gy, shape[3]
    own_bands, cells = bands // pieces, nx * ny
    return (
        own_bands % (gx * gy) == 0
        and own_bands % (2 * TILE) == 0
        and pieces % 2 == 0
        and power_of_two(pieces)
        and ny % TILE == 0
        and nz % 128 == 0
        and bands % 64 == 0
        and cells % (2 * TILE) == 0
        and cells % (pieces * TILE // 2) == 0
        and pieces > 2
        and (own_bands // (gx * gy)) * (cells // pieces) % TILE == 0
        and shape[1] > 2 * REACH
    )


def solution(mesh):
    def step(start_bands, potential):
        if whole_fields(mesh, start_bands.shape):
            chips = mesh.shape["band"] // 2
            rest = mesh.devices.shape[1:]
            split = Mesh(mesh.devices.reshape((chips, 2) + rest), ("chip", "core") + mesh.axis_names[1:])
            program, band = on_device_fields, ("chip", "core")
        else:
            split, program, band = mesh, on_device_halo, "band"
        return jax.shard_map(
            program,
            mesh=split,
            in_specs=(P(band, "gx", "gy", None), P("gx", "gy", None)),
            out_specs=P(band, "gx", "gy", None),
            check_vma=False,
        )(start_bands, potential)

    return step
```

```python
import functools
import math

import jax
import jax.numpy as jnp
from jax import lax
from jax.experimental import pallas as pl
from jax.experimental.pallas import tpu as pltpu
from jax.sharding import Mesh, PartitionSpec as P

DEGREE = 4


COEFFS = (
    -5369.0 / 1800.0,
    12.0 / 7.0,
    -15.0 / 56.0,
    10.0 / 189.0,
    -1.0 / 112.0,
    2.0 / 1925.0,
    -1.0 / 16632.0,
)
REACH = len(COEFFS) - 1
LOWER_END = -0.5
CUT_LOW = 3.0
CUT_HIGH = 12.7
TILE = 8


def filter_weights(degree):
    half_width = (CUT_HIGH - CUT_LOW) / 2.0
    middle = (CUT_HIGH + CUT_LOW) / 2.0
    sigma = half_width / (LOWER_END - middle)
    tau = 2.0 / sigma
    first = sigma / half_width
    others = []
    for index in range(degree - 1):
        sigma_new = 1.0 / (tau - sigma)
        others.append((2.0 * sigma_new / half_width, sigma * sigma_new))
        sigma = sigma_new
    return (middle, first, others)


def padded_2(block, sides, width):
    for axis, dim in sides:
        count = lax.axis_size(axis)
        forward = [(i, i + 1) for i in range(count - 1)]
        forward.append((count - 1, 0))
        backward = [(target, source) for source, target in forward]
        low = lax.ppermute(
            lax.slice_in_dim(block, block.shape[dim] - width, None, axis=dim), axis, forward
        )
        high = lax.ppermute(lax.slice_in_dim(block, 0, width, axis=dim), axis, backward)
        block = jnp.concatenate([low, block, high], axis=dim)
    return block


def hamiltonian(field, potential):
    width_x = field.shape[1]
    width_y = field.shape[2]
    padded = padded_2(field, (("gx", 1), ("gy", 2)), REACH)
    laplace = 3.0 * COEFFS[0] * field
    for offset in range(1, REACH + 1):
        ahead_x = padded[:, REACH + offset : REACH + offset + width_x, REACH : REACH + width_y]
        behind_x = padded[:, REACH - offset : REACH - offset + width_x, REACH : REACH + width_y]
        ahead_y = padded[:, REACH : REACH + width_x, REACH + offset : REACH + offset + width_y]
        behind_y = padded[:, REACH : REACH + width_x, REACH - offset : REACH - offset + width_y]
        neighbours = ahead_x + behind_x
        neighbours = neighbours + ahead_y + behind_y
        neighbours = neighbours + jnp.roll(field, -offset, 3) + jnp.roll(field, offset, 3)
        laplace = laplace + COEFFS[offset] * neighbours
    return -0.5 * laplace + potential * field


def chebyshev(field, potential):
    middle, first, others = filter_weights(DEGREE)
    current = (hamiltonian(field, potential) - middle * field) * first
    previous = field
    for scale_now, scale_back in others:
        following = (
            hamiltonian(current, potential) - middle * current
        ) * scale_now - scale_back * previous
        previous = current
        current = following
    return current


def invert_factor(margin, identity):
    lower_factor = jnp.linalg.cholesky(margin)
    return jax.scipy.linalg.solve_triangular(lower_factor, identity, lower=True)


def on_device_halo(start_bands, potential):
    filtered = chebyshev(start_bands, potential)
    own_bands = filtered.shape[0]
    flattened = filtered.reshape(own_bands, -1)
    total_cells = flattened.shape[1] * lax.axis_size("gx") * lax.axis_size("gy")
    all_bands = own_bands * lax.axis_size("band")
    identity = jnp.eye(all_bands, dtype=jnp.float32)
    products = jnp.dot(
        flattened,
        lax.all_gather(flattened, "band", axis=0, tiled=True).T,
        precision=lax.Precision.HIGHEST,
        preferred_element_type=jnp.float32,
    )
    first_row = lax.axis_index("band") * own_bands
    summed = lax.psum(products, ("gx", "gy"))
    margin = lax.all_gather(summed, "band", axis=0, tiled=True) * (1.0 / total_cells)
    inverse = invert_factor(margin, identity)
    own_rows = lax.dynamic_slice_in_dim(inverse, first_row, own_bands, 0)
    rotated = jnp.dot(
        own_rows,
        lax.all_gather(flattened, "band", axis=0, tiled=True),
        precision=lax.Precision.HIGHEST,
        preferred_element_type=jnp.float32,
    )
    return rotated.reshape(filtered.shape)


def split3(value):
    high = value.astype(jnp.bfloat16)
    rest = value - high.astype(jnp.float32)
    mid = rest.astype(jnp.bfloat16)
    low = (rest - mid.astype(jnp.float32)).astype(jnp.bfloat16)
    return high, mid, low


def z_weights(nz):
    row = lax.broadcasted_iota(jnp.int32, (nz, nz), 0)
    col = lax.broadcasted_iota(jnp.int32, (nz, nz), 1)
    apart = jnp.abs(row - col)
    apart = jnp.minimum(apart, nz - apart)
    circulant = jnp.zeros((nz, nz), jnp.float32)
    for offset in range(1, REACH + 1):
        circulant = jnp.where(apart == offset, -0.5 * COEFFS[offset], circulant)
    return split3(circulant)


def place(buf, k, x, tile, height, value):
    buf[k, x, pl.ds(tile * TILE, TILE), :] = value
    if tile == 0:
        buf[k, x, pl.ds(height, TILE), :] = value


def along_z(field, w1_ref, w2_ref):
    nz = field.shape[1]
    high, mid, low = split3(field)
    part = jnp.dot(jnp.concatenate([high, mid], 1), w1_ref[...], preferred_element_type=jnp.float32)
    rest = jnp.dot(jnp.concatenate([low, high], 1), w2_ref[...], preferred_element_type=jnp.float32)
    return part[:, :nz] + part[:, nz:] + rest


def along_xy(src, k, height, wanted):
    width = src.shape[1]
    tiles = range(height // TILE)
    window = {}

    def plane(x, t):
        if (x, t) not in window:
            window[x, t] = src[k, x % width, pl.ds(t * TILE, TILE), :]
        return window[x, t]

    for x in range(width):
        rows, pairs = {}, {}

        def shifted(at):
            if at not in rows:
                rows[at] = src[k, x, pl.ds(at, TILE), :]
            return rows[at]

        def pair(*ends):
            ends = tuple(sorted(at % height for at in ends))
            if ends not in pairs:
                pairs[ends] = shifted(ends[0]) + shifted(ends[1])
            return pairs[ends]

        totals = []
        for t in tiles if wanted else ():
            total = None
            for j in range(1, REACH + 1):
                near = plane(x + j, t) + plane(x - j, t)
                near = near + pair(t * TILE + j, t * TILE - j)
                near = (-0.5 * COEFFS[j]) * near
                total = near if total is None else total + near
            totals.append(total)
        yield x, [plane(x, t) for t in tiles], totals


def laplace_kernel(dims, in_ref, field_ref, lap_ref, w1_ref, w2_ref):
    gx, gy, own, nx, ny, nz, pieces, skip = dims
    width, height, cells = gx * nx, gy * ny, nx * ny
    high, mid, low = z_weights(nz)
    for at in (0, nz):
        w1_ref[pl.ds(at, nz), pl.ds(0, nz)] = high
        w1_ref[pl.ds(at, nz), pl.ds(nz, nz)] = mid
    w2_ref[pl.ds(0, nz), :] = high
    w2_ref[pl.ds(nz, nz), :] = low
    for g in range(gx * gy):
        at_x, at_y = (g % gx) * nx, (g // gx) * ny
        for k in range(own):
            for i in range(nx):
                for t in range(ny // TILE):
                    value = in_ref[g, pl.ds(k * cells + i * ny + t * TILE, TILE), :]
                    place(field_ref, k, at_x + i, at_y // TILE + t, height, value)
    field = field_ref[:, :, pl.ds(0, height), :].reshape(own * width * height, nz)
    lap_ref[...] = along_z(field, w1_ref, w2_ref).reshape(own, width, height, nz)
    for k in range(own):
        for x, _, totals in along_xy(field_ref, k, height, True):
            for tile, total in enumerate(totals):
                rows = pl.ds(tile * TILE, TILE)
                lap_ref[k, x, rows, :] = lap_ref[k, x, rows, :] + total


def filter_kernel(dims, field_ref, lap_ref, half_ref, other_ref, w1_ref, w2_ref, out_ref, pot, buf_a, buf_b, zbuf):
    gx, gy, own, nx, ny, nz, pieces, skip = dims
    width, height, cells = gx * nx, gy * ny, nx * ny
    half = cells // 2
    rows = cells // pieces
    middle, first, others = filter_weights(DEGREE)
    shift = -middle - 1.5 * COEFFS[0]

    core = lax.axis_index("core")
    for g in range(gx * gy):
        mine = pl.ds(pl.multiple_of(core * half, TILE), half)
        theirs = pl.ds(pl.multiple_of((1 - core) * half, TILE), half)
        pot[g, mine, :] = half_ref[g, pl.ds(skip, half), :] + shift
        pot[g, theirs, :] = other_ref[g] + shift

    chain = (field_ref, buf_a, buf_b, buf_a)
    steps = [(first, None)] + others
    for step, (scale, back) in enumerate(steps):
        src, dst, old = chain[step], buf_b if step % 2 else buf_a, chain[step - 1]
        last = step == len(steps) - 1
        if step:
            field = src[:, :, pl.ds(0, height), :].reshape(own * width * height, nz)
            zbuf[...] = along_z(field, w1_ref, w2_ref).reshape(own, width, height, nz)
        squares = [jnp.zeros((TILE, nz), jnp.float32) for _ in range(own)]
        for k in range(own):
            for x, centres, totals in along_xy(src, k, height, bool(step)):
                for tile in range(height // TILE):
                    g = (tile * TILE // ny) * gx + x // nx
                    in_pencil = (x % nx) * ny + (tile * TILE) % ny
                    plain = pl.ds(tile * TILE, TILE)
                    if step:
                        total = zbuf[k, x, plain, :] + totals[tile]
                    else:
                        total = lap_ref[k, x, plain, :]
                    total = total + pot[g, pl.ds(in_pencil, TILE), :] * centres[tile]
                    value = scale * total
                    if step:
                        value = value - back * old[k, x, plain, :]
                    if not last:
                        place(dst, k, x, tile, height, value)
                        continue
                    squares[k] = squares[k] + value * value
                    for r in range(0, TILE, TILE // 2):
                        piece, row = divmod(in_pencil + r, rows)
                        to = piece_owner(piece, pieces) * gx * gy + g
                        out_ref[to, pl.ds(k * rows + row, TILE // 2), :] = value[r : r + TILE // 2]
    scales = []
    for k in range(own):
        mean = jnp.sum(squares[k], keepdims=True) * (1.0 / (width * height * nz))
        scales.append(jnp.broadcast_to(lax.rsqrt(mean), (TILE, nz)))
    line = lax.broadcasted_iota(jnp.int32, (TILE, nz), 0)
    for at in range(0, own * rows, TILE):
        factor = scales[at // rows]
        for k in range(at // rows + 1, (at + TILE - 1) // rows + 1):
            factor = jnp.where(line + at < k * rows, factor, scales[k])
        for to in range(out_ref.shape[0]):
            out_ref[to, pl.ds(at, TILE), :] = out_ref[to, pl.ds(at, TILE), :] * factor


def piece_owner(piece, pieces):
    chips = pieces // 2
    return (piece % chips) * 2 + piece // chips


def first_laplace(packed, dims):
    gx, gy, bands, nx, ny, nz, pieces, skip = dims
    width, height = gx * nx, gy * ny
    vmem = pl.BlockSpec(memory_space=pltpu.VMEM)
    cells = bands * width * height * nz
    return pl.pallas_call(
        functools.partial(laplace_kernel, dims),
        out_shape=(
            jax.ShapeDtypeStruct((bands, width, height + TILE, nz), jnp.float32),
            jax.ShapeDtypeStruct((bands, width, height, nz), jnp.float32),
            jax.ShapeDtypeStruct((2 * nz, 2 * nz), jnp.bfloat16),
            jax.ShapeDtypeStruct((2 * nz, nz), jnp.bfloat16),
        ),
        in_specs=[vmem],
        out_specs=(vmem,) * 4,
        compiler_params=pltpu.CompilerParams(vmem_limit_bytes=12 * 1024 * 1024),
        cost_estimate=pl.CostEstimate(flops=44 * cells, bytes_accessed=16 * cells, transcendentals=0),
        name="laplace",
    )(packed)


def apply_filter(field, laplace, packed, other, weights, dims):
    gx, gy, bands, nx, ny, nz, pieces, skip = dims
    vmem = pl.BlockSpec(memory_space=pltpu.VMEM)
    return pl.pallas_call(
        functools.partial(filter_kernel, dims),
        out_shape=jax.ShapeDtypeStruct((pieces * gx * gy, bands * nx * ny // pieces, nz), jnp.float32),
        in_specs=[vmem] * 6,
        out_specs=vmem,
        scratch_shapes=[
            pltpu.VMEM((gx * gy, nx * ny, nz), jnp.float32),
            pltpu.VMEM(field.shape, jnp.float32),
            pltpu.VMEM(field.shape, jnp.float32),
            pltpu.VMEM(laplace.shape, jnp.float32),
        ],
        compiler_params=pltpu.CompilerParams(vmem_limit_bytes=12 * 1024 * 1024),
        name="filter",
    )(field, laplace, packed, other, *weights)


def margin_kernel(rows, bands, scale, grid, x_ref, out_ref):
    highs, mids, lows = [], [], []
    for r in range(rows):
        high, mid, low = split3(x_ref[pl.ds(r, bands, stride=rows), :])
        highs.append(high)
        mids.append(mid)
        lows.append(low)
    terms = [jnp.concatenate(term, 1) for term in (highs, mids, lows)]
    stacked = jnp.concatenate(terms, 0)
    products = lax.dot_general(stacked, stacked, (((1,), (1,)), ((), ())), preferred_element_type=jnp.float32)

    def block(i, j):
        return products[i * bands : (i + 1) * bands, j * bands : (j + 1) * bands]

    small = block(0, 2) + block(2, 0) + block(1, 1)
    total = (small + (block(0, 1) + block(1, 0)) + block(0, 0)) * scale
    half = bands // 2
    row = lax.broadcasted_iota(jnp.int32, (half, half), 0)
    col = lax.broadcasted_iota(jnp.int32, (half, half), 1)
    strict = jnp.where(row > col, total[:half, :half], total[half:, half:])
    for core, part in enumerate((total[half:, :half], strict)):
        folded = jnp.concatenate([part[at : at + TILE] for at in range(0, half, TILE)], 1)
        for to in range(out_ref.shape[0]):
            if to // grid % 2 == core:
                out_ref[to] = folded


def partial_margin(blocks, bands, scale, pieces, grid):
    rows = blocks.shape[0] // bands
    return pl.pallas_call(
        functools.partial(margin_kernel, rows, bands, scale, grid),
        out_shape=jax.ShapeDtypeStruct((pieces * grid, TILE, (bands // 2) ** 2 // TILE), jnp.float32),
        in_specs=[pl.BlockSpec(memory_space=pltpu.VMEM)],
        out_specs=pl.BlockSpec(memory_space=pltpu.VMEM),
        compiler_params=pltpu.CompilerParams(vmem_limit_bytes=8 * 1024 * 1024),
        name="margin",
    )(blocks)


def sum_kernel(in_ref, out_ref):
    total = in_ref[0]
    for term in range(1, in_ref.shape[0]):
        total = total + in_ref[term]
    out_ref[...] = total


def sum_first(value):
    return pl.pallas_call(
        sum_kernel,
        out_shape=jax.ShapeDtypeStruct(value.shape[1:], value.dtype),
        in_specs=[pl.BlockSpec(memory_space=pltpu.VMEM)],
        out_specs=pl.BlockSpec(memory_space=pltpu.VMEM),
        compiler_params=pltpu.CompilerParams(vmem_limit_bytes=4 * 1024 * 1024),
        name="sum",
    )(value)


def eliminate(margin):
    bands = margin.shape[0]
    tiles = bands // TILE
    margin = jnp.concatenate([margin, margin], 1)
    width = 2 * bands
    lines = lax.broadcasted_iota(jnp.int32, (TILE, width), 0)
    lanes = lax.broadcasted_iota(jnp.int32, (TILE, width), 1)
    both = []
    for t in range(tiles):
        right = margin[t * TILE : (t + 1) * TILE]
        eye = jnp.where(lines + t * TILE == lanes % bands, 1.0, 0.0)
        both.append([eye, jnp.where(lanes < bands, eye, right)])

    def spread(t, at):
        return jnp.broadcast_to(both[t][1][:, bands + at : bands + at + 1], (TILE, width))

    def line_of(value, at):
        return jnp.broadcast_to(value[at : at + 1, :], (TILE, width))

    heads = [spread(0, c) for c in range(TILE)]
    for p in range(tiles):
        here = range(p * TILE, (p + 1) * TILE)
        panel = [{t: spread(t, at) for t in range(p + 1, tiles)} for at in here]
        later = [spread(p + 1, at + TILE) for at in here] if p + 1 < tiles else []
        square = [[line_of(heads[c], d) if d >= c else None for d in range(TILE)] for c in range(TILE)]
        pivots = None
        for j in range(TILE):
            pivot = square[j][j]
            pivots = pivot if j == 0 else jnp.where(lines == j, pivot, pivots)
            ratio = pl.reciprocal(pivot, approx=True)
            for c in range(j + 1, TILE):
                for d in range(c, TILE):
                    square[c][d] = square[c][d] - (square[j][c] * square[j][d]) * ratio
            factor = {t: panel[j][t] * ratio for t in range(p + 1, tiles)}
            factor[p] = jnp.where(lines > j, heads[j] * ratio, 0.0)
            for c in range(j + 1, TILE):
                heads[c] = heads[c] - factor[p] * square[j][c]
                for t in range(p + 1, tiles):
                    panel[c][t] = panel[c][t] - factor[t] * square[j][c]
            for c, column in enumerate(later):
                later[c] = column - factor[p + 1] * line_of(panel[j][p + 1], c)
            pair = [line_of(value, j) for value in both[p]]
            for t in range(p, tiles):
                both[t] = [value - factor[t] * line for value, line in zip(both[t], pair)]
        heads = later
        scale = lax.rsqrt(pivots)
        both[p] = [value * scale for value in both[p]]
    return [jnp.concatenate(value, 1) for value in both]


def split_pair(split_ref, at, part, pair, bands):
    rows = part.shape[0] // bands
    nz = part.shape[1]
    for i in range(2):
        terms = split3(part[pl.ds(2 * pair + i, bands, stride=rows), :])
        for j, term in enumerate(terms):
            split_ref[at, pl.ds(j * bands, bands), pl.ds(i * nz, nz)] = term


def inverse_kernel(dims, *refs):
    bands, own = dims
    own_ref, other_ref, left_ref, inv_ref = refs
    half = bands // 2
    here, there = own_ref[...], other_ref[...]
    first = lax.axis_index("core") == 0
    cross, strict = [
        jnp.concatenate([value[:, at : at + half] for at in range(0, half * half // TILE, half)], 0)
        for value in (jnp.where(first, here, there), jnp.where(first, there, here))
    ]
    row = lax.broadcasted_iota(jnp.int32, (half, half), 0)
    col = lax.broadcasted_iota(jnp.int32, (half, half), 1)
    turned = strict.T
    low = jnp.where(row == col, 1.0, jnp.where(row > col, strict, turned))
    high = jnp.where(row == col, 1.0, jnp.where(row < col, strict, turned))
    margin = jnp.concatenate(
        [jnp.concatenate([low, cross.T], 1), jnp.concatenate([cross, high], 1)], 0
    )
    for t, value in enumerate(eliminate(margin)):
        inv_ref[pl.ds(t * TILE, TILE), :] = value
    first = pl.multiple_of((lax.axis_index("chip") * 2 + lax.axis_index("core")) * own, TILE)
    rows = inv_ref[pl.ds(first, own), pl.ds(0, 3 * bands)]
    lanes = lax.broadcasted_iota(jnp.int32, rows.shape, 1)
    high = rows.astype(jnp.bfloat16)
    rest = rows - high.astype(jnp.float32)
    mid = rest.astype(jnp.bfloat16)
    low = rest - mid.astype(jnp.float32)
    left_ref[pl.ds(0, own), :] = high
    left_ref[pl.ds(own, own), :] = jnp.where(lanes < 2 * bands, rest, 0.0).astype(jnp.bfloat16)
    left_ref[pl.ds(2 * own, own), :] = jnp.where(lanes < bands, low, 0.0).astype(jnp.bfloat16)


def inverse_rows(margins, own, bands):
    vmem = pl.BlockSpec(memory_space=pltpu.VMEM)
    return pl.pallas_call(
        functools.partial(inverse_kernel, (bands, own)),
        out_shape=jax.ShapeDtypeStruct((3 * own, 3 * bands), jnp.bfloat16),
        in_specs=[vmem] * len(margins),
        out_specs=vmem,
        scratch_shapes=[pltpu.VMEM((bands, 4 * bands), jnp.float32)],
        compiler_params=pltpu.CompilerParams(vmem_limit_bytes=4 * 1024 * 1024),
        name="inverse",
    )(*margins)


def rotate_kernel(dims, left_ref, *refs):
    bands, own = dims
    parts, out_ref = refs[:-1], refs[-1]
    rows = parts[0].shape[0] // bands
    nz = parts[0].shape[1]
    left = left_ref[...]
    chips = len(parts) // 2
    chip, core = lax.axis_index("chip"), lax.axis_index("core")
    for index, part in enumerate(parts):
        piece = (core ^ (index // chips)) * chips + (chip ^ (index % chips))
        for r in range(0, rows, 2):
            terms = [split3(part[pl.ds(r + i, bands, stride=rows), :]) for i in range(2)]
            block = jnp.concatenate([jnp.concatenate(term, 1) for term in zip(*terms)], 0)
            product = jnp.dot(left, block, preferred_element_type=jnp.float32)
            value = product[:own] + (product[own : 2 * own] + product[2 * own :])
            for i in range(2):
                start = piece * rows + r + i
                out_ref[pl.ds(start, own, stride=rows * len(parts)), :] = value[:, i * nz : (i + 1) * nz]


def rotate(left, parts, bands):
    rows = parts[0].shape[0] // bands
    own = left.shape[0] // 3
    nz = parts[0].shape[1]
    vmem = pl.BlockSpec(memory_space=pltpu.VMEM)
    return pl.pallas_call(
        functools.partial(rotate_kernel, (bands, own)),
        out_shape=jax.ShapeDtypeStruct((own * rows * len(parts), nz), jnp.float32),
        in_specs=[vmem] * (1 + len(parts)),
        out_specs=vmem,
        compiler_params=pltpu.CompilerParams(vmem_limit_bytes=6 * 1024 * 1024),
        name="rotate",
    )(left, *parts)


def on_device_fields(start_bands, potential):
    own_bands, nx, ny, nz = start_bands.shape
    gx, gy, chips = lax.axis_size("gx"), lax.axis_size("gy"), lax.axis_size("chip")
    pieces = 2 * chips
    grid = gx * gy
    own = own_bands // grid
    cells = nx * ny
    bands = own_bands * pieces
    rows = cells // pieces
    core = lax.axis_index("core")
    swap = [(0, 1), (1, 0)]

    fields = start_bands.reshape(grid, own * cells, nz)
    flat_potential = potential.reshape(cells, nz)
    half = cells // 2
    own_half = lax.dynamic_slice_in_dim(flat_potential, core * half, half, 0)
    packed = lax.optimization_barrier(jnp.pad(fields, ((0, 0), (0, half), (0, 0))))
    packed = packed.at[:, own * cells :, :].set(own_half[None])
    packed = lax.all_to_all(packed, ("gy", "gx"), 0, 0)
    other = lax.ppermute(packed[:, own * cells :, :], "core", swap)
    dims = (gx, gy, own, nx, ny, nz, pieces, own * cells)
    field, laplace, *weights = first_laplace(packed, dims)
    filtered = apply_filter(field, laplace, packed, other, weights, dims)
    blocks = lax.all_to_all(filtered, ("chip", "core", "gy", "gx"), 0, 0).reshape(bands * rows, nz)

    def tied(value, first):
        return lax.optimization_barrier((value, first))[0]

    def copies(value, *axes):
        count = math.prod(lax.axis_size(axis) for axis in axes)
        pairs = [[(i, i ^ mask) for i in range(count)] for mask in range(1, count)]
        return [value] + [lax.ppermute(value, axes, pair) for pair in pairs]

    spread = partial_margin(blocks, bands, 1.0 / (cells * nz * grid), pieces, grid)
    parts = copies(blocks, "chip")
    crossed = [lax.ppermute(blocks, "core", swap)]
    crossed, spread = lax.optimization_barrier((crossed, spread))
    margins = lax.all_to_all(spread, ("chip", "core", "gx", "gy"), 0, 0)
    margins = copies(sum_first(margins), "core")
    far, margins = lax.optimization_barrier((parts[1:], margins))
    parts += crossed + [lax.ppermute(part, "core", swap) for part in far]
    left = inverse_rows(margins, own_bands, bands)
    rotated = rotate(left, parts, bands)
    return rotated.reshape(start_bands.shape)


def power_of_two(count):
    return count & (count - 1) == 0


def whole_fields(mesh, shape):
    gx, gy, pieces = mesh.shape["gx"], mesh.shape["gy"], mesh.shape["band"]
    bands, nx, ny, nz = shape[0], shape[1] // gx, shape[2] // gy, shape[3]
    own_bands, cells = bands // pieces, nx * ny
    return (
        own_bands % (gx * gy) == 0
        and own_bands % (2 * TILE) == 0
        and pieces % 2 == 0
        and power_of_two(pieces)
        and ny % TILE == 0
        and nz % 128 == 0
        and bands % 64 == 0
        and cells % (2 * TILE) == 0
        and cells % (pieces * TILE // 2) == 0
        and pieces > 2
        and (own_bands // (gx * gy)) * (cells // pieces) % TILE == 0
        and shape[1] > 2 * REACH
    )


def solution(mesh):
    def step(start_bands, potential):
        if whole_fields(mesh, start_bands.shape):
            chips = mesh.shape["band"] // 2
            rest = mesh.devices.shape[1:]
            split = Mesh(mesh.devices.reshape((chips, 2) + rest), ("chip", "core") + mesh.axis_names[1:])
            program, band = on_device_fields, ("chip", "core")
        else:
            split, program, band = mesh, on_device_halo, "band"
        return jax.shard_map(
            program,
            mesh=split,
            in_specs=(P(band, "gx", "gy", None), P("gx", "gy", None)),
            out_specs=P(band, "gx", "gy", None),
            check_vma=False,
        )(start_bands, potential)

    return step
```

```python
import functools
import math

import jax
import jax.numpy as jnp
from jax import lax
from jax.experimental import pallas as pl
from jax.experimental.pallas import tpu as pltpu
from jax.sharding import Mesh, PartitionSpec as P

DEGREE = 4


COEFFS = (
    -5369.0 / 1800.0,
    12.0 / 7.0,
    -15.0 / 56.0,
    10.0 / 189.0,
    -1.0 / 112.0,
    2.0 / 1925.0,
    -1.0 / 16632.0,
)
REACH = len(COEFFS) - 1
LOWER_END = -0.5
CUT_LOW = 3.0
CUT_HIGH = 12.7
TILE = 8


def filter_weights(degree):
    half_width = (CUT_HIGH - CUT_LOW) / 2.0
    middle = (CUT_HIGH + CUT_LOW) / 2.0
    sigma = half_width / (LOWER_END - middle)
    tau = 2.0 / sigma
    first = sigma / half_width
    others = []
    for index in range(degree - 1):
        sigma_new = 1.0 / (tau - sigma)
        others.append((2.0 * sigma_new / half_width, sigma * sigma_new))
        sigma = sigma_new
    return (middle, first, others)


def padded_2(block, sides, width):
    for axis, dim in sides:
        count = lax.axis_size(axis)
        forward = [(i, i + 1) for i in range(count - 1)]
        forward.append((count - 1, 0))
        backward = [(target, source) for source, target in forward]
        low = lax.ppermute(
            lax.slice_in_dim(block, block.shape[dim] - width, None, axis=dim), axis, forward
        )
        high = lax.ppermute(lax.slice_in_dim(block, 0, width, axis=dim), axis, backward)
        block = jnp.concatenate([low, block, high], axis=dim)
    return block


def hamiltonian(field, potential):
    width_x = field.shape[1]
    width_y = field.shape[2]
    padded = padded_2(field, (("gx", 1), ("gy", 2)), REACH)
    laplace = 3.0 * COEFFS[0] * field
    for offset in range(1, REACH + 1):
        ahead_x = padded[:, REACH + offset : REACH + offset + width_x, REACH : REACH + width_y]
        behind_x = padded[:, REACH - offset : REACH - offset + width_x, REACH : REACH + width_y]
        ahead_y = padded[:, REACH : REACH + width_x, REACH + offset : REACH + offset + width_y]
        behind_y = padded[:, REACH : REACH + width_x, REACH - offset : REACH - offset + width_y]
        neighbours = ahead_x + behind_x
        neighbours = neighbours + ahead_y + behind_y
        neighbours = neighbours + jnp.roll(field, -offset, 3) + jnp.roll(field, offset, 3)
        laplace = laplace + COEFFS[offset] * neighbours
    return -0.5 * laplace + potential * field


def chebyshev(field, potential):
    middle, first, others = filter_weights(DEGREE)
    current = (hamiltonian(field, potential) - middle * field) * first
    previous = field
    for scale_now, scale_back in others:
        following = (
            hamiltonian(current, potential) - middle * current
        ) * scale_now - scale_back * previous
        previous = current
        current = following
    return current


def invert_factor(margin, identity):
    lower_factor = jnp.linalg.cholesky(margin)
    return jax.scipy.linalg.solve_triangular(lower_factor, identity, lower=True)


def on_device_halo(start_bands, potential):
    filtered = chebyshev(start_bands, potential)
    own_bands = filtered.shape[0]
    flattened = filtered.reshape(own_bands, -1)
    total_cells = flattened.shape[1] * lax.axis_size("gx") * lax.axis_size("gy")
    all_bands = own_bands * lax.axis_size("band")
    identity = jnp.eye(all_bands, dtype=jnp.float32)
    products = jnp.dot(
        flattened,
        lax.all_gather(flattened, "band", axis=0, tiled=True).T,
        precision=lax.Precision.HIGHEST,
        preferred_element_type=jnp.float32,
    )
    first_row = lax.axis_index("band") * own_bands
    summed = lax.psum(products, ("gx", "gy"))
    margin = lax.all_gather(summed, "band", axis=0, tiled=True) * (1.0 / total_cells)
    inverse = invert_factor(margin, identity)
    own_rows = lax.dynamic_slice_in_dim(inverse, first_row, own_bands, 0)
    rotated = jnp.dot(
        own_rows,
        lax.all_gather(flattened, "band", axis=0, tiled=True),
        precision=lax.Precision.HIGHEST,
        preferred_element_type=jnp.float32,
    )
    return rotated.reshape(filtered.shape)


def split3(value):
    high = value.astype(jnp.bfloat16)
    rest = value - high.astype(jnp.float32)
    mid = rest.astype(jnp.bfloat16)
    low = (rest - mid.astype(jnp.float32)).astype(jnp.bfloat16)
    return high, mid, low


def z_weights(nz):
    row = lax.broadcasted_iota(jnp.int32, (nz, nz), 0)
    col = lax.broadcasted_iota(jnp.int32, (nz, nz), 1)
    apart = jnp.abs(row - col)
    apart = jnp.minimum(apart, nz - apart)
    circulant = jnp.zeros((nz, nz), jnp.float32)
    for offset in range(1, REACH + 1):
        circulant = jnp.where(apart == offset, -0.5 * COEFFS[offset], circulant)
    return split3(circulant)


def place(buf, k, x, tile, height, value):
    buf[k, x, pl.ds(tile * TILE, TILE), :] = value
    if tile == 0:
        buf[k, x, pl.ds(height, TILE), :] = value


def along_z(field, w1_ref, w2_ref):
    nz = field.shape[1]
    high, mid, low = split3(field)
    part = jnp.dot(jnp.concatenate([high, mid], 1), w1_ref[...], preferred_element_type=jnp.float32)
    rest = jnp.dot(jnp.concatenate([low, high], 1), w2_ref[...], preferred_element_type=jnp.float32)
    return part[:, :nz] + part[:, nz:] + rest


def along_xy(src, k, height, wanted):
    width = src.shape[1]
    tiles = range(height // TILE)
    window = {}

    def plane(x, t):
        if (x, t) not in window:
            window[x, t] = src[k, x % width, pl.ds(t * TILE, TILE), :]
        return window[x, t]

    for x in range(width):
        rows, pairs = {}, {}

        def shifted(at):
            if at not in rows:
                rows[at] = src[k, x, pl.ds(at, TILE), :]
            return rows[at]

        def pair(*ends):
            ends = tuple(sorted(at % height for at in ends))
            if ends not in pairs:
                pairs[ends] = shifted(ends[0]) + shifted(ends[1])
            return pairs[ends]

        totals = []
        for t in tiles if wanted else ():
            total = None
            for j in range(1, REACH + 1):
                near = plane(x + j, t) + plane(x - j, t)
                near = near + pair(t * TILE + j, t * TILE - j)
                near = (-0.5 * COEFFS[j]) * near
                total = near if total is None else total + near
            totals.append(total)
        yield x, [plane(x, t) for t in tiles], totals


def laplace_kernel(dims, in_ref, field_ref, lap_ref, w1_ref, w2_ref):
    gx, gy, own, nx, ny, nz, pieces, skip = dims
    width, height, cells = gx * nx, gy * ny, nx * ny
    high, mid, low = z_weights(nz)
    for at in (0, nz):
        w1_ref[pl.ds(at, nz), pl.ds(0, nz)] = high
        w1_ref[pl.ds(at, nz), pl.ds(nz, nz)] = mid
    w2_ref[pl.ds(0, nz), :] = high
    w2_ref[pl.ds(nz, nz), :] = low
    for g in range(gx * gy):
        at_x, at_y = (g % gx) * nx, (g // gx) * ny
        for k in range(own):
            for i in range(nx):
                for t in range(ny // TILE):
                    value = in_ref[g, pl.ds(k * cells + i * ny + t * TILE, TILE), :]
                    place(field_ref, k, at_x + i, at_y // TILE + t, height, value)
    field = field_ref[:, :, pl.ds(0, height), :].reshape(own * width * height, nz)
    lap_ref[...] = along_z(field, w1_ref, w2_ref).reshape(own, width, height, nz)
    for k in range(own):
        for x, _, totals in along_xy(field_ref, k, height, True):
            for tile, total in enumerate(totals):
                rows = pl.ds(tile * TILE, TILE)
                lap_ref[k, x, rows, :] = lap_ref[k, x, rows, :] + total


def filter_kernel(dims, field_ref, lap_ref, half_ref, other_ref, w1_ref, w2_ref, out_ref, pot, buf_a, buf_b, zbuf):
    gx, gy, own, nx, ny, nz, pieces, skip = dims
    width, height, cells = gx * nx, gy * ny, nx * ny
    half = cells // 2
    rows = cells // pieces
    middle, first, others = filter_weights(DEGREE)
    shift = -middle - 1.5 * COEFFS[0]

    core = lax.axis_index("core")
    for g in range(gx * gy):
        mine = pl.ds(pl.multiple_of(core * half, TILE), half)
        theirs = pl.ds(pl.multiple_of((1 - core) * half, TILE), half)
        pot[g, mine, :] = half_ref[g, pl.ds(skip, half), :] + shift
        pot[g, theirs, :] = other_ref[g] + shift

    chain = (field_ref, buf_a, buf_b, buf_a)
    steps = [(first, None)] + others
    for step, (scale, back) in enumerate(steps):
        src, dst, old = chain[step], buf_b if step % 2 else buf_a, chain[step - 1]
        last = step == len(steps) - 1
        if step:
            field = src[:, :, pl.ds(0, height), :].reshape(own * width * height, nz)
            zbuf[...] = along_z(field, w1_ref, w2_ref).reshape(own, width, height, nz)
        squares = [jnp.zeros((TILE, nz), jnp.float32) for _ in range(own)]
        for k in range(own):
            for x, centres, totals in along_xy(src, k, height, bool(step)):
                for tile in range(height // TILE):
                    g = (tile * TILE // ny) * gx + x // nx
                    in_pencil = (x % nx) * ny + (tile * TILE) % ny
                    plain = pl.ds(tile * TILE, TILE)
                    if step:
                        total = zbuf[k, x, plain, :] + totals[tile]
                    else:
                        total = lap_ref[k, x, plain, :]
                    total = total + pot[g, pl.ds(in_pencil, TILE), :] * centres[tile]
                    value = scale * total
                    if step:
                        value = value - back * old[k, x, plain, :]
                    if not last:
                        place(dst, k, x, tile, height, value)
                        continue
                    squares[k] = squares[k] + value * value
                    for r in range(0, TILE, TILE // 2):
                        piece, row = divmod(in_pencil + r, rows)
                        to = piece_owner(piece, pieces) * gx * gy + g
                        out_ref[to, pl.ds(k * rows + row, TILE // 2), :] = value[r : r + TILE // 2]
    scales = []
    for k in range(own):
        mean = jnp.sum(squares[k], keepdims=True) * (1.0 / (width * height * nz))
        scales.append(jnp.broadcast_to(lax.rsqrt(mean), (TILE, nz)))
    line = lax.broadcasted_iota(jnp.int32, (TILE, nz), 0)
    for at in range(0, own * rows, TILE):
        factor = scales[at // rows]
        for k in range(at // rows + 1, (at + TILE - 1) // rows + 1):
            factor = jnp.where(line + at < k * rows, factor, scales[k])
        for to in range(out_ref.shape[0]):
            out_ref[to, pl.ds(at, TILE), :] = out_ref[to, pl.ds(at, TILE), :] * factor


def piece_owner(piece, pieces):
    chips = pieces // 2
    return (piece % chips) * 2 + piece // chips


def first_laplace(packed, dims):
    gx, gy, bands, nx, ny, nz, pieces, skip = dims
    width, height = gx * nx, gy * ny
    vmem = pl.BlockSpec(memory_space=pltpu.VMEM)
    cells = bands * width * height * nz
    return pl.pallas_call(
        functools.partial(laplace_kernel, dims),
        out_shape=(
            jax.ShapeDtypeStruct((bands, width, height + TILE, nz), jnp.float32),
            jax.ShapeDtypeStruct((bands, width, height, nz), jnp.float32),
            jax.ShapeDtypeStruct((2 * nz, 2 * nz), jnp.bfloat16),
            jax.ShapeDtypeStruct((2 * nz, nz), jnp.bfloat16),
        ),
        in_specs=[vmem],
        out_specs=(vmem,) * 4,
        compiler_params=pltpu.CompilerParams(vmem_limit_bytes=12 * 1024 * 1024),
        cost_estimate=pl.CostEstimate(flops=44 * cells, bytes_accessed=16 * cells, transcendentals=0),
        name="laplace",
    )(packed)


def apply_filter(field, laplace, packed, other, weights, dims):
    gx, gy, bands, nx, ny, nz, pieces, skip = dims
    vmem = pl.BlockSpec(memory_space=pltpu.VMEM)
    return pl.pallas_call(
        functools.partial(filter_kernel, dims),
        out_shape=jax.ShapeDtypeStruct((pieces * gx * gy, bands * nx * ny // pieces, nz), jnp.float32),
        in_specs=[vmem] * 6,
        out_specs=vmem,
        scratch_shapes=[
            pltpu.VMEM((gx * gy, nx * ny, nz), jnp.float32),
            pltpu.VMEM(field.shape, jnp.float32),
            pltpu.VMEM(field.shape, jnp.float32),
            pltpu.VMEM(laplace.shape, jnp.float32),
        ],
        compiler_params=pltpu.CompilerParams(vmem_limit_bytes=12 * 1024 * 1024),
        name="filter",
    )(field, laplace, packed, other, *weights)


def margin_kernel(rows, bands, scale, grid, x_ref, out_ref):
    highs, mids, lows = [], [], []
    for r in range(rows):
        high, mid, low = split3(x_ref[pl.ds(r, bands, stride=rows), :])
        highs.append(high)
        mids.append(mid)
        lows.append(low)
    terms = [jnp.concatenate(term, 1) for term in (highs, mids, lows)]
    stacked = jnp.concatenate(terms, 0)
    products = lax.dot_general(stacked, stacked, (((1,), (1,)), ((), ())), preferred_element_type=jnp.float32)

    def block(i, j):
        return products[i * bands : (i + 1) * bands, j * bands : (j + 1) * bands]

    small = block(0, 2) + block(2, 0) + block(1, 1)
    total = (small + (block(0, 1) + block(1, 0)) + block(0, 0)) * scale
    half = bands // 2
    row = lax.broadcasted_iota(jnp.int32, (half, half), 0)
    col = lax.broadcasted_iota(jnp.int32, (half, half), 1)
    strict = jnp.where(row > col, total[:half, :half], total[half:, half:])
    for core, part in enumerate((total[half:, :half], strict)):
        folded = jnp.concatenate([part[at : at + TILE] for at in range(0, half, TILE)], 1)
        for to in range(out_ref.shape[0]):
            if to // grid % 2 == core:
                out_ref[to] = folded


def partial_margin(blocks, bands, scale, pieces, grid):
    rows = blocks.shape[0] // bands
    return pl.pallas_call(
        functools.partial(margin_kernel, rows, bands, scale, grid),
        out_shape=jax.ShapeDtypeStruct((pieces * grid, TILE, (bands // 2) ** 2 // TILE), jnp.float32),
        in_specs=[pl.BlockSpec(memory_space=pltpu.VMEM)],
        out_specs=pl.BlockSpec(memory_space=pltpu.VMEM),
        compiler_params=pltpu.CompilerParams(vmem_limit_bytes=8 * 1024 * 1024),
        name="margin",
    )(blocks)


def sum_kernel(in_ref, out_ref):
    total = in_ref[0]
    for term in range(1, in_ref.shape[0]):
        total = total + in_ref[term]
    out_ref[...] = total


def sum_first(value):
    return pl.pallas_call(
        sum_kernel,
        out_shape=jax.ShapeDtypeStruct(value.shape[1:], value.dtype),
        in_specs=[pl.BlockSpec(memory_space=pltpu.VMEM)],
        out_specs=pl.BlockSpec(memory_space=pltpu.VMEM),
        compiler_params=pltpu.CompilerParams(vmem_limit_bytes=4 * 1024 * 1024),
        name="sum",
    )(value)


def eliminate(margin):
    bands = margin.shape[0]
    tiles = bands // TILE
    margin = jnp.concatenate([margin, margin], 1)
    width = 2 * bands
    lines = lax.broadcasted_iota(jnp.int32, (TILE, width), 0)
    lanes = lax.broadcasted_iota(jnp.int32, (TILE, width), 1)
    both = []
    for t in range(tiles):
        right = margin[t * TILE : (t + 1) * TILE]
        eye = jnp.where(lines + t * TILE == lanes % bands, 1.0, 0.0)
        both.append([eye, jnp.where(lanes < bands, eye, right)])

    def spread(t, at):
        return jnp.broadcast_to(both[t][1][:, bands + at : bands + at + 1], (TILE, width))

    def line_of(value, at):
        return jnp.broadcast_to(value[at : at + 1, :], (TILE, width))

    heads = [spread(0, c) for c in range(TILE)]
    for p in range(tiles):
        here = range(p * TILE, (p + 1) * TILE)
        panel = [{t: spread(t, at) for t in range(p + 1, tiles)} for at in here]
        later = [spread(p + 1, at + TILE) for at in here] if p + 1 < tiles else []
        square = [[line_of(heads[c], d) if d >= c else None for d in range(TILE)] for c in range(TILE)]
        pivots = None
        for j in range(TILE):
            pivot = square[j][j]
            pivots = pivot if j == 0 else jnp.where(lines == j, pivot, pivots)
            ratio = pl.reciprocal(pivot, approx=True)
            for c in range(j + 1, TILE):
                for d in range(c, TILE):
                    square[c][d] = square[c][d] - (square[j][c] * square[j][d]) * ratio
            factor = {t: panel[j][t] * ratio for t in range(p + 1, tiles)}
            factor[p] = jnp.where(lines > j, heads[j] * ratio, 0.0)
            for c in range(j + 1, TILE):
                heads[c] = heads[c] - factor[p] * square[j][c]
                for t in range(p + 1, tiles):
                    panel[c][t] = panel[c][t] - factor[t] * square[j][c]
            for c, column in enumerate(later):
                later[c] = column - factor[p + 1] * line_of(panel[j][p + 1], c)
            pair = [line_of(value, j) for value in both[p]]
            for t in range(p, tiles):
                both[t] = [value - factor[t] * line for value, line in zip(both[t], pair)]
        heads = later
        scale = lax.rsqrt(pivots)
        both[p] = [value * scale for value in both[p]]
    return [jnp.concatenate(value, 1) for value in both]


def split_pair(split_ref, at, part, pair, bands):
    rows = part.shape[0] // bands
    nz = part.shape[1]
    for i in range(2):
        terms = split3(part[pl.ds(2 * pair + i, bands, stride=rows), :])
        for j, term in enumerate(terms):
            split_ref[at, pl.ds(j * bands, bands), pl.ds(i * nz, nz)] = term


def inverse_kernel(dims, *refs):
    bands, own = dims
    own_ref, other_ref, left_ref, inv_ref = refs
    half = bands // 2
    here, there = own_ref[...], other_ref[...]
    first = lax.axis_index("core") == 0
    cross, strict = [
        jnp.concatenate([value[:, at : at + half] for at in range(0, half * half // TILE, half)], 0)
        for value in (jnp.where(first, here, there), jnp.where(first, there, here))
    ]
    row = lax.broadcasted_iota(jnp.int32, (half, half), 0)
    col = lax.broadcasted_iota(jnp.int32, (half, half), 1)
    turned = strict.T
    low = jnp.where(row == col, 1.0, jnp.where(row > col, strict, turned))
    high = jnp.where(row == col, 1.0, jnp.where(row < col, strict, turned))
    margin = jnp.concatenate(
        [jnp.concatenate([low, cross.T], 1), jnp.concatenate([cross, high], 1)], 0
    )
    for t, value in enumerate(eliminate(margin)):
        inv_ref[pl.ds(t * TILE, TILE), :] = value
    first = pl.multiple_of((lax.axis_index("chip") * 2 + lax.axis_index("core")) * own, TILE)
    rows = inv_ref[pl.ds(first, own), pl.ds(0, 3 * bands)]
    lanes = lax.broadcasted_iota(jnp.int32, rows.shape, 1)
    high = rows.astype(jnp.bfloat16)
    rest = rows - high.astype(jnp.float32)
    mid = rest.astype(jnp.bfloat16)
    low = rest - mid.astype(jnp.float32)
    left_ref[pl.ds(0, own), :] = high
    left_ref[pl.ds(own, own), :] = jnp.where(lanes < 2 * bands, rest, 0.0).astype(jnp.bfloat16)
    left_ref[pl.ds(2 * own, own), :] = jnp.where(lanes < bands, low, 0.0).astype(jnp.bfloat16)


def inverse_rows(margins, own, bands):
    vmem = pl.BlockSpec(memory_space=pltpu.VMEM)
    return pl.pallas_call(
        functools.partial(inverse_kernel, (bands, own)),
        out_shape=jax.ShapeDtypeStruct((3 * own, 3 * bands), jnp.bfloat16),
        in_specs=[vmem] * len(margins),
        out_specs=vmem,
        scratch_shapes=[pltpu.VMEM((bands, 4 * bands), jnp.float32)],
        compiler_params=pltpu.CompilerParams(vmem_limit_bytes=4 * 1024 * 1024),
        name="inverse",
    )(*margins)


def rotate_kernel(dims, left_ref, *refs):
    bands, own = dims
    parts, out_ref = refs[:-1], refs[-1]
    rows = parts[0].shape[0] // bands
    nz = parts[0].shape[1]
    left = left_ref[...]
    chips = len(parts) // 2
    chip, core = lax.axis_index("chip"), lax.axis_index("core")
    for index, part in enumerate(parts):
        piece = (core ^ (index // chips)) * chips + (chip ^ (index % chips))
        for r in range(0, rows, 2):
            terms = [split3(part[pl.ds(r + i, bands, stride=rows), :]) for i in range(2)]
            block = jnp.concatenate([jnp.concatenate(term, 1) for term in zip(*terms)], 0)
            product = jnp.dot(left, block, preferred_element_type=jnp.float32)
            value = product[:own] + (product[own : 2 * own] + product[2 * own :])
            for i in range(2):
                start = piece * rows + r + i
                out_ref[pl.ds(start, own, stride=rows * len(parts)), :] = value[:, i * nz : (i + 1) * nz]


def rotate(left, parts, bands):
    rows = parts[0].shape[0] // bands
    own = left.shape[0] // 3
    nz = parts[0].shape[1]
    vmem = pl.BlockSpec(memory_space=pltpu.VMEM)
    return pl.pallas_call(
        functools.partial(rotate_kernel, (bands, own)),
        out_shape=jax.ShapeDtypeStruct((own * rows * len(parts), nz), jnp.float32),
        in_specs=[vmem] * (1 + len(parts)),
        out_specs=vmem,
        compiler_params=pltpu.CompilerParams(vmem_limit_bytes=6 * 1024 * 1024),
        name="rotate",
    )(left, *parts)


def on_device_fields(start_bands, potential):
    own_bands, nx, ny, nz = start_bands.shape
    gx, gy, chips = lax.axis_size("gx"), lax.axis_size("gy"), lax.axis_size("chip")
    pieces = 2 * chips
    grid = gx * gy
    own = own_bands // grid
    cells = nx * ny
    bands = own_bands * pieces
    rows = cells // pieces
    core = lax.axis_index("core")
    swap = [(0, 1), (1, 0)]

    fields = start_bands.reshape(grid, own * cells, nz)
    flat_potential = potential.reshape(cells, nz)
    half = cells // 2
    own_half = lax.dynamic_slice_in_dim(flat_potential, core * half, half, 0)
    packed = lax.optimization_barrier(jnp.pad(fields, ((0, 0), (0, half), (0, 0))))
    packed = packed.at[:, own * cells :, :].set(own_half[None])
    packed = lax.all_to_all(packed, ("gy", "gx"), 0, 0)
    other = lax.ppermute(packed[:, own * cells :, :], "core", swap)
    dims = (gx, gy, own, nx, ny, nz, pieces, own * cells)
    field, laplace, *weights = first_laplace(packed, dims)
    filtered = apply_filter(field, laplace, packed, other, weights, dims)
    blocks = lax.all_to_all(filtered, ("chip", "core", "gy", "gx"), 0, 0).reshape(bands * rows, nz)

    def tied(value, first):
        return lax.optimization_barrier((value, first))[0]

    def copies(value, *axes):
        count = math.prod(lax.axis_size(axis) for axis in axes)
        pairs = [[(i, i ^ mask) for i in range(count)] for mask in range(1, count)]
        return [value] + [lax.ppermute(value, axes, pair) for pair in pairs]

    spread = partial_margin(blocks, bands, 1.0 / (cells * nz * grid), pieces, grid)
    parts = copies(blocks, "chip")
    margins = lax.all_to_all(spread, ("chip", "core", "gx", "gy"), 0, 0)
    margins = copies(sum_first(margins), "core")
    crossed = [lax.ppermute(tied(blocks, margins[0]), "core", swap)]
    far, margins = lax.optimization_barrier((parts[1:], margins))
    parts += crossed + [lax.ppermute(part, "core", swap) for part in far]
    left = inverse_rows(margins, own_bands, bands)
    rotated = rotate(left, parts, bands)
    return rotated.reshape(start_bands.shape)


def power_of_two(count):
    return count & (count - 1) == 0


def whole_fields(mesh, shape):
    gx, gy, pieces = mesh.shape["gx"], mesh.shape["gy"], mesh.shape["band"]
    bands, nx, ny, nz = shape[0], shape[1] // gx, shape[2] // gy, shape[3]
    own_bands, cells = bands // pieces, nx * ny
    return (
        own_bands % (gx * gy) == 0
        and own_bands % (2 * TILE) == 0
        and pieces % 2 == 0
        and power_of_two(pieces)
        and ny % TILE == 0
        and nz % 128 == 0
        and bands % 64 == 0
        and cells % (2 * TILE) == 0
        and cells % (pieces * TILE // 2) == 0
        and pieces > 2
        and (own_bands // (gx * gy)) * (cells // pieces) % TILE == 0
        and shape[1] > 2 * REACH
    )


def solution(mesh):
    def step(start_bands, potential):
        if whole_fields(mesh, start_bands.shape):
            chips = mesh.shape["band"] // 2
            rest = mesh.devices.shape[1:]
            split = Mesh(mesh.devices.reshape((chips, 2) + rest), ("chip", "core") + mesh.axis_names[1:])
            program, band = on_device_fields, ("chip", "core")
        else:
            split, program, band = mesh, on_device_halo, "band"
        return jax.shard_map(
            program,
            mesh=split,
            in_specs=(P(band, "gx", "gy", None), P("gx", "gy", None)),
            out_specs=P(band, "gx", "gy", None),
            check_vma=False,
        )(start_bands, potential)

    return step
```

```python
import functools
import math

import jax
import jax.numpy as jnp
from jax import lax
from jax.experimental import pallas as pl
from jax.experimental.pallas import tpu as pltpu
from jax.sharding import Mesh, PartitionSpec as P

DEGREE = 4


COEFFS = (
    -5369.0 / 1800.0,
    12.0 / 7.0,
    -15.0 / 56.0,
    10.0 / 189.0,
    -1.0 / 112.0,
    2.0 / 1925.0,
    -1.0 / 16632.0,
)
REACH = len(COEFFS) - 1
LOWER_END = -0.5
CUT_LOW = 3.0
CUT_HIGH = 12.7
TILE = 8


def filter_weights(degree):
    half_width = (CUT_HIGH - CUT_LOW) / 2.0
    middle = (CUT_HIGH + CUT_LOW) / 2.0
    sigma = half_width / (LOWER_END - middle)
    tau = 2.0 / sigma
    first = sigma / half_width
    others = []
    for index in range(degree - 1):
        sigma_new = 1.0 / (tau - sigma)
        others.append((2.0 * sigma_new / half_width, sigma * sigma_new))
        sigma = sigma_new
    return (middle, first, others)


def padded_2(block, sides, width):
    for axis, dim in sides:
        count = lax.axis_size(axis)
        forward = [(i, i + 1) for i in range(count - 1)]
        forward.append((count - 1, 0))
        backward = [(target, source) for source, target in forward]
        low = lax.ppermute(
            lax.slice_in_dim(block, block.shape[dim] - width, None, axis=dim), axis, forward
        )
        high = lax.ppermute(lax.slice_in_dim(block, 0, width, axis=dim), axis, backward)
        block = jnp.concatenate([low, block, high], axis=dim)
    return block


def hamiltonian(field, potential):
    width_x = field.shape[1]
    width_y = field.shape[2]
    padded = padded_2(field, (("gx", 1), ("gy", 2)), REACH)
    laplace = 3.0 * COEFFS[0] * field
    for offset in range(1, REACH + 1):
        ahead_x = padded[:, REACH + offset : REACH + offset + width_x, REACH : REACH + width_y]
        behind_x = padded[:, REACH - offset : REACH - offset + width_x, REACH : REACH + width_y]
        ahead_y = padded[:, REACH : REACH + width_x, REACH + offset : REACH + offset + width_y]
        behind_y = padded[:, REACH : REACH + width_x, REACH - offset : REACH - offset + width_y]
        neighbours = ahead_x + behind_x
        neighbours = neighbours + ahead_y + behind_y
        neighbours = neighbours + jnp.roll(field, -offset, 3) + jnp.roll(field, offset, 3)
        laplace = laplace + COEFFS[offset] * neighbours
    return -0.5 * laplace + potential * field


def chebyshev(field, potential):
    middle, first, others = filter_weights(DEGREE)
    current = (hamiltonian(field, potential) - middle * field) * first
    previous = field
    for scale_now, scale_back in others:
        following = (
            hamiltonian(current, potential) - middle * current
        ) * scale_now - scale_back * previous
        previous = current
        current = following
    return current


def invert_factor(margin, identity):
    lower_factor = jnp.linalg.cholesky(margin)
    return jax.scipy.linalg.solve_triangular(lower_factor, identity, lower=True)


def on_device_halo(start_bands, potential):
    filtered = chebyshev(start_bands, potential)
    own_bands = filtered.shape[0]
    flattened = filtered.reshape(own_bands, -1)
    total_cells = flattened.shape[1] * lax.axis_size("gx") * lax.axis_size("gy")
    all_bands = own_bands * lax.axis_size("band")
    identity = jnp.eye(all_bands, dtype=jnp.float32)
    products = jnp.dot(
        flattened,
        lax.all_gather(flattened, "band", axis=0, tiled=True).T,
        precision=lax.Precision.HIGHEST,
        preferred_element_type=jnp.float32,
    )
    first_row = lax.axis_index("band") * own_bands
    summed = lax.psum(products, ("gx", "gy"))
    margin = lax.all_gather(summed, "band", axis=0, tiled=True) * (1.0 / total_cells)
    inverse = invert_factor(margin, identity)
    own_rows = lax.dynamic_slice_in_dim(inverse, first_row, own_bands, 0)
    rotated = jnp.dot(
        own_rows,
        lax.all_gather(flattened, "band", axis=0, tiled=True),
        precision=lax.Precision.HIGHEST,
        preferred_element_type=jnp.float32,
    )
    return rotated.reshape(filtered.shape)


def split3(value):
    high = value.astype(jnp.bfloat16)
    rest = value - high.astype(jnp.float32)
    mid = rest.astype(jnp.bfloat16)
    low = (rest - mid.astype(jnp.float32)).astype(jnp.bfloat16)
    return high, mid, low


def z_weights(nz):
    row = lax.broadcasted_iota(jnp.int32, (nz, nz), 0)
    col = lax.broadcasted_iota(jnp.int32, (nz, nz), 1)
    apart = jnp.abs(row - col)
    apart = jnp.minimum(apart, nz - apart)
    circulant = jnp.zeros((nz, nz), jnp.float32)
    for offset in range(1, REACH + 1):
        circulant = jnp.where(apart == offset, -0.5 * COEFFS[offset], circulant)
    return split3(circulant)


def place(buf, k, x, tile, height, value):
    buf[k, x, pl.ds(tile * TILE, TILE), :] = value
    if tile == 0:
        buf[k, x, pl.ds(height, TILE), :] = value


def along_z(field, w1_ref, w2_ref):
    nz = field.shape[1]
    high, mid, low = split3(field)
    part = jnp.dot(jnp.concatenate([high, mid], 1), w1_ref[...], preferred_element_type=jnp.float32)
    rest = jnp.dot(jnp.concatenate([low, high], 1), w2_ref[...], preferred_element_type=jnp.float32)
    return part[:, :nz] + part[:, nz:] + rest


def along_xy(src, k, height, wanted):
    width = src.shape[1]
    tiles = range(height // TILE)
    window = {}

    def plane(x, t):
        if (x, t) not in window:
            window[x, t] = src[k, x % width, pl.ds(t * TILE, TILE), :]
        return window[x, t]

    for x in range(width):
        rows, pairs = {}, {}

        def shifted(at):
            if at not in rows:
                rows[at] = src[k, x, pl.ds(at, TILE), :]
            return rows[at]

        def pair(*ends):
            ends = tuple(sorted(at % height for at in ends))
            if ends not in pairs:
                pairs[ends] = shifted(ends[0]) + shifted(ends[1])
            return pairs[ends]

        totals = []
        for t in tiles if wanted else ():
            total = None
            for j in range(1, REACH + 1):
                near = plane(x + j, t) + plane(x - j, t)
                near = near + pair(t * TILE + j, t * TILE - j)
                near = (-0.5 * COEFFS[j]) * near
                total = near if total is None else total + near
            totals.append(total)
        yield x, [plane(x, t) for t in tiles], totals


def laplace_kernel(dims, in_ref, field_ref, lap_ref, w1_ref, w2_ref):
    gx, gy, own, nx, ny, nz, pieces, skip = dims
    width, height, cells = gx * nx, gy * ny, nx * ny
    high, mid, low = z_weights(nz)
    for at in (0, nz):
        w1_ref[pl.ds(at, nz), pl.ds(0, nz)] = high
        w1_ref[pl.ds(at, nz), pl.ds(nz, nz)] = mid
    w2_ref[pl.ds(0, nz), :] = high
    w2_ref[pl.ds(nz, nz), :] = low
    for g in range(gx * gy):
        at_x, at_y = (g % gx) * nx, (g // gx) * ny
        for k in range(own):
            for i in range(nx):
                for t in range(ny // TILE):
                    value = in_ref[g, pl.ds(k * cells + i * ny + t * TILE, TILE), :]
                    place(field_ref, k, at_x + i, at_y // TILE + t, height, value)
    field = field_ref[:, :, pl.ds(0, height), :].reshape(own * width * height, nz)
    lap_ref[...] = along_z(field, w1_ref, w2_ref).reshape(own, width, height, nz)
    for k in range(own):
        for x, _, totals in along_xy(field_ref, k, height, True):
            for tile, total in enumerate(totals):
                rows = pl.ds(tile * TILE, TILE)
                lap_ref[k, x, rows, :] = lap_ref[k, x, rows, :] + total


def filter_kernel(dims, field_ref, lap_ref, half_ref, other_ref, w1_ref, w2_ref, out_ref, pot, buf_a, buf_b, zbuf):
    gx, gy, own, nx, ny, nz, pieces, skip = dims
    width, height, cells = gx * nx, gy * ny, nx * ny
    half = cells // 2
    rows = cells // pieces
    middle, first, others = filter_weights(DEGREE)
    shift = -middle - 1.5 * COEFFS[0]

    core = lax.axis_index("core")
    for g in range(gx * gy):
        mine = pl.ds(pl.multiple_of(core * half, TILE), half)
        theirs = pl.ds(pl.multiple_of((1 - core) * half, TILE), half)
        pot[g, mine, :] = half_ref[g, pl.ds(skip, half), :] + shift
        pot[g, theirs, :] = other_ref[g] + shift

    chain = (field_ref, buf_a, buf_b, buf_a)
    steps = [(first, None)] + others
    for step, (scale, back) in enumerate(steps):
        src, dst, old = chain[step], buf_b if step % 2 else buf_a, chain[step - 1]
        last = step == len(steps) - 1
        if step:
            field = src[:, :, pl.ds(0, height), :].reshape(own * width * height, nz)
            zbuf[...] = along_z(field, w1_ref, w2_ref).reshape(own, width, height, nz)
        squares = [jnp.zeros((TILE, nz), jnp.float32) for _ in range(own)]
        for k in range(own):
            for x, centres, totals in along_xy(src, k, height, bool(step)):
                for tile in range(height // TILE):
                    g = (tile * TILE // ny) * gx + x // nx
                    in_pencil = (x % nx) * ny + (tile * TILE) % ny
                    plain = pl.ds(tile * TILE, TILE)
                    if step:
                        total = zbuf[k, x, plain, :] + totals[tile]
                    else:
                        total = lap_ref[k, x, plain, :]
                    total = total + pot[g, pl.ds(in_pencil, TILE), :] * centres[tile]
                    value = scale * total
                    if step:
                        value = value - back * old[k, x, plain, :]
                    if not last:
                        place(dst, k, x, tile, height, value)
                        continue
                    squares[k] = squares[k] + value * value
                    for r in range(0, TILE, TILE // 2):
                        piece, row = divmod(in_pencil + r, rows)
                        to = piece_owner(piece, pieces) * gx * gy + g
                        out_ref[to, pl.ds(k * rows + row, TILE // 2), :] = value[r : r + TILE // 2]
    scales = []
    for k in range(own):
        mean = jnp.sum(squares[k], keepdims=True) * (1.0 / (width * height * nz))
        scales.append(jnp.broadcast_to(lax.rsqrt(mean), (TILE, nz)))
    line = lax.broadcasted_iota(jnp.int32, (TILE, nz), 0)
    for at in range(0, own * rows, TILE):
        factor = scales[at // rows]
        for k in range(at // rows + 1, (at + TILE - 1) // rows + 1):
            factor = jnp.where(line + at < k * rows, factor, scales[k])
        for to in range(out_ref.shape[0]):
            out_ref[to, pl.ds(at, TILE), :] = out_ref[to, pl.ds(at, TILE), :] * factor


def piece_owner(piece, pieces):
    chips = pieces // 2
    return (piece % chips) * 2 + piece // chips


def first_laplace(packed, dims):
    gx, gy, bands, nx, ny, nz, pieces, skip = dims
    width, height = gx * nx, gy * ny
    vmem = pl.BlockSpec(memory_space=pltpu.VMEM)
    cells = bands * width * height * nz
    return pl.pallas_call(
        functools.partial(laplace_kernel, dims),
        out_shape=(
            jax.ShapeDtypeStruct((bands, width, height + TILE, nz), jnp.float32),
            jax.ShapeDtypeStruct((bands, width, height, nz), jnp.float32),
            jax.ShapeDtypeStruct((2 * nz, 2 * nz), jnp.bfloat16),
            jax.ShapeDtypeStruct((2 * nz, nz), jnp.bfloat16),
        ),
        in_specs=[vmem],
        out_specs=(vmem,) * 4,
        compiler_params=pltpu.CompilerParams(vmem_limit_bytes=12 * 1024 * 1024),
        cost_estimate=pl.CostEstimate(flops=44 * cells, bytes_accessed=16 * cells, transcendentals=0),
        name="laplace",
    )(packed)


def apply_filter(field, laplace, packed, other, weights, dims):
    gx, gy, bands, nx, ny, nz, pieces, skip = dims
    vmem = pl.BlockSpec(memory_space=pltpu.VMEM)
    return pl.pallas_call(
        functools.partial(filter_kernel, dims),
        out_shape=jax.ShapeDtypeStruct((pieces * gx * gy, bands * nx * ny // pieces, nz), jnp.float32),
        in_specs=[vmem] * 6,
        out_specs=vmem,
        scratch_shapes=[
            pltpu.VMEM((gx * gy, nx * ny, nz), jnp.float32),
            pltpu.VMEM(field.shape, jnp.float32),
            pltpu.VMEM(field.shape, jnp.float32),
            pltpu.VMEM(laplace.shape, jnp.float32),
        ],
        compiler_params=pltpu.CompilerParams(vmem_limit_bytes=12 * 1024 * 1024),
        name="filter",
    )(field, laplace, packed, other, *weights)


def margin_kernel(rows, bands, scale, grid, x_ref, out_ref):
    highs, mids, lows = [], [], []
    for r in range(rows):
        high, mid, low = split3(x_ref[pl.ds(r, bands, stride=rows), :])
        highs.append(high)
        mids.append(mid)
        lows.append(low)
    terms = [jnp.concatenate(term, 1) for term in (highs, mids, lows)]
    stacked = jnp.concatenate(terms, 0)
    products = lax.dot_general(stacked, stacked, (((1,), (1,)), ((), ())), preferred_element_type=jnp.float32)

    def block(i, j):
        return products[i * bands : (i + 1) * bands, j * bands : (j + 1) * bands]

    small = block(0, 2) + block(2, 0) + block(1, 1)
    total = (small + (block(0, 1) + block(1, 0)) + block(0, 0)) * scale
    half = bands // 2
    row = lax.broadcasted_iota(jnp.int32, (half, half), 0)
    col = lax.broadcasted_iota(jnp.int32, (half, half), 1)
    strict = jnp.where(row > col, total[:half, :half], total[half:, half:])
    for core, part in enumerate((total[half:, :half], strict)):
        folded = jnp.concatenate([part[at : at + TILE] for at in range(0, half, TILE)], 1)
        for to in range(out_ref.shape[0]):
            if to // grid % 2 == core:
                out_ref[to] = folded


def partial_margin(blocks, bands, scale, pieces, grid):
    rows = blocks.shape[0] // bands
    return pl.pallas_call(
        functools.partial(margin_kernel, rows, bands, scale, grid),
        out_shape=jax.ShapeDtypeStruct((pieces * grid, TILE, (bands // 2) ** 2 // TILE), jnp.float32),
        in_specs=[pl.BlockSpec(memory_space=pltpu.VMEM)],
        out_specs=pl.BlockSpec(memory_space=pltpu.VMEM),
        compiler_params=pltpu.CompilerParams(vmem_limit_bytes=8 * 1024 * 1024),
        name="margin",
    )(blocks)


def sum_kernel(in_ref, out_ref):
    total = in_ref[0]
    for term in range(1, in_ref.shape[0]):
        total = total + in_ref[term]
    out_ref[...] = total


def sum_first(value):
    return pl.pallas_call(
        sum_kernel,
        out_shape=jax.ShapeDtypeStruct(value.shape[1:], value.dtype),
        in_specs=[pl.BlockSpec(memory_space=pltpu.VMEM)],
        out_specs=pl.BlockSpec(memory_space=pltpu.VMEM),
        compiler_params=pltpu.CompilerParams(vmem_limit_bytes=4 * 1024 * 1024),
        name="sum",
    )(value)


def eliminate(margin):
    bands = margin.shape[0]
    tiles = bands // TILE
    margin = jnp.concatenate([margin, margin], 1)
    width = 2 * bands
    lines = lax.broadcasted_iota(jnp.int32, (TILE, width), 0)
    lanes = lax.broadcasted_iota(jnp.int32, (TILE, width), 1)
    both = []
    for t in range(tiles):
        right = margin[t * TILE : (t + 1) * TILE]
        eye = jnp.where(lines + t * TILE == lanes % bands, 1.0, 0.0)
        both.append([eye, jnp.where(lanes < bands, eye, right)])

    def spread(t, at):
        return jnp.broadcast_to(both[t][1][:, bands + at : bands + at + 1], (TILE, width))

    def line_of(value, at):
        return jnp.broadcast_to(value[at : at + 1, :], (TILE, width))

    heads = [spread(0, c) for c in range(TILE)]
    for p in range(tiles):
        here = range(p * TILE, (p + 1) * TILE)
        panel = [{t: spread(t, at) for t in range(p + 1, tiles)} for at in here]
        later = [spread(p + 1, at + TILE) for at in here] if p + 1 < tiles else []
        square = [[line_of(heads[c], d) if d >= c else None for d in range(TILE)] for c in range(TILE)]
        pivots = None
        for j in range(TILE):
            pivot = square[j][j]
            pivots = pivot if j == 0 else jnp.where(lines == j, pivot, pivots)
            ratio = pl.reciprocal(pivot, approx=True)
            for c in range(j + 1, TILE):
                scaled = square[j][c] * ratio
                for d in range(c, TILE):
                    square[c][d] = square[c][d] - scaled * square[j][d]
            factor = {t: panel[j][t] * ratio for t in range(p + 1, tiles)}
            factor[p] = jnp.where(lines > j, heads[j] * ratio, 0.0)
            for c in range(j + 1, TILE):
                heads[c] = heads[c] - factor[p] * square[j][c]
                for t in range(p + 1, tiles):
                    panel[c][t] = panel[c][t] - factor[t] * square[j][c]
            for c, column in enumerate(later):
                later[c] = column - factor[p + 1] * line_of(panel[j][p + 1], c)
            pair = [line_of(value, j) for value in both[p]]
            for t in range(p, tiles):
                both[t] = [value - factor[t] * line for value, line in zip(both[t], pair)]
        heads = later
        scale = lax.rsqrt(pivots)
        both[p] = [value * scale for value in both[p]]
    return [jnp.concatenate(value, 1) for value in both]


def split_pair(split_ref, at, part, pair, bands):
    rows = part.shape[0] // bands
    nz = part.shape[1]
    for i in range(2):
        terms = split3(part[pl.ds(2 * pair + i, bands, stride=rows), :])
        for j, term in enumerate(terms):
            split_ref[at, pl.ds(j * bands, bands), pl.ds(i * nz, nz)] = term


def inverse_kernel(dims, *refs):
    bands, own = dims
    own_ref, other_ref, left_ref, inv_ref = refs
    half = bands // 2
    here, there = own_ref[...], other_ref[...]
    first = lax.axis_index("core") == 0
    cross, strict = [
        jnp.concatenate([value[:, at : at + half] for at in range(0, half * half // TILE, half)], 0)
        for value in (jnp.where(first, here, there), jnp.where(first, there, here))
    ]
    row = lax.broadcasted_iota(jnp.int32, (half, half), 0)
    col = lax.broadcasted_iota(jnp.int32, (half, half), 1)
    turned = strict.T
    low = jnp.where(row == col, 1.0, jnp.where(row > col, strict, turned))
    high = jnp.where(row == col, 1.0, jnp.where(row < col, strict, turned))
    margin = jnp.concatenate(
        [jnp.concatenate([low, cross.T], 1), jnp.concatenate([cross, high], 1)], 0
    )
    for t, value in enumerate(eliminate(margin)):
        inv_ref[pl.ds(t * TILE, TILE), :] = value
    first = pl.multiple_of((lax.axis_index("chip") * 2 + lax.axis_index("core")) * own, TILE)
    rows = inv_ref[pl.ds(first, own), pl.ds(0, 3 * bands)]
    lanes = lax.broadcasted_iota(jnp.int32, rows.shape, 1)
    high = rows.astype(jnp.bfloat16)
    rest = rows - high.astype(jnp.float32)
    mid = rest.astype(jnp.bfloat16)
    low = rest - mid.astype(jnp.float32)
    left_ref[pl.ds(0, own), :] = high
    left_ref[pl.ds(own, own), :] = jnp.where(lanes < 2 * bands, rest, 0.0).astype(jnp.bfloat16)
    left_ref[pl.ds(2 * own, own), :] = jnp.where(lanes < bands, low, 0.0).astype(jnp.bfloat16)


def inverse_rows(margins, own, bands):
    vmem = pl.BlockSpec(memory_space=pltpu.VMEM)
    return pl.pallas_call(
        functools.partial(inverse_kernel, (bands, own)),
        out_shape=jax.ShapeDtypeStruct((3 * own, 3 * bands), jnp.bfloat16),
        in_specs=[vmem] * len(margins),
        out_specs=vmem,
        scratch_shapes=[pltpu.VMEM((bands, 4 * bands), jnp.float32)],
        compiler_params=pltpu.CompilerParams(vmem_limit_bytes=4 * 1024 * 1024),
        name="inverse",
    )(*margins)


def rotate_kernel(dims, left_ref, *refs):
    bands, own = dims
    parts, out_ref = refs[:-1], refs[-1]
    rows = parts[0].shape[0] // bands
    nz = parts[0].shape[1]
    left = left_ref[...]
    chips = len(parts) // 2
    chip, core = lax.axis_index("chip"), lax.axis_index("core")
    for index, part in enumerate(parts):
        piece = (core ^ (index // chips)) * chips + (chip ^ (index % chips))
        for r in range(0, rows, 2):
            terms = [split3(part[pl.ds(r + i, bands, stride=rows), :]) for i in range(2)]
            block = jnp.concatenate([jnp.concatenate(term, 1) for term in zip(*terms)], 0)
            product = jnp.dot(left, block, preferred_element_type=jnp.float32)
            value = product[:own] + (product[own : 2 * own] + product[2 * own :])
            for i in range(2):
                start = piece * rows + r + i
                out_ref[pl.ds(start, own, stride=rows * len(parts)), :] = value[:, i * nz : (i + 1) * nz]


def rotate(left, parts, bands):
    rows = parts[0].shape[0] // bands
    own = left.shape[0] // 3
    nz = parts[0].shape[1]
    vmem = pl.BlockSpec(memory_space=pltpu.VMEM)
    return pl.pallas_call(
        functools.partial(rotate_kernel, (bands, own)),
        out_shape=jax.ShapeDtypeStruct((own * rows * len(parts), nz), jnp.float32),
        in_specs=[vmem] * (1 + len(parts)),
        out_specs=vmem,
        compiler_params=pltpu.CompilerParams(vmem_limit_bytes=6 * 1024 * 1024),
        name="rotate",
    )(left, *parts)


def on_device_fields(start_bands, potential):
    own_bands, nx, ny, nz = start_bands.shape
    gx, gy, chips = lax.axis_size("gx"), lax.axis_size("gy"), lax.axis_size("chip")
    pieces = 2 * chips
    grid = gx * gy
    own = own_bands // grid
    cells = nx * ny
    bands = own_bands * pieces
    rows = cells // pieces
    core = lax.axis_index("core")
    swap = [(0, 1), (1, 0)]

    fields = start_bands.reshape(grid, own * cells, nz)
    flat_potential = potential.reshape(cells, nz)
    half = cells // 2
    own_half = lax.dynamic_slice_in_dim(flat_potential, core * half, half, 0)
    packed = lax.optimization_barrier(jnp.pad(fields, ((0, 0), (0, half), (0, 0))))
    packed = packed.at[:, own * cells :, :].set(own_half[None])
    packed = lax.all_to_all(packed, ("gy", "gx"), 0, 0)
    other = lax.ppermute(packed[:, own * cells :, :], "core", swap)
    dims = (gx, gy, own, nx, ny, nz, pieces, own * cells)
    field, laplace, *weights = first_laplace(packed, dims)
    filtered = apply_filter(field, laplace, packed, other, weights, dims)
    blocks = lax.all_to_all(filtered, ("chip", "core", "gy", "gx"), 0, 0).reshape(bands * rows, nz)

    def tied(value, first):
        return lax.optimization_barrier((value, first))[0]

    def copies(value, *axes):
        count = math.prod(lax.axis_size(axis) for axis in axes)
        pairs = [[(i, i ^ mask) for i in range(count)] for mask in range(1, count)]
        return [value] + [lax.ppermute(value, axes, pair) for pair in pairs]

    spread = partial_margin(blocks, bands, 1.0 / (cells * nz * grid), pieces, grid)
    parts = copies(blocks, "chip")
    margins = lax.all_to_all(spread, ("chip", "core", "gx", "gy"), 0, 0)
    margins = copies(sum_first(margins), "core")
    crossed = [lax.ppermute(tied(blocks, margins[0]), "core", swap)]
    far, margins = lax.optimization_barrier((parts[1:], margins))
    parts += crossed + [lax.ppermute(part, "core", swap) for part in far]
    left = inverse_rows(margins, own_bands, bands)
    rotated = rotate(left, parts, bands)
    return rotated.reshape(start_bands.shape)


def power_of_two(count):
    return count & (count - 1) == 0


def whole_fields(mesh, shape):
    gx, gy, pieces = mesh.shape["gx"], mesh.shape["gy"], mesh.shape["band"]
    bands, nx, ny, nz = shape[0], shape[1] // gx, shape[2] // gy, shape[3]
    own_bands, cells = bands // pieces, nx * ny
    return (
        own_bands % (gx * gy) == 0
        and own_bands % (2 * TILE) == 0
        and pieces % 2 == 0
        and power_of_two(pieces)
        and ny % TILE == 0
        and nz % 128 == 0
        and bands % 64 == 0
        and cells % (2 * TILE) == 0
        and cells % (pieces * TILE // 2) == 0
        and pieces > 2
        and (own_bands // (gx * gy)) * (cells // pieces) % TILE == 0
        and shape[1] > 2 * REACH
    )


def solution(mesh):
    def step(start_bands, potential):
        if whole_fields(mesh, start_bands.shape):
            chips = mesh.shape["band"] // 2
            rest = mesh.devices.shape[1:]
            split = Mesh(mesh.devices.reshape((chips, 2) + rest), ("chip", "core") + mesh.axis_names[1:])
            program, band = on_device_fields, ("chip", "core")
        else:
            split, program, band = mesh, on_device_halo, "band"
        return jax.shard_map(
            program,
            mesh=split,
            in_specs=(P(band, "gx", "gy", None), P("gx", "gy", None)),
            out_specs=P(band, "gx", "gy", None),
            check_vma=False,
        )(start_bands, potential)

    return step
```
